128 devices in a mesh: gx: 16 (over y_hi, x, core), gy: 8 (over y_lo, z).
Axes of the slice: x: 4, y: 4 (y_hi: 2, y_lo: 2; y = y_hi * 2 + y_lo), z: 4, core: 2. Of those that a mesh axis runs over, the one named last changes fastest.
Arguments:
- right_side: float32 [3, 16, 128, 1024], P(None, None, 'gx', 'gy'), may hold values from -6 to 6
- density: int32 [16, 128, 1024], P(None, 'gx', 'gy'), may hold values from 0 to 15
- fixed_mask: int32 [16, 128, 1024], P(None, 'gx', 'gy'), may hold values 0 or 1
Outputs:
- correction: float32 [3, 16, 128, 1024], P(None, None, 'gx', 'gy')
The draws below stay inside these ranges and needn't reach their ends.
All inputs are finite; a program needn't handle non-finite values. No bound on the sum of `fixed_mask` on one device may be relied on, other than what follows from the above.
Results may differ from the reference program's by a relative error of at most 0.0001.
Values sent between devices are 32-bit elements; how exact they have to be, the bound alone decides.
No kernel may reach another device: no remote copies, remote signals or barrier semaphores. Data moves between devices by JAX's collectives and lax.ppermute only.
A program may use at most 64 MiB of HBM per device.

```python
import math
import jax
import jax.numpy as jnp
import numpy as np

NZ = 16
LEVELS = 4
Q = 16
NX = 128
NY = 1024


def draw_right_side(key, part):
    key = jax.random.fold_in(key, 7)
    shape = (3, NZ, NX, NY)
    return jnp.clip(1.6 * jax.random.normal(key, shape, jnp.float32), -6.0, 6.0)


def with_ends(array, stream_key, low, top_value):
    longest = array.shape.index(max(array.shape))
    spots = []
    for shift in (0, 1):
        where = [jax.random.randint(jax.random.fold_in(stream_key, axis), (), 0, length) for axis, length in enumerate(array.shape)]
        where[longest] = (where[longest] + shift) % array.shape[longest]
        spots.append(tuple(where))
    return array.at[spots[0]].set(low).at[spots[1]].set(top_value)


def setup_inputs(seed: int = 0) -> dict:
    keys = jax.random.split(jax.random.key(seed), 4)
    right_side = draw_right_side(jax.random.fold_in(keys[3], 71), 0)
    density = with_ends(jax.random.randint(keys[1], (NZ, NX, NY), 0, Q), jax.random.fold_in(keys[1], 1), 0, Q - 1).astype(jnp.int32)
    fixed_mask = with_ends((jax.random.randint(keys[2], (NZ, NX, NY), 0, 8) < 1).astype(jnp.int32), jax.random.fold_in(keys[2], 1), 0, 1)
    return dict(right_side=right_side, density=density, fixed_mask=fixed_mask)


JACOBI_WEIGHT = 0.6
SOFT_FLOOR = 0.1

def corner_bits(corner):
    return (corner >> 2 & 1, corner >> 1 & 1, corner & 1)

def element_matrix():
    poisson = 0.3
    lame_first = poisson / ((1.0 + poisson) * (1.0 - 2.0 * poisson))
    shear_mod = 0.5 / (1.0 + poisson)
    elastic = np.zeros((6, 6))
    elastic[:3, :3] = lame_first
    for direction in range(3):
        elastic[direction, direction] = lame_first + 2.0 * shear_mod
        elastic[direction + 3, direction + 3] = shear_mod
    points = [0.5 - 0.5 / math.sqrt(3.0), 0.5 + 0.5 / math.sqrt(3.0)]
    matrix = np.zeros((24, 24))
    for point_z in points:
        for point_x in points:
            for point_y in points:
                coords = (point_z, point_x, point_y)
                strain = np.zeros((6, 24))
                for corner in range(8):
                    offsets = corner_bits(corner)
                    gradient = []
                    for direction in range(3):
                        product = 1.0
                        for second in range(3):
                            if second == direction:
                                factor = 1.0 if offsets[second] else -1.0
                            else:
                                factor = coords[second] if offsets[second] else 1.0 - coords[second]
                            product = product * factor
                        gradient.append(product)
                    column = 3 * corner
                    strain[0, column] = gradient[0]
                    strain[1, column + 1] = gradient[1]
                    strain[2, column + 2] = gradient[2]
                    strain[3, column] = gradient[1]
                    strain[3, column + 1] = gradient[0]
                    strain[4, column + 1] = gradient[2]
                    strain[4, column + 2] = gradient[1]
                    strain[5, column] = gradient[2]
                    strain[5, column + 2] = gradient[0]
                matrix = matrix + 0.125 * (strain.T @ elastic @ strain)
    return matrix.reshape(8, 3, 8, 3)

def young_modulus(density):
    return SOFT_FLOOR + (1.0 - SOFT_FLOOR) * (density.astype(jnp.float32) / (Q - 1)) ** 3

def level_coefficient(grown_scale, pad_low, spacing, anchor_x, anchor_y, total_x, total_y):
    layers, span_x, span_y = grown_scale.shape
    if spacing == 1:
        coarse = grown_scale[:, :span_x - 1, :span_y - 1]
    else:
        padded = jnp.pad(grown_scale, ((0, spacing), (0, 0), (0, 0)))
        coarse = 0.0
        for corner in range(8):
            offset_z, offset_x, offset_y = corner_bits(corner)
            coarse = coarse + padded[offset_z * spacing:offset_z * spacing + layers, offset_x * spacing:offset_x * spacing + span_x - spacing, offset_y * spacing:offset_y * spacing + span_y - spacing]
        coarse = 0.125 * coarse
    cell_z = jnp.arange(layers, dtype=jnp.int32)
    cell_x = anchor_x - pad_low + jnp.arange(span_x - spacing, dtype=jnp.int32)
    cell_y = anchor_y - pad_low + jnp.arange(span_y - spacing, dtype=jnp.int32)
    inside = (cell_z <= layers - 1 - spacing)[:, None, None] & ((cell_x >= 0) & (cell_x <= total_x - 1 - spacing))[None, :, None] & ((cell_y >= 0) & (cell_y <= total_y - 1 - spacing))[None, None, :]
    return jnp.where(inside, coarse, 0.0)

def diagonal_terms(coefficient, pad_low, spacing, span_x, span_y, element_table):
    layers = coefficient.shape[0]
    scaled = jnp.pad(coefficient, ((spacing, 0), (0, 0), (0, 0)))
    totals = [0.0, 0.0, 0.0]
    for corner in range(8):
        offset_z, offset_x, offset_y = corner_bits(corner)
        weight = scaled[spacing - spacing * offset_z:spacing - spacing * offset_z + layers, pad_low - spacing * offset_x:pad_low - spacing * offset_x + span_x, pad_low - spacing * offset_y:pad_low - spacing * offset_y + span_y]
        for out_comp in range(3):
            totals[out_comp] = totals[out_comp] + float(element_table[corner, out_comp, corner, out_comp]) * weight
    return spacing * jnp.stack(totals)

def stiffness(values, pad_field, coefficient, pad_low, spacing, margin, element_table):
    layers = values.shape[1]
    span_x = values.shape[2] - 2 * pad_field + 2 * margin
    span_y = values.shape[3] - 2 * pad_field + 2 * margin
    lifted = jnp.pad(values, ((0, 0), (spacing, spacing), (0, 0), (0, 0)))
    scaled = jnp.pad(coefficient, ((spacing, 0), (0, 0), (0, 0)))
    totals = [0.0, 0.0, 0.0]
    for corner in range(8):
        offset_z, offset_x, offset_y = corner_bits(corner)
        low_x = pad_low - margin - spacing * offset_x
        low_y = pad_low - margin - spacing * offset_y
        weight = scaled[spacing - spacing * offset_z:spacing - spacing * offset_z + layers, low_x:low_x + span_x, low_y:low_y + span_y]
        partial_value = [0.0, 0.0, 0.0]
        for second in range(8):
            other_z, other_x, other_y = corner_bits(second)
            first_z = spacing + spacing * (other_z - offset_z)
            first_x = pad_field - margin + spacing * (other_x - offset_x)
            first_y = pad_field - margin + spacing * (other_y - offset_y)
            shifted = lifted[:, first_z:first_z + layers, first_x:first_x + span_x, first_y:first_y + span_y]
            for out_comp in range(3):
                for in_comp in range(3):
                    coupling = float(element_table[corner, out_comp, second, in_comp])
                    if abs(coupling) > 1e-12:
                        partial_value[out_comp] = partial_value[out_comp] + coupling * shifted[in_comp]
        for out_comp in range(3):
            totals[out_comp] = totals[out_comp] + weight * partial_value[out_comp]
    return spacing * jnp.stack(totals)

def spread(values, pad_field, spacing, side_weight, center, margin):
    layers = values.shape[1]
    span_x = values.shape[2] - 2 * pad_field + 2 * margin
    span_y = values.shape[3] - 2 * pad_field + 2 * margin
    lifted = jnp.pad(values, ((0, 0), (spacing, spacing), (0, 0), (0, 0)))
    along_z = center * lifted[:, spacing:spacing + layers] + side_weight * (lifted[:, 2 * spacing:2 * spacing + layers] + lifted[:, :layers])
    anchor = pad_field - margin
    along_x = center * along_z[:, :, anchor:anchor + span_x] + side_weight * (along_z[:, :, anchor + spacing:anchor + spacing + span_x] + along_z[:, :, anchor - spacing:anchor - spacing + span_x])
    along_y = center * along_x[:, :, :, anchor:anchor + span_y] + side_weight * (along_x[:, :, :, anchor + spacing:anchor + spacing + span_y] + along_x[:, :, :, anchor - spacing:anchor - spacing + span_y])
    return along_y

def zero_rim(values, width):
    return jnp.pad(values, ((0, 0), (0, 0), (width, width), (width, width)))

def reference(right_side, density, fixed_mask):
    reach_max = 2 ** (LEVELS - 1)
    wide_x = right_side.shape[2]
    wide_y = right_side.shape[3]
    free_dofs = (1 - fixed_mask).astype(jnp.float32)
    element_table = element_matrix()
    grown_scale = jnp.pad(young_modulus(density), ((0, 0), (reach_max, reach_max), (reach_max, reach_max)))
    residuals, corrections, coefficients, diagonals = ([], [], [], [])
    current = free_dofs * right_side
    for level_index in range(LEVELS):
        spacing = 2 ** level_index
        coefficient = level_coefficient(grown_scale, reach_max, spacing, 0, 0, NX, NY)
        diagonal_now = diagonal_terms(coefficient, reach_max, spacing, wide_x, wide_y, element_table)
        smoothed = free_dofs * JACOBI_WEIGHT * current / diagonal_now
        residuals.append(current)
        corrections.append(smoothed)
        coefficients.append(coefficient)
        diagonals.append(diagonal_now)
        if level_index < LEVELS - 1:
            leftover = current - stiffness(zero_rim(smoothed, spacing), spacing, coefficient, reach_max, spacing, 0, element_table)
            current = spread(zero_rim(leftover, spacing), spacing, spacing, 0.5, 1.0, 0)
    coarsest = LEVELS - 1
    spacing = 2 ** coarsest
    combined = corrections[coarsest]
    applied = stiffness(zero_rim(combined, spacing), spacing, coefficients[coarsest], reach_max, spacing, 0, element_table)
    combined = combined + free_dofs * JACOBI_WEIGHT * (residuals[coarsest] - applied) / diagonals[coarsest]
    for level_index in range(LEVELS - 2, -1, -1):
        spacing = 2 ** level_index
        combined = corrections[level_index] + spread(zero_rim(combined, spacing), spacing, spacing, 0.25, 0.5, 0)
        applied = stiffness(zero_rim(combined, spacing), spacing, coefficients[level_index], reach_max, spacing, 0, element_table)
        combined = combined + free_dofs * JACOBI_WEIGHT * (residuals[level_index] - applied) / diagonals[level_index]
    return free_dofs * combined
```

```python
import jax
import jax.numpy as jnp
from jax import lax
from jax.experimental import pallas as pl
from jax.experimental.pallas import tpu as pltpu
from jax.sharding import PartitionSpec as P

LEVELS = 4
Q = 16
JACOBI_WEIGHT = 0.6
SOFT_FLOOR = 0.1
LAME_FIRST = 0.3 / (1.3 * 0.4)
SHEAR_MOD = 0.5 / 1.3
RATIO = LAME_FIRST / SHEAR_MOD
UNIT = SHEAR_MOD / 16.0
GAIN = JACOBI_WEIGHT / ((RATIO + 4.0) * 16.0 / 9.0)
TINY = 1e-30

SLAB = 8
LANES = 128
EDGE = 40
QUARTER = 32
REACH = 36
KEYS = [(i, az, ay) for i in range(3) for az in range(2) for ay in range(2)]
VMEM_BYTES = 50 * 1024 * 1024
F32 = jnp.float32


def roll(value, shift, axis):
    shift %= value.shape[axis]
    return value if shift == 0 else pltpu.roll(value, shift, axis)


def z_up(planes, step):
    if len(planes) == 1:
        return [roll(planes[0], -step, 0)]
    return [planes[1], roll(planes[0], -1, 0)]


def z_down(planes, step):
    if len(planes) == 1:
        return [roll(planes[0], step, 0)]
    return [roll(planes[1], 1, 0), planes[0]]


def rows_of(shape):
    return lax.broadcasted_iota(jnp.int32, shape, 0)


def lanes_of(shape):
    return lax.broadcasted_iota(jnp.int32, shape, 1)


def to_modes(fields, step, spacing):
    modes = {}
    for i, planes in enumerate(fields):
        ahead = [roll(p, -spacing, 1) for p in planes]
        for ay, along in ((0, [b + a for a, b in zip(planes, ahead)]), (1, [b - a for a, b in zip(planes, ahead)])):
            above = z_up(along, step)
            modes[i, 0, ay] = [b + a for a, b in zip(along, above)]
            modes[i, 1, ay] = [b - a for a, b in zip(along, above)]
    return modes


def from_modes(modes, step, spacing):
    fields = []
    for i in range(3):
        along = []
        for ay in range(2):
            low = [s - d for s, d in zip(modes[i, 0, ay], modes[i, 1, ay])]
            high = z_down([s + d for s, d in zip(modes[i, 0, ay], modes[i, 1, ay])], step)
            along.append([a + b for a, b in zip(low, high)])
        fields.append([(s - d) + roll(s + d, spacing, 1) for s, d in zip(along[0], along[1])])
    return fields


def cell(low, high, scale):
    full = {}
    for i, az, ay in KEYS:
        if az or ay:
            full[i, az, 0, ay] = high[i, az, ay] + low[i, az, ay]
        full[i, az, 1, ay] = high[i, az, ay] - low[i, az, ay]

    def mode(i, *dims):
        return full[i, int(0 in dims), int(1 in dims), int(2 in dims)]

    out = {}

    def put(value, i, *dims):
        out[i, int(0 in dims), int(1 in dims), int(2 in dims)] = value

    twice = 2.0 * scale
    half = 0.5 * scale * (RATIO / 1.5)
    third = scale * (1.0 / 3.0)
    trace = (RATIO * scale) * (mode(0, 0) + mode(1, 1) + mode(2, 2))
    for i in range(3):
        put(trace + twice * mode(i, i), i, i)
    for i, j in ((0, 1), (0, 2), (1, 2)):
        shear = scale * (mode(i, j) + mode(j, i))
        put(shear, i, j)
        put(shear, j, i)
    for q in range(3):
        p, r = [d for d in range(3) if d != q]
        first, second = mode(p, p, q), mode(r, r, q)
        both = half * (first + second)
        put(both + scale * first, p, p, q)
        put(both + scale * second, r, r, q)
    others = [[d for d in range(3) if d != i] for i in range(3)]
    total = mode(0, *others[0]) + mode(1, *others[1]) + mode(2, *others[2])
    for i in range(3):
        put(third * (total + mode(i, *others[i])), i, *others[i])
    ninth = scale * ((RATIO + 4.0) / 9.0)
    for i in range(3):
        put(ninth * mode(i, 0, 1, 2), i, 0, 1, 2)

    to_low, to_high = {}, {}
    for i, az, ay in KEYS:
        difference = out[i, az, 1, ay]
        if az or ay:
            to_low[i, az, ay] = out[i, az, 0, ay] - difference
            to_high[i, az, ay] = out[i, az, 0, ay] + difference
        else:
            to_low[i, az, ay] = -difference
            to_high[i, az, ay] = difference
    return to_low, to_high


def spread_plane(planes, step, spacing):
    rows = rows_of(planes[0].shape)
    above, below = z_up(planes, step), z_down(planes, step)
    if len(planes) == 1:
        above = [jnp.where(rows < 8 - step, above[0], 0.0)]
        below = [jnp.where(rows >= step, below[0], 0.0)]
    else:
        above = [above[0], jnp.where(rows < 7, above[1], 0.0)]
        below = [jnp.where(rows >= 1, below[0], 0.0), below[1]]
    along = [p + 0.5 * (a + b) for p, a, b in zip(planes, above, below)]
    return [p + 0.5 * (roll(p, spacing, 1) + roll(p, -spacing, 1)) for p in along]


def edges_kernel(right_ref, density_ref, mask_ref, own_ref, first_ref, last_ref):
    lanes = lanes_of((8, LANES))
    for x in range(SLAB):
        for e in range(2):
            rows = pl.ds(e * 8 + x, 8, stride=16)
            free = 1.0 - mask_ref[rows, :].astype(F32)
            level = density_ref[rows, :].astype(F32) / (Q - 1)
            young = SOFT_FLOOR + (1.0 - SOFT_FLOOR) * (level * level * level)
            fields = [free * right_ref[i, rows, :] for i in range(3)] + [UNIT * young, free]
            for f, value in enumerate(fields):
                own_ref[x, f, e] = value
            for group in range(2):
                members = fields[3 * group : 3 * group + 3]
                first = last = None
                for n, value in enumerate(members):
                    begin = roll(value, EDGE * n, 1)
                    end = roll(value, EDGE * n - (LANES - EDGE), 1)
                    first = begin if n == 0 else jnp.where(lanes < EDGE * n, first, begin)
                    last = end if n == 0 else jnp.where(lanes < EDGE * n, last, end)
                first_ref[x, group, e] = first
                last_ref[x, group, e] = last


WIDE = 2 * LANES


def fine_kernel(
    meta_ref, own_ref, after_ref, before_ref, pair_ref, far_ref,
    out_ref, value_ref, scale_out_ref, gain_ref,
    res, scale, mode, ahead, node, left,
):
    slab, line, core = meta_ref[0], meta_ref[1], meta_ref[2]
    lanes = lanes_of((8, LANES))
    wide = lanes_of((8, WIDE))
    rows = rows_of((8, WIDE))
    local = jnp.where(wide < 192, wide, wide - WIDE)
    place = local + LANES * line
    node_in = (place >= 0) & (place < 8 * LANES) & (local >= -EDGE) & (local < LANES + EDGE)
    cell_in = (place >= 0) & (place < 8 * LANES - 1)
    first_slab, last_slab = slab == 0, slab == 15

    def field(x, f, e):
        group, n = f // 3, f % 3
        if 0 <= x < SLAB:
            mid, hi, lo = own_ref[x, f, e], after_ref[x, group, e], before_ref[x, group, e]
        else:
            p = x + 3 if x < 0 else x - SLAB
            is_pair = (core == 1) if x < 0 else (core == 0)
            mid, hi, lo = (
                jnp.where(is_pair, pair_ref[p, s, e], far_ref[p, s, e])
                for s in (f, 5 + group, 7 + group)
            )
        hi = roll(hi, -EDGE * n, 1)
        lo = roll(lo, (LANES - EDGE) - EDGE * n, 1)
        return jnp.concatenate([mid, jnp.where(lanes < 64, hi, lo)], axis=1)

    def inside(mask, x, top):
        if x < 0:
            return mask & jnp.logical_not(first_slab)
        if x >= top:
            return mask & jnp.logical_not(last_slab)
        return mask

    for x in range(-3, SLAB + 2):
        for e in range(2):
            cells = inside(cell_in, x, SLAB - 1)
            if e == 1:
                cells = cells & (rows < 7)
            scale[x + 3, e] = jnp.where(cells, field(x, 3, e), 0.0)

    for x in range(-2, SLAB + 2):
        total = []
        for e in range(2):
            total.append(scale[x + 3, e] + scale[x + 2, e])
        total = [a + b for a, b in zip(total, z_down(total, 1))]
        total = [a + roll(a, 1, 1) for a in total]
        nodes = inside(node_in, x, SLAB)
        gains = []
        for e in range(2):
            free = jnp.where(nodes, field(x, 4, e), 0.0)
            gains.append(GAIN * free / jnp.maximum(total[e], TINY))
            if 0 <= x < SLAB:
                gain_ref[x, e] = gains[e][:, :LANES]
                left[x, 3, e] = free
        values = []
        for i in range(3):
            planes = []
            for e in range(2):
                now = jnp.where(nodes, field(x, i, e), 0.0)
                res[x + 2, i, e] = now
                planes.append(gains[e] * now)
                if -1 <= x < SLAB + 1:
                    value_ref[x + 1, i, e] = planes[e]
            values.append(planes)
        for k, key in enumerate(KEYS):
            pass
        modes = to_modes(values, 1, 1)
        for k, key in enumerate(KEYS):
            for e in range(2):
                mode[x + 2, k, e] = modes[key][e]
    for x in range(-1, SLAB):
        for e in range(2):
            scale_out_ref[x + 1, e] = scale[x + 3, e]

    for k in range(12):
        for e in range(2):
            ahead[k, e] = jnp.zeros((8, WIDE), F32)

    def sweep(n, carry):
        for e in range(2):
            for t in range(2):
                part = slice(t * LANES, (t + 1) * LANES)
                low = {key: mode[n, k, e, :, part] for k, key in enumerate(KEYS)}
                high = {key: mode[n + 1, k, e, :, part] for k, key in enumerate(KEYS)}
                to_low, to_high = cell(low, high, scale[n + 1, e, :, part])
                for k, key in enumerate(KEYS):
                    node[k, e, :, part] = to_low[key] + ahead[k, e, :, part]
                    ahead[k, e, :, part] = to_high[key]
        modes = {key: [node[k, e] for e in range(2)] for k, key in enumerate(KEYS)}
        applied = from_modes(modes, 1, 1)
        x = n - 2
        keep = node_in & jnp.logical_not((x < 0) & first_slab) & jnp.logical_not((x >= SLAB) & last_slab)
        for i in range(3):
            rest = [jnp.where(keep, res[n, i, e] - applied[i][e], 0.0) for e in range(2)]
            rest = spread_plane(rest, 1, 1)
            for e in range(2):
                res[n, i, e] = rest[e]
        return carry

    lax.fori_loop(0, SLAB + 3, sweep, 0)

    for x in range(SLAB):
        for e in range(2):
            fields = []
            for i in range(3):
                fields.append(res[x + 2, i, e] + 0.5 * (res[x + 1, i, e] + res[x + 3, i, e]))
            fields.append(left[x, 3, e])
            young = field(x, 3, e)
            for quarter in range(4):
                start = REACH - QUARTER * quarter
                window = roll(young, start, 1)[:, :LANES]
                target = e * 8 + (x % 2) * 4 + quarter
                for f in range(4):
                    main = roll(fields[f], start, 1)[:, :LANES]
                    piece = roll(window, 102 - 26 * f, 1)
                    out_ref[target, x // 2, f] = jnp.where(lanes < 102, main, piece)


COUNT = 64
PAD = 4


def coarse_kernel(meta_ref, in_ref, out_ref, young, free, res, value, gain, scale, spread, mode, ahead):
    start = meta_ref[3]
    shape = (8, LANES)
    lanes = lanes_of(shape)
    rows = rows_of(shape)
    place = lanes + start
    node_in = (place >= 0) & (place < 8 * LANES)
    first_in = node_in & (lanes >= 2) & (lanes < 102)
    zero = jnp.zeros(shape, F32)
    unroll = 4

    def loop(body):
        def step(i, carry):
            for u in range(unroll):
                body(unroll * i + u, i, u)
            return carry

        lax.fori_loop(0, COUNT // unroll, step, 0)

    for p in range(PAD):
        for i in range(3):
            spread[p, i] = zero
            spread[PAD + COUNT + p, i] = zero
        for k in range(12):
            mode[COUNT + p, k] = zero
        young[COUNT + p] = zero

    def unpack(x, i, u):
        total = zero
        tiles = [in_ref[x, f] for f in range(4)]
        for f in range(4):
            total = jnp.where(lanes >= 26 * f, roll(tiles[f], 26 * f - 102, 1), total)
        young[x] = total
        for f in range(3):
            res[0, x, f] = jnp.where(first_in, tiles[f], 0.0)
        free[x] = jnp.where(first_in, tiles[3], 0.0)

    loop(unpack)

    for level in range(1, LEVELS):
        step, spacing = 2 ** (level - 1), 2**level
        cells = (place >= 0) & (place <= 8 * LANES - 1 - spacing) & (rows < 8 - step)
        for p in range(step):
            scale[level - 1, p] = zero

        def fill_scale(x, i, u):
            total = young[x] + young[x + step]
            total = total + roll(total, -step, 0)
            total = total + roll(total, -spacing, 1)
            inside = cells & (x < COUNT - step)
            scale[level - 1, x + PAD] = jnp.where(inside, (0.125 * spacing) * total, 0.0)

        def fill_gain(x, i, u):
            total = scale[level - 1, x + PAD] + scale[level - 1, x + PAD - step]
            total = total + roll(total, step, 0)
            total = total + roll(total, spacing, 1)
            gain[level - 1, x] = GAIN * free[x] / jnp.maximum(total, TINY)

        for p in range(PAD):
            scale[level - 1, p] = zero
        loop(fill_scale)
        loop(fill_gain)

    def put_modes(x, fields, step, spacing):
        modes = to_modes([[f] for f in fields], step, spacing)
        for k, key in enumerate(KEYS):
            mode[x, k] = modes[key][0]

    def sweep(level, finish):
        step, spacing = 2 ** (level - 1), 2**level
        for p in range(step):
            for k in range(12):
                ahead[p, k] = zero

        def body(x, i, u):
            low = {key: mode[x, k] for k, key in enumerate(KEYS)}
            high = {key: mode[x + step, k] for k, key in enumerate(KEYS)}
            to_low, to_high = cell(low, high, scale[level - 1, x + PAD])
            modes = {key: [to_low[key] + ahead[x, k]] for k, key in enumerate(KEYS)}
            for k, key in enumerate(KEYS):
                ahead[x + step, k] = to_high[key]
            applied = from_modes(modes, step, spacing)
            finish(x, i, u, [a[0] for a in applied])

        loop(body)

    for level in range(1, LEVELS):
        step, spacing = 2 ** (level - 1), 2**level

        def smooth(x, i, u):
            fields = []
            for f in range(3):
                if level == 1:
                    now = res[0, x, f]
                else:
                    reach = step // 2
                    sides = spread[PAD + x - reach, f] + spread[PAD + x + reach, f]
                    now = jnp.where(node_in, spread[PAD + x, f] + 0.5 * sides, 0.0)
                    res[level - 1, x, f] = now
                fields.append(gain[level - 1, x] * now)
                value[level - 1, x, f] = fields[f]
            put_modes(x, fields, step, spacing)

        def restrict(x, i, u, applied):
            for f in range(3):
                rest = res[level - 1, x, f] - applied[f]
                spread[PAD + x, f] = spread_plane([rest], step, spacing)[0]

        def correct(x, i, u, applied):
            for f in range(3):
                rest = res[level - 1, x, f] - applied[f]
                spread[PAD + x, f] = value[level - 1, x, f] + gain[level - 1, x] * rest

        loop(smooth)
        sweep(level, restrict if level < LEVELS - 1 else correct)

    for level in range(LEVELS - 2, 0, -1):
        step, spacing = 2 ** (level - 1), 2**level

        def prolong(x, i, u):
            fields = []
            for f in range(3):
                sides = spread[PAD + x - step, f] + spread[PAD + x + step, f]
                along = spread[PAD + x, f] + 0.5 * sides
                along = spread_plane([along], step, spacing)[0]
                fields.append(jnp.where(node_in, value[level - 1, x, f] + 0.125 * along, 0.0))
                value[level - 1, x, f] = fields[f]
            put_modes(x, fields, step, spacing)

        def correct(x, i, u, applied):
            fields = []
            for f in range(3):
                rest = res[level - 1, x, f] - applied[f]
                fields.append(value[level - 1, x, f] + gain[level - 1, x] * rest)
            if level > 1:
                for f in range(3):
                    spread[PAD + x, f] = fields[f]
                return
            packed = roll(fields[0], -34, 1)
            for f in range(1, 3):
                packed = jnp.where(lanes < EDGE * f, packed, roll(fields[f], EDGE * f - 34, 1))
            out_ref[i, u + 1] = packed
            if u == 0:

                @pl.when(i > 0)
                def _():
                    out_ref[i - 1, 5] = packed

            if u == 3:

                @pl.when(i < COUNT // unroll - 1)
                def _():
                    out_ref[i + 1, 0] = packed

        loop(prolong)
        sweep(level, correct)
    out_ref[0, 0] = zero
    out_ref[COUNT // unroll - 1, 5] = zero


def last_kernel(own_ref, value_ref, scale_ref, gain_ref, in_ref, out_ref, coarse, mode, ahead, node, field):
    lanes = lanes_of((8, LANES))
    for n in range(SLAB + 4):
        slot, parity = n // 2, n % 2
        for i in range(3):
            planes = []
            for e in range(2):
                parts = [
                    roll(in_ref[e * 8 + parity * 4 + q, slot], QUARTER * q - 2 - EDGE * i, 1)
                    for q in range(4)
                ]
                main = parts[0]
                for q in range(1, 4):
                    main = jnp.where(lanes < QUARTER * q, main, parts[q])
                side = jnp.where(lanes < 64, parts[3], parts[0])
                planes.append(jnp.concatenate([main, side], axis=1))
            planes = spread_plane(planes, 1, 1)
            for e in range(2):
                coarse[n, i, e] = planes[e]

    def prolong(n, carry):
        fields = []
        for i in range(3):
            planes = []
            for e in range(2):
                along = coarse[n + 1, i, e] + 0.5 * (coarse[n, i, e] + coarse[n + 2, i, e])
                planes.append(value_ref[n, i, e] + 0.125 * along)
                field[n, i, e] = planes[e][:, :LANES]
            fields.append(planes)
        modes = to_modes(fields, 1, 1)
        for k, key in enumerate(KEYS):
            for e in range(2):
                mode[n, k, e] = modes[key][e]
        return carry

    lax.fori_loop(0, SLAB + 2, prolong, 0)

    for k in range(12):
        for e in range(2):
            ahead[k, e] = jnp.zeros((8, WIDE), F32)

    for n in range(SLAB + 1):
        x = n - 1
        for e in range(2):
            for t in range(2):
                part = slice(t * LANES, (t + 1) * LANES)
                low = {key: mode[n, k, e, :, part] for k, key in enumerate(KEYS)}
                high = {key: mode[n + 1, k, e, :, part] for k, key in enumerate(KEYS)}
                to_low, to_high = cell(low, high, scale_ref[n, e, :, part])
                for k, key in enumerate(KEYS):
                    if x >= 0:
                        node[k, e, :, part] = to_low[key] + ahead[k, e, :, part]
                    ahead[k, e, :, part] = to_high[key]
        if x < 0:
            continue
        modes = {key: [node[k, e] for e in range(2)] for k, key in enumerate(KEYS)}
        applied = from_modes(modes, 1, 1)
        for i in range(3):
            for e in range(2):
                rest = own_ref[x, i, e] - applied[i][e][:, :LANES]
                total = field[n, i, e] + gain_ref[x, e] * rest
                out_ref[i, pl.ds(e * 8 + x, 8, stride=16), :] = own_ref[x, 4, e] * total


def shapes(*sizes):
    return [jax.ShapeDtypeStruct(size, F32) for size in sizes]


def scratch(*sizes):
    return [pltpu.VMEM(size, F32) for size in sizes]


def call(kernel, name, out, scratches, scalars, arrays):
    specs = [pl.BlockSpec(memory_space=pltpu.SMEM)] * len(scalars)
    specs += [pl.BlockSpec(memory_space=pltpu.VMEM)] * len(arrays)
    return pl.pallas_call(
        kernel,
        out_shape=out,
        in_specs=specs,
        out_specs=[pl.BlockSpec(memory_space=pltpu.VMEM)] * len(out),
        scratch_shapes=scratches,
        compiler_params=pltpu.CompilerParams(vmem_limit_bytes=VMEM_BYTES),
        name=name,
    )(*scalars, *arrays)


def on_device(right_side, density, fixed_mask):
    slab, line = lax.axis_index("gx"), lax.axis_index("gy")
    slabs, lines = lax.axis_size("gx"), lax.axis_size("gy")
    core = slab % 2
    start = LANES * line + QUARTER * (slab % 4) - REACH
    meta = jnp.stack([slab, line, core, start]).astype(jnp.int32)
    rows = 16 * SLAB

    own, first, last = call(
        edges_kernel,
        "edges",
        shapes((SLAB, 5, 2, 8, LANES), (SLAB, 2, 2, 8, LANES), (SLAB, 2, 2, 8, LANES)),
        [],
        [],
        [right_side.reshape(3, rows, LANES), density.reshape(rows, LANES), fixed_mask.reshape(rows, LANES)],
    )
    after = lax.ppermute(first, "gy", [((j + 1) % lines, j) for j in range(lines)])
    before = lax.ppermute(last, "gy", [(j, (j + 1) % lines) for j in range(lines)])

    def columns(begin):
        parts = [lax.dynamic_slice_in_dim(a, begin, 3, axis=0) for a in (own, after, before)]
        return jnp.concatenate(parts, axis=1)

    pair = lax.ppermute(columns(5 * (1 - core)), "gx", [(i, i ^ 1) for i in range(slabs)])
    swaps = [(i, (i + 1) % slabs) for i in range(1, slabs, 2)]
    far = lax.ppermute(columns(5 * core), "gx", swaps + [(b, a) for a, b in swaps])

    packed, value, scale, gain = call(
        fine_kernel,
        "fine",
        shapes(
            (slabs, 4, 4, 8, LANES),
            (SLAB + 2, 3, 2, 8, WIDE),
            (SLAB + 1, 2, 8, WIDE),
            (SLAB, 2, 8, LANES),
        ),
        scratch(
            (SLAB + 4, 3, 2, 8, WIDE),
            (SLAB + 5, 2, 8, WIDE),
            (SLAB + 4, 12, 2, 8, WIDE),
            (12, 2, 8, WIDE),
            (12, 2, 8, WIDE),
            (SLAB, 4, 2, 8, WIDE),
        ),
        [meta],
        [own, after, before, pair, far],
    )
    packed = lax.all_to_all(packed, "gx", 0, 0)
    (result,) = call(
        coarse_kernel,
        "coarse",
        shapes((slabs, 6, 8, LANES)),
        scratch(
            (COUNT + PAD, 8, LANES),
            (COUNT, 8, LANES),
            (3, COUNT, 3, 8, LANES),
            (3, COUNT, 3, 8, LANES),
            (3, COUNT, 8, LANES),
            (3, PAD + COUNT, 8, LANES),
            (2 * PAD + COUNT, 3, 8, LANES),
            (COUNT + PAD, 12, 8, LANES),
            (COUNT + PAD, 12, 8, LANES),
        ),
        [meta],
        [packed.reshape(COUNT, 4, 8, LANES)],
    )
    result = lax.all_to_all(result, "gx", 0, 0)
    (correction,) = call(
        last_kernel,
        "last",
        shapes((3, rows, LANES)),
        scratch(
            (SLAB + 4, 3, 2, 8, WIDE),
            (SLAB + 2, 12, 2, 8, WIDE),
            (12, 2, 8, WIDE),
            (12, 2, 8, WIDE),
            (SLAB + 2, 3, 2, 8, LANES),
        ),
        [],
        [own, value, scale, gain, result],
    )
    return correction.reshape(right_side.shape)


def solution(mesh):
    in_specs = (P(None, None, "gx", "gy"), P(None, "gx", "gy"), P(None, "gx", "gy"))
    out_specs = P(None, None, "gx", "gy")
    return jax.shard_map(
        on_device, mesh=mesh, in_specs=in_specs, out_specs=out_specs, check_vma=False
    )
```

```python
import jax
import jax.numpy as jnp
from jax import lax
from jax.experimental import pallas as pl
from jax.experimental.pallas import tpu as pltpu
from jax.sharding import PartitionSpec as P

LEVELS = 4
Q = 16
JACOBI_WEIGHT = 0.6
SOFT_FLOOR = 0.1
LAME_FIRST = 0.3 / (1.3 * 0.4)
SHEAR_MOD = 0.5 / 1.3
RATIO = LAME_FIRST / SHEAR_MOD
UNIT = SHEAR_MOD / 16.0
GAIN = JACOBI_WEIGHT / ((RATIO + 4.0) * 16.0 / 9.0)
TINY = 1e-30

SLAB = 8
LANES = 128
FINE_UNROLL = 11
LAST_UNROLL = 10
EDGE = 40
QUARTER = 32
REACH = 36
KEYS = [(i, az, ay) for i in range(3) for az in range(2) for ay in range(2)]
VMEM_BYTES = 50 * 1024 * 1024
F32 = jnp.float32


def roll(value, shift, axis):
    shift %= value.shape[axis]
    return value if shift == 0 else pltpu.roll(value, shift, axis)


def z_up(planes, step):
    if len(planes) == 1:
        return [roll(planes[0], -step, 0)]
    return [planes[1], roll(planes[0], -1, 0)]


def z_down(planes, step):
    if len(planes) == 1:
        return [roll(planes[0], step, 0)]
    return [roll(planes[1], 1, 0), planes[0]]


def fori(count, body, unroll):
    if unroll == count:
        for n in range(count):
            body(n, 0)
    else:
        lax.fori_loop(0, count, body, 0)


def rows_of(shape):
    return lax.broadcasted_iota(jnp.int32, shape, 0)


def lanes_of(shape):
    return lax.broadcasted_iota(jnp.int32, shape, 1)


def to_modes(fields, step, spacing):
    modes = {}
    for i, planes in enumerate(fields):
        ahead = [roll(p, -spacing, 1) for p in planes]
        for ay, along in ((0, [b + a for a, b in zip(planes, ahead)]), (1, [b - a for a, b in zip(planes, ahead)])):
            above = z_up(along, step)
            modes[i, 0, ay] = [b + a for a, b in zip(along, above)]
            modes[i, 1, ay] = [b - a for a, b in zip(along, above)]
    return modes


def from_modes(modes, step, spacing):
    fields = []
    for i in range(3):
        along = []
        for ay in range(2):
            low = [s - d for s, d in zip(modes[i, 0, ay], modes[i, 1, ay])]
            high = z_down([s + d for s, d in zip(modes[i, 0, ay], modes[i, 1, ay])], step)
            along.append([a + b for a, b in zip(low, high)])
        fields.append([(s - d) + roll(s + d, spacing, 1) for s, d in zip(along[0], along[1])])
    return fields


def cell(low, high, scale):
    full = {}
    for i, az, ay in KEYS:
        if az or ay:
            full[i, az, 0, ay] = high[i, az, ay] + low[i, az, ay]
        full[i, az, 1, ay] = high[i, az, ay] - low[i, az, ay]

    def mode(i, *dims):
        return full[i, int(0 in dims), int(1 in dims), int(2 in dims)]

    out = {}

    def put(value, i, *dims):
        out[i, int(0 in dims), int(1 in dims), int(2 in dims)] = value

    twice = 2.0 * scale
    half = 0.5 * scale * (RATIO / 1.5)
    third = scale * (1.0 / 3.0)
    trace = (RATIO * scale) * (mode(0, 0) + mode(1, 1) + mode(2, 2))
    for i in range(3):
        put(trace + twice * mode(i, i), i, i)
    for i, j in ((0, 1), (0, 2), (1, 2)):
        shear = scale * (mode(i, j) + mode(j, i))
        put(shear, i, j)
        put(shear, j, i)
    for q in range(3):
        p, r = [d for d in range(3) if d != q]
        first, second = mode(p, p, q), mode(r, r, q)
        both = half * (first + second)
        put(both + scale * first, p, p, q)
        put(both + scale * second, r, r, q)
    others = [[d for d in range(3) if d != i] for i in range(3)]
    total = mode(0, *others[0]) + mode(1, *others[1]) + mode(2, *others[2])
    for i in range(3):
        put(third * (total + mode(i, *others[i])), i, *others[i])
    ninth = scale * ((RATIO + 4.0) / 9.0)
    for i in range(3):
        put(ninth * mode(i, 0, 1, 2), i, 0, 1, 2)

    to_low, to_high = {}, {}
    for i, az, ay in KEYS:
        difference = out[i, az, 1, ay]
        if az or ay:
            to_low[i, az, ay] = out[i, az, 0, ay] - difference
            to_high[i, az, ay] = out[i, az, 0, ay] + difference
        else:
            to_low[i, az, ay] = -difference
            to_high[i, az, ay] = difference
    return to_low, to_high


def spread_plane(planes, step, spacing):
    rows = rows_of(planes[0].shape)
    above, below = z_up(planes, step), z_down(planes, step)
    if len(planes) == 1:
        above = [jnp.where(rows < 8 - step, above[0], 0.0)]
        below = [jnp.where(rows >= step, below[0], 0.0)]
    else:
        above = [above[0], jnp.where(rows < 7, above[1], 0.0)]
        below = [jnp.where(rows >= 1, below[0], 0.0), below[1]]
    along = [p + 0.5 * (a + b) for p, a, b in zip(planes, above, below)]
    return [p + 0.5 * (roll(p, spacing, 1) + roll(p, -spacing, 1)) for p in along]


def edges_kernel(right_ref, density_ref, mask_ref, own_ref, first_ref, last_ref):
    lanes = lanes_of((8, LANES))
    for x in range(SLAB):
        for e in range(2):
            rows = pl.ds(e * 8 + x, 8, stride=16)
            free = 1.0 - mask_ref[rows, :].astype(F32)
            level = density_ref[rows, :].astype(F32) / (Q - 1)
            young = SOFT_FLOOR + (1.0 - SOFT_FLOOR) * (level * level * level)
            fields = [free * right_ref[i, rows, :] for i in range(3)] + [UNIT * young, free]
            for f, value in enumerate(fields):
                own_ref[x, f, e] = value
            for group in range(2):
                members = fields[3 * group : 3 * group + 3]
                first = last = None
                for n, value in enumerate(members):
                    begin = roll(value, EDGE * n, 1)
                    end = roll(value, EDGE * n - (LANES - EDGE), 1)
                    first = begin if n == 0 else jnp.where(lanes < EDGE * n, first, begin)
                    last = end if n == 0 else jnp.where(lanes < EDGE * n, last, end)
                first_ref[x, group, e] = first
                last_ref[x, group, e] = last


WIDE = 2 * LANES

FINE_SCRATCH = (
    (SLAB + 4, 3, 2, 8, WIDE),
    (SLAB + 5, 2, 8, WIDE),
    (SLAB + 4, 12, 2, 8, WIDE),
    (12, 2, 8, WIDE),
    (12, 2, 8, WIDE),
    (SLAB, 4, 2, 8, WIDE),
)


def fine_kernel(
    meta_ref, own_ref, after_ref, before_ref, pair_ref, far_ref,
    out_ref, value_ref, scale_out_ref, gain_ref,
    res, scale, mode, ahead, node, left,
):
    slab, line, core = meta_ref[0], meta_ref[1], meta_ref[2]
    lanes = lanes_of((8, LANES))
    wide = lanes_of((8, WIDE))
    rows = rows_of((8, WIDE))
    local = jnp.where(wide < 192, wide, wide - WIDE)
    place = local + LANES * line
    node_in = (place >= 0) & (place < 8 * LANES) & (local >= -EDGE) & (local < LANES + EDGE)
    cell_in = (place >= 0) & (place < 8 * LANES - 1)
    first_slab, last_slab = slab == 0, slab == 15

    def field(x, f, e):
        group, n = f // 3, f % 3
        if 0 <= x < SLAB:
            mid, hi, lo = own_ref[x, f, e], after_ref[x, group, e], before_ref[x, group, e]
        else:
            p = x + 3 if x < 0 else x - SLAB
            is_pair = (core == 1) if x < 0 else (core == 0)
            mid, hi, lo = (
                jnp.where(is_pair, pair_ref[p, s, e], far_ref[p, s, e])
                for s in (f, 5 + group, 7 + group)
            )
        hi = roll(hi, -EDGE * n, 1)
        lo = roll(lo, (LANES - EDGE) - EDGE * n, 1)
        return jnp.concatenate([mid, jnp.where(lanes < 64, hi, lo)], axis=1)

    def inside(mask, x, top):
        if x < 0:
            return mask & jnp.logical_not(first_slab)
        if x >= top:
            return mask & jnp.logical_not(last_slab)
        return mask

    for x in range(-3, SLAB + 2):
        for e in range(2):
            cells = inside(cell_in, x, SLAB - 1)
            if e == 1:
                cells = cells & (rows < 7)
            scale[x + 3, e] = jnp.where(cells, field(x, 3, e), 0.0)

    for x in range(-2, SLAB + 2):
        total = []
        for e in range(2):
            total.append(scale[x + 3, e] + scale[x + 2, e])
        total = [a + b for a, b in zip(total, z_down(total, 1))]
        total = [a + roll(a, 1, 1) for a in total]
        nodes = inside(node_in, x, SLAB)
        gains = []
        for e in range(2):
            free = jnp.where(nodes, field(x, 4, e), 0.0)
            gains.append(GAIN * free / jnp.maximum(total[e], TINY))
            if 0 <= x < SLAB:
                gain_ref[x, e] = gains[e][:, :LANES]
                left[x, 3, e] = free
        values = []
        for i in range(3):
            planes = []
            for e in range(2):
                now = jnp.where(nodes, field(x, i, e), 0.0)
                res[x + 2, i, e] = now
                planes.append(gains[e] * now)
                if -1 <= x < SLAB + 1:
                    value_ref[x + 1, i, e] = planes[e]
            values.append(planes)
        for k, key in enumerate(KEYS):
            pass
        modes = to_modes(values, 1, 1)
        for k, key in enumerate(KEYS):
            for e in range(2):
                mode[x + 2, k, e] = modes[key][e]
    for x in range(-1, SLAB):
        for e in range(2):
            scale_out_ref[x + 1, e] = scale[x + 3, e]

    for k in range(12):
        for e in range(2):
            ahead[k, e] = jnp.zeros((8, WIDE), F32)

    def sweep(n, carry):
        for e in range(2):
            for t in range(2):
                part = slice(t * LANES, (t + 1) * LANES)
                low = {key: mode[n, k, e, :, part] for k, key in enumerate(KEYS)}
                high = {key: mode[n + 1, k, e, :, part] for k, key in enumerate(KEYS)}
                to_low, to_high = cell(low, high, scale[n + 1, e, :, part])
                for k, key in enumerate(KEYS):
                    node[k, e, :, part] = to_low[key] + ahead[k, e, :, part]
                    ahead[k, e, :, part] = to_high[key]
        modes = {key: [node[k, e] for e in range(2)] for k, key in enumerate(KEYS)}
        applied = from_modes(modes, 1, 1)
        x = n - 2
        keep = node_in & jnp.logical_not((x < 0) & first_slab) & jnp.logical_not((x >= SLAB) & last_slab)
        for i in range(3):
            rest = [jnp.where(keep, res[n, i, e] - applied[i][e], 0.0) for e in range(2)]
            rest = spread_plane(rest, 1, 1)
            for e in range(2):
                res[n, i, e] = rest[e]
        return carry

    fori(SLAB + 3, sweep, FINE_UNROLL)

    for x in range(SLAB):
        for e in range(2):
            fields = []
            for i in range(3):
                fields.append(res[x + 2, i, e] + 0.5 * (res[x + 1, i, e] + res[x + 3, i, e]))
            fields.append(left[x, 3, e])
            young = field(x, 3, e)
            for quarter in range(4):
                start = REACH - QUARTER * quarter
                window = roll(young, start, 1)[:, :LANES]
                target = e * 8 + (x % 2) * 4 + quarter
                for f in range(4):
                    main = roll(fields[f], start, 1)[:, :LANES]
                    piece = roll(window, 102 - 26 * f, 1)
                    out_ref[target, x // 2, f] = jnp.where(lanes < 102, main, piece)


COUNT = 64
UNROLL = 16
UNROLL_SWEEP = 16
PAD = 4

COARSE_SCRATCH = (
    (COUNT + PAD, 8, LANES),
    (COUNT, 8, LANES),
    (3, COUNT, 3, 8, LANES),
    (3, COUNT, 3, 8, LANES),
    (3, COUNT, 8, LANES),
    (3, PAD + COUNT, 8, LANES),
    (2 * PAD + COUNT, 3, 8, LANES),
    (COUNT + PAD, 12, 8, LANES),
    (COUNT + PAD, 12, 8, LANES),
)


def coarse_kernel(meta_ref, in_ref, out_ref, young, free, res, value, gain, scale, spread, mode, ahead):
    start = meta_ref[3]
    shape = (8, LANES)
    lanes = lanes_of(shape)
    rows = rows_of(shape)
    place = lanes + start
    node_in = (place >= 0) & (place < 8 * LANES)
    first_in = node_in & (lanes >= 2) & (lanes < 102)
    zero = jnp.zeros(shape, F32)

    def loop(body, unroll):
        def step(i, carry):
            for u in range(unroll):
                body(unroll * i + u, i * (unroll // 4) + u // 4, u % 4)
            return carry

        lax.fori_loop(0, COUNT // unroll, step, 0)

    for p in range(PAD):
        for i in range(3):
            spread[p, i] = zero
            spread[PAD + COUNT + p, i] = zero
        for k in range(12):
            mode[COUNT + p, k] = zero
        young[COUNT + p] = zero

    def unpack(x, i, u):
        total = zero
        tiles = [in_ref[x, f] for f in range(4)]
        for f in range(4):
            total = jnp.where(lanes >= 26 * f, roll(tiles[f], 26 * f - 102, 1), total)
        young[x] = total
        for f in range(3):
            res[0, x, f] = jnp.where(first_in, tiles[f], 0.0)
        free[x] = jnp.where(first_in, tiles[3], 0.0)

    loop(unpack, UNROLL)

    for level in range(1, LEVELS):
        step, spacing = 2 ** (level - 1), 2**level
        cells = (place >= 0) & (place <= 8 * LANES - 1 - spacing) & (rows < 8 - step)
        for p in range(step):
            scale[level - 1, p] = zero

        def fill_scale(x, i, u):
            total = young[x] + young[x + step]
            total = total + roll(total, -step, 0)
            total = total + roll(total, -spacing, 1)
            inside = cells & (x < COUNT - step)
            scale[level - 1, x + PAD] = jnp.where(inside, (0.125 * spacing) * total, 0.0)

        def fill_gain(x, i, u):
            total = scale[level - 1, x + PAD] + scale[level - 1, x + PAD - step]
            total = total + roll(total, step, 0)
            total = total + roll(total, spacing, 1)
            gain[level - 1, x] = GAIN * free[x] / jnp.maximum(total, TINY)

        for p in range(PAD):
            scale[level - 1, p] = zero
        loop(fill_scale, UNROLL)
        loop(fill_gain, UNROLL)

    def put_modes(x, fields, step, spacing):
        modes = to_modes([[f] for f in fields], step, spacing)
        for k, key in enumerate(KEYS):
            mode[x, k] = modes[key][0]

    def sweep(level, finish):
        step, spacing = 2 ** (level - 1), 2**level
        for p in range(step):
            for k in range(12):
                ahead[p, k] = zero

        def body(x, i, u):
            low = {key: mode[x, k] for k, key in enumerate(KEYS)}
            high = {key: mode[x + step, k] for k, key in enumerate(KEYS)}
            to_low, to_high = cell(low, high, scale[level - 1, x + PAD])
            modes = {key: [to_low[key] + ahead[x, k]] for k, key in enumerate(KEYS)}
            for k, key in enumerate(KEYS):
                ahead[x + step, k] = to_high[key]
            applied = from_modes(modes, step, spacing)
            finish(x, i, u, [a[0] for a in applied])

        loop(body, UNROLL_SWEEP)

    for level in range(1, LEVELS):
        step, spacing = 2 ** (level - 1), 2**level

        def smooth(x, i, u):
            fields = []
            for f in range(3):
                if level == 1:
                    now = res[0, x, f]
                else:
                    reach = step // 2
                    sides = spread[PAD + x - reach, f] + spread[PAD + x + reach, f]
                    now = jnp.where(node_in, spread[PAD + x, f] + 0.5 * sides, 0.0)
                    res[level - 1, x, f] = now
                fields.append(gain[level - 1, x] * now)
                value[level - 1, x, f] = fields[f]
            put_modes(x, fields, step, spacing)

        def restrict(x, i, u, applied):
            for f in range(3):
                rest = res[level - 1, x, f] - applied[f]
                spread[PAD + x, f] = spread_plane([rest], step, spacing)[0]

        def correct(x, i, u, applied):
            for f in range(3):
                rest = res[level - 1, x, f] - applied[f]
                spread[PAD + x, f] = value[level - 1, x, f] + gain[level - 1, x] * rest

        loop(smooth, UNROLL)
        sweep(level, restrict if level < LEVELS - 1 else correct)

    for level in range(LEVELS - 2, 0, -1):
        step, spacing = 2 ** (level - 1), 2**level

        def prolong(x, i, u):
            fields = []
            for f in range(3):
                sides = spread[PAD + x - step, f] + spread[PAD + x + step, f]
                along = spread[PAD + x, f] + 0.5 * sides
                along = spread_plane([along], step, spacing)[0]
                fields.append(jnp.where(node_in, value[level - 1, x, f] + 0.125 * along, 0.0))
                value[level - 1, x, f] = fields[f]
            put_modes(x, fields, step, spacing)

        def correct(x, i, u, applied):
            fields = []
            for f in range(3):
                rest = res[level - 1, x, f] - applied[f]
                fields.append(value[level - 1, x, f] + gain[level - 1, x] * rest)
            if level > 1:
                for f in range(3):
                    spread[PAD + x, f] = fields[f]
                return
            packed = roll(fields[0], -34, 1)
            for f in range(1, 3):
                packed = jnp.where(lanes < EDGE * f, packed, roll(fields[f], EDGE * f - 34, 1))
            out_ref[i, u + 1] = packed
            if u == 0:

                @pl.when(i > 0)
                def _():
                    out_ref[i - 1, 5] = packed

            if u == 3:

                @pl.when(i < COUNT // 4 - 1)
                def _():
                    out_ref[i + 1, 0] = packed

        loop(prolong, UNROLL)
        sweep(level, correct)
    out_ref[0, 0] = zero
    out_ref[COUNT // 4 - 1, 5] = zero


LAST_SCRATCH = (
    (SLAB + 4, 3, 2, 8, WIDE),
    (SLAB + 2, 12, 2, 8, WIDE),
    (12, 2, 8, WIDE),
    (12, 2, 8, WIDE),
    (SLAB + 2, 3, 2, 8, LANES),
)


def last_kernel(own_ref, value_ref, scale_ref, gain_ref, in_ref, out_ref, coarse, mode, ahead, node, field):
    lanes = lanes_of((8, LANES))
    for n in range(SLAB + 4):
        slot, parity = n // 2, n % 2
        for i in range(3):
            planes = []
            for e in range(2):
                parts = [
                    roll(in_ref[e * 8 + parity * 4 + q, slot], QUARTER * q - 2 - EDGE * i, 1)
                    for q in range(4)
                ]
                main = parts[0]
                for q in range(1, 4):
                    main = jnp.where(lanes < QUARTER * q, main, parts[q])
                side = jnp.where(lanes < 64, parts[3], parts[0])
                planes.append(jnp.concatenate([main, side], axis=1))
            planes = spread_plane(planes, 1, 1)
            for e in range(2):
                coarse[n, i, e] = planes[e]

    def prolong(n, carry):
        fields = []
        for i in range(3):
            planes = []
            for e in range(2):
                along = coarse[n + 1, i, e] + 0.5 * (coarse[n, i, e] + coarse[n + 2, i, e])
                planes.append(value_ref[n, i, e] + 0.125 * along)
                field[n, i, e] = planes[e][:, :LANES]
            fields.append(planes)
        modes = to_modes(fields, 1, 1)
        for k, key in enumerate(KEYS):
            for e in range(2):
                mode[n, k, e] = modes[key][e]
        return carry

    fori(SLAB + 2, prolong, LAST_UNROLL)

    for k in range(12):
        for e in range(2):
            ahead[k, e] = jnp.zeros((8, WIDE), F32)

    for n in range(SLAB + 1):
        x = n - 1
        for e in range(2):
            for t in range(2):
                part = slice(t * LANES, (t + 1) * LANES)
                low = {key: mode[n, k, e, :, part] for k, key in enumerate(KEYS)}
                high = {key: mode[n + 1, k, e, :, part] for k, key in enumerate(KEYS)}
                to_low, to_high = cell(low, high, scale_ref[n, e, :, part])
                for k, key in enumerate(KEYS):
                    if x >= 0:
                        node[k, e, :, part] = to_low[key] + ahead[k, e, :, part]
                    ahead[k, e, :, part] = to_high[key]
        if x < 0:
            continue
        modes = {key: [node[k, e] for e in range(2)] for k, key in enumerate(KEYS)}
        applied = from_modes(modes, 1, 1)
        for i in range(3):
            for e in range(2):
                rest = own_ref[x, i, e] - applied[i][e][:, :LANES]
                total = field[n, i, e] + gain_ref[x, e] * rest
                out_ref[i, pl.ds(e * 8 + x, 8, stride=16), :] = own_ref[x, 4, e] * total


def shapes(*sizes):
    return [jax.ShapeDtypeStruct(size, F32) for size in sizes]


def scratch(*sizes):
    return [pltpu.VMEM(size, F32) for size in sizes]


def call(kernel, name, out, scratches, scalars, arrays):
    specs = [pl.BlockSpec(memory_space=pltpu.SMEM)] * len(scalars)
    specs += [pl.BlockSpec(memory_space=pltpu.VMEM)] * len(arrays)
    return pl.pallas_call(
        kernel,
        out_shape=out,
        in_specs=specs,
        out_specs=[pl.BlockSpec(memory_space=pltpu.VMEM)] * len(out),
        scratch_shapes=scratches,
        compiler_params=pltpu.CompilerParams(vmem_limit_bytes=VMEM_BYTES),
        name=name,
    )(*scalars, *arrays)


def on_device(right_side, density, fixed_mask):
    slab, line = lax.axis_index("gx"), lax.axis_index("gy")
    slabs, lines = lax.axis_size("gx"), lax.axis_size("gy")
    core = slab % 2
    start = LANES * line + QUARTER * (slab % 4) - REACH
    meta = jnp.stack([slab, line, core, start]).astype(jnp.int32)
    rows = 16 * SLAB

    own, first, last = call(
        edges_kernel,
        "edges",
        shapes((SLAB, 5, 2, 8, LANES), (SLAB, 2, 2, 8, LANES), (SLAB, 2, 2, 8, LANES)),
        [],
        [],
        [right_side.reshape(3, rows, LANES), density.reshape(rows, LANES), fixed_mask.reshape(rows, LANES)],
    )
    after = lax.ppermute(first, "gy", [((j + 1) % lines, j) for j in range(lines)])
    before = lax.ppermute(last, "gy", [(j, (j + 1) % lines) for j in range(lines)])

    def columns(begin):
        parts = [lax.dynamic_slice_in_dim(a, begin, 3, axis=0) for a in (own, after, before)]
        return jnp.concatenate(parts, axis=1)

    pair = lax.ppermute(columns(5 * (1 - core)), "gx", [(i, i ^ 1) for i in range(slabs)])
    swaps = [(i, (i + 1) % slabs) for i in range(1, slabs, 2)]
    far = lax.ppermute(columns(5 * core), "gx", swaps + [(b, a) for a, b in swaps])

    packed, value, scale, gain = call(
        fine_kernel,
        "fine",
        shapes(
            (slabs, 4, 4, 8, LANES),
            (SLAB + 2, 3, 2, 8, WIDE),
            (SLAB + 1, 2, 8, WIDE),
            (SLAB, 2, 8, LANES),
        ),
        scratch(*FINE_SCRATCH),
        [meta],
        [own, after, before, pair, far],
    )
    packed = lax.all_to_all(packed, "gx", 0, 0)
    (result,) = call(
        coarse_kernel,
        "coarse",
        shapes((slabs, 6, 8, LANES)),
        scratch(*COARSE_SCRATCH),
        [meta],
        [packed.reshape(COUNT, 4, 8, LANES)],
    )
    result = lax.all_to_all(result, "gx", 0, 0)
    (correction,) = call(
        last_kernel,
        "last",
        shapes((3, rows, LANES)),
        scratch(*LAST_SCRATCH),
        [],
        [own, value, scale, gain, result],
    )
    return correction.reshape(right_side.shape)


def solution(mesh):
    in_specs = (P(None, None, "gx", "gy"), P(None, "gx", "gy"), P(None, "gx", "gy"))
    out_specs = P(None, None, "gx", "gy")
    return jax.shard_map(
        on_device, mesh=mesh, in_specs=in_specs, out_specs=out_specs, check_vma=False
    )
```

```python
import jax
import jax.numpy as jnp
from jax import lax
from jax.experimental import pallas as pl
from jax.experimental.pallas import tpu as pltpu
from jax.sharding import PartitionSpec as P

LEVELS = 4
Q = 16
JACOBI_WEIGHT = 0.6
SOFT_FLOOR = 0.1
LAME_FIRST = 0.3 / (1.3 * 0.4)
SHEAR_MOD = 0.5 / 1.3
RATIO = LAME_FIRST / SHEAR_MOD
UNIT = SHEAR_MOD / 16.0
GAIN = JACOBI_WEIGHT / ((RATIO + 4.0) * 16.0 / 9.0)
TINY = 1e-30

SLAB = 8
LANES = 128
FINE_UNROLL = 11
LAST_UNROLL = 10
EDGE = 40
REACH = 36
WINDOW = 100
PIECE = WINDOW // 4
BACK = 66
KEYS = [(i, az, ay) for i in range(3) for az in range(2) for ay in range(2)]
VMEM_BYTES = 50 * 1024 * 1024
F32 = jnp.float32


def roll(value, shift, axis):
    shift %= value.shape[axis]
    return value if shift == 0 else pltpu.roll(value, shift, axis)


def z_up(planes, step):
    if len(planes) == 1:
        return [roll(planes[0], -step, 0)]
    return [planes[1], roll(planes[0], -1, 0)]


def z_down(planes, step):
    if len(planes) == 1:
        return [roll(planes[0], step, 0)]
    return [roll(planes[1], 1, 0), planes[0]]


def fori(count, body, unroll):
    if unroll == count:
        for n in range(count):
            body(n, 0)
    else:
        lax.fori_loop(0, count, body, 0)


def rows_of(shape):
    return lax.broadcasted_iota(jnp.int32, shape, 0)


def lanes_of(shape):
    return lax.broadcasted_iota(jnp.int32, shape, 1)


def to_modes(fields, step, spacing):
    modes = {}
    for i, planes in enumerate(fields):
        ahead = [roll(p, -spacing, 1) for p in planes]
        for ay, along in ((0, [b + a for a, b in zip(planes, ahead)]), (1, [b - a for a, b in zip(planes, ahead)])):
            above = z_up(along, step)
            modes[i, 0, ay] = [b + a for a, b in zip(along, above)]
            modes[i, 1, ay] = [b - a for a, b in zip(along, above)]
    return modes


def from_modes(modes, step, spacing):
    fields = []
    for i in range(3):
        along = []
        for ay in range(2):
            low = [s - d for s, d in zip(modes[i, 0, ay], modes[i, 1, ay])]
            high = z_down([s + d for s, d in zip(modes[i, 0, ay], modes[i, 1, ay])], step)
            along.append([a + b for a, b in zip(low, high)])
        fields.append([(s - d) + roll(s + d, spacing, 1) for s, d in zip(along[0], along[1])])
    return fields


def cell(low, high, scale):
    full = {}
    for i, az, ay in KEYS:
        if az or ay:
            full[i, az, 0, ay] = high[i, az, ay] + low[i, az, ay]
        full[i, az, 1, ay] = high[i, az, ay] - low[i, az, ay]

    def mode(i, *dims):
        return full[i, int(0 in dims), int(1 in dims), int(2 in dims)]

    out = {}

    def put(value, i, *dims):
        out[i, int(0 in dims), int(1 in dims), int(2 in dims)] = value

    twice = 2.0 * scale
    half = 0.5 * scale * (RATIO / 1.5)
    third = scale * (1.0 / 3.0)
    trace = (RATIO * scale) * (mode(0, 0) + mode(1, 1) + mode(2, 2))
    for i in range(3):
        put(trace + twice * mode(i, i), i, i)
    for i, j in ((0, 1), (0, 2), (1, 2)):
        shear = scale * (mode(i, j) + mode(j, i))
        put(shear, i, j)
        put(shear, j, i)
    for q in range(3):
        p, r = [d for d in range(3) if d != q]
        first, second = mode(p, p, q), mode(r, r, q)
        both = half * (first + second)
        put(both + scale * first, p, p, q)
        put(both + scale * second, r, r, q)
    others = [[d for d in range(3) if d != i] for i in range(3)]
    total = mode(0, *others[0]) + mode(1, *others[1]) + mode(2, *others[2])
    for i in range(3):
        put(third * (total + mode(i, *others[i])), i, *others[i])
    ninth = scale * ((RATIO + 4.0) / 9.0)
    for i in range(3):
        put(ninth * mode(i, 0, 1, 2), i, 0, 1, 2)

    to_low, to_high = {}, {}
    for i, az, ay in KEYS:
        difference = out[i, az, 1, ay]
        if az or ay:
            to_low[i, az, ay] = out[i, az, 0, ay] - difference
            to_high[i, az, ay] = out[i, az, 0, ay] + difference
        else:
            to_low[i, az, ay] = -difference
            to_high[i, az, ay] = difference
    return to_low, to_high


def spread_plane(planes, step, spacing):
    rows = rows_of(planes[0].shape)
    above, below = z_up(planes, step), z_down(planes, step)
    if len(planes) == 1:
        above = [jnp.where(rows < 8 - step, above[0], 0.0)]
        below = [jnp.where(rows >= step, below[0], 0.0)]
    else:
        above = [above[0], jnp.where(rows < 7, above[1], 0.0)]
        below = [jnp.where(rows >= 1, below[0], 0.0), below[1]]
    along = [p + 0.5 * (a + b) for p, a, b in zip(planes, above, below)]
    return [p + 0.5 * (roll(p, spacing, 1) + roll(p, -spacing, 1)) for p in along]


def edges_kernel(right_ref, density_ref, mask_ref, own_ref, first_ref, last_ref):
    lanes = lanes_of((8, LANES))
    for x in range(SLAB):
        for e in range(2):
            rows = pl.ds(e * 8 + x, 8, stride=16)
            free = 1.0 - mask_ref[rows, :].astype(F32)
            level = density_ref[rows, :].astype(F32) / (Q - 1)
            young = SOFT_FLOOR + (1.0 - SOFT_FLOOR) * (level * level * level)
            fields = [free * right_ref[i, rows, :] for i in range(3)] + [UNIT * young, free]
            for f, value in enumerate(fields):
                own_ref[x, f, e] = value
            for group in range(2):
                members = fields[3 * group : 3 * group + 3]
                first = last = None
                for n, value in enumerate(members):
                    begin = roll(value, EDGE * n, 1)
                    end = roll(value, EDGE * n - (LANES - EDGE), 1)
                    first = begin if n == 0 else jnp.where(lanes < EDGE * n, first, begin)
                    last = end if n == 0 else jnp.where(lanes < EDGE * n, last, end)
                first_ref[x, group, e] = first
                last_ref[x, group, e] = last


WIDE = 2 * LANES

FINE_SCRATCH = (
    (SLAB + 4, 3, 2, 8, WIDE),
    (SLAB + 5, 2, 8, WIDE),
    (SLAB + 4, 12, 2, 8, WIDE),
    (12, 2, 8, WIDE),
    (12, 2, 8, WIDE),
    (5, SLAB, 2, 8, WIDE),
)


def fine_kernel(
    meta_ref, own_ref, after_ref, before_ref, pair_ref, far_ref,
    out_ref, value_ref, scale_out_ref, gain_ref,
    res, scale, mode, ahead, node, gather,
):
    slab, line, core = meta_ref[0], meta_ref[1], meta_ref[2]
    lanes = lanes_of((8, LANES))
    wide = lanes_of((8, WIDE))
    rows = rows_of((8, WIDE))
    local = jnp.where(wide < 192, wide, wide - WIDE)
    place = local + LANES * line
    node_in = (place >= 0) & (place < 8 * LANES) & (local >= -EDGE) & (local < LANES + EDGE)
    cell_in = (place >= 0) & (place < 8 * LANES - 1)
    first_slab, last_slab = slab == 0, slab == 15

    def field(x, f, e):
        group, n = f // 3, f % 3
        if 0 <= x < SLAB:
            mid, hi, lo = own_ref[x, f, e], after_ref[x, group, e], before_ref[x, group, e]
        else:
            p = x + 3 if x < 0 else x - SLAB
            is_pair = (core == 1) if x < 0 else (core == 0)
            mid, hi, lo = (
                jnp.where(is_pair, pair_ref[p, s, e], far_ref[p, s, e])
                for s in (f, 5 + group, 7 + group)
            )
        hi = roll(hi, -EDGE * n, 1)
        lo = roll(lo, (LANES - EDGE) - EDGE * n, 1)
        return jnp.concatenate([mid, jnp.where(lanes < 64, hi, lo)], axis=1)

    def inside(mask, x, top):
        if x < 0:
            return mask & jnp.logical_not(first_slab)
        if x >= top:
            return mask & jnp.logical_not(last_slab)
        return mask

    for x in range(-3, SLAB + 2):
        for e in range(2):
            cells = inside(cell_in, x, SLAB - 1)
            if e == 1:
                cells = cells & (rows < 7)
            scale[x + 3, e] = jnp.where(cells, field(x, 3, e), 0.0)

    for x in range(-2, SLAB + 2):
        total = []
        for e in range(2):
            total.append(scale[x + 3, e] + scale[x + 2, e])
        total = [a + b for a, b in zip(total, z_down(total, 1))]
        total = [a + roll(a, 1, 1) for a in total]
        nodes = inside(node_in, x, SLAB)
        gains = []
        for e in range(2):
            free = jnp.where(nodes, field(x, 4, e), 0.0)
            gains.append(GAIN * free / jnp.maximum(total[e], TINY))
            if 0 <= x < SLAB:
                gain_ref[x, e] = gains[e][:, :LANES]
                gather[3, x, e] = free
        values = []
        for i in range(3):
            planes = []
            for e in range(2):
                now = jnp.where(nodes, field(x, i, e), 0.0)
                res[x + 2, i, e] = now
                planes.append(gains[e] * now)
                if -1 <= x < SLAB + 1:
                    value_ref[x + 1, i, e] = planes[e]
            values.append(planes)
        modes = to_modes(values, 1, 1)
        for k, key in enumerate(KEYS):
            for e in range(2):
                mode[x + 2, k, e] = modes[key][e]
    for x in range(-1, SLAB):
        for e in range(2):
            scale_out_ref[x + 1, e] = scale[x + 3, e]

    for k in range(12):
        for e in range(2):
            ahead[k, e] = jnp.zeros((8, WIDE), F32)

    def sweep(n, carry):
        for e in range(2):
            for t in range(2):
                part = slice(t * LANES, (t + 1) * LANES)
                low = {key: mode[n, k, e, :, part] for k, key in enumerate(KEYS)}
                high = {key: mode[n + 1, k, e, :, part] for k, key in enumerate(KEYS)}
                to_low, to_high = cell(low, high, scale[n + 1, e, :, part])
                for k, key in enumerate(KEYS):
                    node[k, e, :, part] = to_low[key] + ahead[k, e, :, part]
                    ahead[k, e, :, part] = to_high[key]
        modes = {key: [node[k, e] for e in range(2)] for k, key in enumerate(KEYS)}
        applied = from_modes(modes, 1, 1)
        x = n - 2
        keep = node_in & jnp.logical_not((x < 0) & first_slab) & jnp.logical_not((x >= SLAB) & last_slab)
        for i in range(3):
            rest = [jnp.where(keep, res[n, i, e] - applied[i][e], 0.0) for e in range(2)]
            rest = spread_plane(rest, 1, 1)
            for e in range(2):
                res[n, i, e] = rest[e]
        return carry

    fori(SLAB + 3, sweep, FINE_UNROLL)

    for x in range(SLAB):
        for e in range(2):
            for i in range(3):
                gather[i, x, e] = res[x + 2, i, e] + 0.5 * (res[x + 1, i, e] + res[x + 3, i, e])
            gather[4, x, e] = field(x, 3, e)
    source = rows_of((WIDE, WIDE))
    target = lanes_of((WIDE, WIDE))
    y = 2 * (target % LANES) - REACH + target // LANES
    choose = ((target % LANES) < WINDOW) & (source == (y + WIDE) % WIDE)
    rows_in = gather[...].reshape(5 * SLAB * 16, WIDE)
    parts = jnp.dot(
        rows_in, choose.astype(F32), preferred_element_type=F32, precision=lax.Precision.HIGHEST
    )
    parts = parts.reshape(5, SLAB, 2, 8, WIDE)
    for x in range(SLAB):
        for e in range(2):
            for parity in range(2):
                part = slice(parity * LANES, (parity + 1) * LANES)
                young = parts[4, x, e, :, part]
                for f in range(4):
                    piece = roll(young, WINDOW - PIECE * f, 1)
                    out_ref[e * 4 + (x % 2) * 2 + parity, x // 2, f] = jnp.where(
                        lanes < WINDOW, parts[f, x, e, :, part], piece
                    )


OWN = 32
HALO = 18
COUNT = OWN + HALO
PAD = 4
COARSE_SCRATCH = (
    (COUNT + PAD, 8, LANES),
    (COUNT, 8, LANES),
    (3, COUNT, 3, 8, LANES),
    (3, COUNT, 3, 8, LANES),
    (3, COUNT, 8, LANES),
    (3, PAD + COUNT, 8, LANES),
    (2 * PAD + COUNT, 3, 8, LANES),
    (COUNT + PAD, 12, 8, LANES),
    (COUNT + PAD, 12, 8, LANES),
    (OWN + 8, 2, 8, LANES),
)
POINTS = {1: (50, 10), 2: (48, 12), 3: (44, 11)}
SWEEPS = {1: (50, 10), 2: (48, 12), 3: (44, 11)}
POINTS_UP = {2: (39, 13), 1: (36, 12)}
SWEEPS_UP = {2: (39, 13), 1: (36, 12)}


def coarse_kernel(meta_ref, own_ref, side_ref, out_ref, young, free, res, value, gain, scale, spread, mode, ahead, last):
    half, origin = meta_ref[3], meta_ref[4]
    shape = (8, LANES)
    lanes = lanes_of(shape)
    rows = rows_of(shape)
    place = 2 * lanes + origin
    node_in = (place >= 0) & (place < 8 * LANES)
    first_in = node_in & (lanes >= 1) & (lanes < WINDOW - 1)
    zero = jnp.zeros(shape, F32)

    def loop(body, planes):
        count, unroll = planes
        begin = (COUNT - count) * half

        def step(n, carry):
            for u in range(unroll):
                body(begin + unroll * n + u)
            return carry

        lax.fori_loop(0, count // unroll, step, 0)

    for p in range(2 * PAD + COUNT):
        for f in range(3):
            spread[p, f] = zero
    for p in range(PAD):
        young[COUNT + p] = zero
        for k in range(12):
            mode[COUNT + p, k] = zero
        for level in range(3):
            scale[level, p] = zero

    def unpack(tiles, p):
        total = roll(tiles[0], -WINDOW, 1)
        for f in range(1, 4):
            total = jnp.where(lanes >= PIECE * f, roll(tiles[f], PIECE * f - WINDOW, 1), total)
        young[p] = total
        for f in range(3):
            res[0, p, f] = jnp.where(first_in, tiles[f], 0.0)
        free[p] = jnp.where(first_in, tiles[3], 0.0)

    for p in range(OWN):
        unpack([own_ref[p, f] for f in range(4)], p + HALO * half)
    for p in range(HALO):
        unpack([side_ref[p, f] for f in range(4)], p + OWN * (1 - half))

    for level in range(1, LEVELS):
        step, spacing = 2 ** (level - 1), 2**level
        cells = (place >= 0) & (place <= 8 * LANES - 1 - spacing) & (rows < 8 - step)

        def fill_scale(p):
            total = young[p] + young[p + step]
            total = total + roll(total, -step, 0)
            total = total + roll(total, -step, 1)
            inside = cells & (p + (2 * OWN - COUNT) * half < 2 * OWN - step)
            scale[level - 1, p + PAD] = jnp.where(inside, (0.125 * spacing) * total, 0.0)

        def fill_gain(p):
            total = scale[level - 1, p + PAD] + scale[level - 1, p + PAD - step]
            total = total + roll(total, step, 0)
            total = total + roll(total, step, 1)
            gain[level - 1, p] = GAIN * free[p] / jnp.maximum(total, TINY)

        loop(fill_scale, (COUNT, 25))
        loop(fill_gain, (COUNT, 25))

    def put_modes(p, fields, step):
        modes = to_modes([[f] for f in fields], step, step)
        for k, key in enumerate(KEYS):
            mode[p, k] = modes[key][0]

    def sweep(level, planes, finish):
        step = 2 ** (level - 1)
        begin = (COUNT - planes[0]) * half
        for p in range(step):
            for k in range(12):
                ahead[begin + p, k] = zero

        def body(p):
            low = {key: mode[p, k] for k, key in enumerate(KEYS)}
            high = {key: mode[p + step, k] for k, key in enumerate(KEYS)}
            to_low, to_high = cell(low, high, scale[level - 1, p + PAD])
            modes = {key: [to_low[key] + ahead[p, k]] for k, key in enumerate(KEYS)}
            for k, key in enumerate(KEYS):
                ahead[p + step, k] = to_high[key]
            applied = from_modes(modes, step, step)
            finish(p, [a[0] for a in applied])

        loop(body, planes)

    for level in range(1, LEVELS):
        step = 2 ** (level - 1)

        def smooth(p):
            fields = []
            for f in range(3):
                if level == 1:
                    now = res[0, p, f]
                else:
                    reach = step // 2
                    sides = spread[PAD + p - reach, f] + spread[PAD + p + reach, f]
                    now = jnp.where(node_in, spread[PAD + p, f] + 0.5 * sides, 0.0)
                    res[level - 1, p, f] = now
                fields.append(gain[level - 1, p] * now)
                value[level - 1, p, f] = fields[f]
            put_modes(p, fields, step)

        def restrict(p, applied):
            for f in range(3):
                rest = res[level - 1, p, f] - applied[f]
                spread[PAD + p, f] = spread_plane([rest], step, step)[0]

        def correct(p, applied):
            for f in range(3):
                rest = res[level - 1, p, f] - applied[f]
                spread[PAD + p, f] = value[level - 1, p, f] + gain[level - 1, p] * rest

        loop(smooth, POINTS[level])
        sweep(level, SWEEPS[level], restrict if level < LEVELS - 1 else correct)

    last[3, 0] = last[3, 1] = zero
    last[OWN + 4, 0] = last[OWN + 4, 1] = zero
    for level in range(LEVELS - 2, 0, -1):
        step = 2 ** (level - 1)

        def prolong(p):
            fields = []
            for f in range(3):
                sides = spread[PAD + p - step, f] + spread[PAD + p + step, f]
                along = spread[PAD + p, f] + 0.5 * sides
                along = spread_plane([along], step, step)[0]
                fields.append(jnp.where(node_in, value[level - 1, p, f] + 0.125 * along, 0.0))
                value[level - 1, p, f] = fields[f]
            put_modes(p, fields, step)

        def correct(p, applied):
            fields = []
            for f in range(3):
                rest = res[level - 1, p, f] - applied[f]
                fields.append(value[level - 1, p, f] + gain[level - 1, p] * rest)
            if level > 1:
                for f in range(3):
                    spread[PAD + p, f] = fields[f]
                return
            place = p + 4 - HALO * half
            for t in range(2):
                third = roll(fields[2], BACK - 17 - (BACK // 2) * t, 1)
                last[place, t] = jnp.where(lanes < BACK, roll(fields[t], -17, 1), third)

        loop(prolong, POINTS_UP[level])
        sweep(level, SWEEPS_UP[level], correct)
    for d in range(8):
        for p in range(6):
            for t in range(2):
                out_ref[d, p, t] = last[4 * d + p + 3, t]


LAST_SCRATCH = (
    (SLAB + 4, 3, 2, 8, WIDE),
    (SLAB + 2, 12, 2, 8, WIDE),
    (12, 2, 8, WIDE),
    (12, 2, 8, WIDE),
    (SLAB + 2, 3, 2, 8, LANES),
    (SLAB + 4, 3, 2, 8, WIDE),
)


def last_kernel(own_ref, value_ref, scale_ref, gain_ref, in_ref, out_ref, coarse, mode, ahead, node, field, gather):
    lanes = lanes_of((8, LANES))
    for n in range(SLAB + 4):
        slot, parity = n // 2, n % 2
        for e in range(2):
            tiles = [[in_ref[e * 4 + parity * 2 + w, slot, t] for t in range(2)] for w in range(2)]
            for w in range(2):
                part = slice(w * LANES, (w + 1) * LANES)
                first, second = tiles[w]
                third = jnp.where(
                    lanes < BACK // 2, roll(first, -BACK, 1), roll(second, BACK // 2 - BACK, 1)
                )
                gather[n, 0, e, :, part] = first
                gather[n, 1, e, :, part] = second
                gather[n, 2, e, :, part] = third
    source = rows_of((WIDE, WIDE))
    target = lanes_of((WIDE, WIDE))
    y = 2 * (source % LANES) - 2 + source // LANES
    choose = ((source % LANES) < BACK) & (target == (y + WIDE) % WIDE)
    full = jnp.dot(
        gather[...].reshape((SLAB + 4) * 48, WIDE),
        choose.astype(F32),
        preferred_element_type=F32,
        precision=lax.Precision.HIGHEST,
    )
    full = full.reshape(SLAB + 4, 3, 2, 8, WIDE)
    for n in range(SLAB + 4):
        for i in range(3):
            planes = spread_plane([full[n, i, e] for e in range(2)], 1, 1)
            for e in range(2):
                coarse[n, i, e] = planes[e]

    def prolong(n, carry):
        fields = []
        for i in range(3):
            planes = []
            for e in range(2):
                along = coarse[n + 1, i, e] + 0.5 * (coarse[n, i, e] + coarse[n + 2, i, e])
                planes.append(value_ref[n, i, e] + 0.125 * along)
                field[n, i, e] = planes[e][:, :LANES]
            fields.append(planes)
        modes = to_modes(fields, 1, 1)
        for k, key in enumerate(KEYS):
            for e in range(2):
                mode[n, k, e] = modes[key][e]
        return carry

    fori(SLAB + 2, prolong, LAST_UNROLL)

    for k in range(12):
        for e in range(2):
            ahead[k, e] = jnp.zeros((8, WIDE), F32)

    for n in range(SLAB + 1):
        x = n - 1
        for e in range(2):
            for t in range(2):
                part = slice(t * LANES, (t + 1) * LANES)
                low = {key: mode[n, k, e, :, part] for k, key in enumerate(KEYS)}
                high = {key: mode[n + 1, k, e, :, part] for k, key in enumerate(KEYS)}
                to_low, to_high = cell(low, high, scale_ref[n, e, :, part])
                for k, key in enumerate(KEYS):
                    if x >= 0:
                        node[k, e, :, part] = to_low[key] + ahead[k, e, :, part]
                    ahead[k, e, :, part] = to_high[key]
        if x < 0:
            continue
        modes = {key: [node[k, e] for e in range(2)] for k, key in enumerate(KEYS)}
        applied = from_modes(modes, 1, 1)
        for i in range(3):
            for e in range(2):
                rest = own_ref[x, i, e] - applied[i][e][:, :LANES]
                total = field[n, i, e] + gain_ref[x, e] * rest
                out_ref[i, pl.ds(e * 8 + x, 8, stride=16), :] = own_ref[x, 4, e] * total


def shapes(*sizes):
    return [jax.ShapeDtypeStruct(size, F32) for size in sizes]


def scratch(*sizes):
    return [pltpu.VMEM(size, F32) for size in sizes]


def call(kernel, name, out, scratches, scalars, arrays):
    specs = [pl.BlockSpec(memory_space=pltpu.SMEM)] * len(scalars)
    specs += [pl.BlockSpec(memory_space=pltpu.VMEM)] * len(arrays)
    return pl.pallas_call(
        kernel,
        out_shape=out,
        in_specs=specs,
        out_specs=[pl.BlockSpec(memory_space=pltpu.VMEM)] * len(out),
        scratch_shapes=scratches,
        compiler_params=pltpu.CompilerParams(vmem_limit_bytes=VMEM_BYTES),
        name=name,
    )(*scalars, *arrays)


def on_device(right_side, density, fixed_mask):
    slab, line = lax.axis_index("gx"), lax.axis_index("gy")
    slabs, lines = lax.axis_size("gx"), lax.axis_size("gy")
    core = slab % 2
    half = slab // 8
    origin = LANES * line - REACH + core
    meta = jnp.stack([slab, line, core, half, origin]).astype(jnp.int32)
    groups = [list(range(8)), list(range(8, 16))]
    rows = 16 * SLAB

    own, first, last = call(
        edges_kernel,
        "edges",
        shapes((SLAB, 5, 2, 8, LANES), (SLAB, 2, 2, 8, LANES), (SLAB, 2, 2, 8, LANES)),
        [],
        [],
        [right_side.reshape(3, rows, LANES), density.reshape(rows, LANES), fixed_mask.reshape(rows, LANES)],
    )
    after = lax.ppermute(first, "gy", [((j + 1) % lines, j) for j in range(lines)])
    before = lax.ppermute(last, "gy", [(j, (j + 1) % lines) for j in range(lines)])

    def columns(begin):
        parts = [lax.dynamic_slice_in_dim(a, begin, 3, axis=0) for a in (own, after, before)]
        return jnp.concatenate(parts, axis=1)

    pair = lax.ppermute(columns(5 * (1 - core)), "gx", [(i, i ^ 1) for i in range(slabs)])
    swaps = [(i, (i + 1) % slabs) for i in range(1, slabs, 2)]
    far = lax.ppermute(columns(5 * core), "gx", swaps + [(b, a) for a, b in swaps])

    packed, value, scale, gain = call(
        fine_kernel,
        "fine",
        shapes(
            (8, 4, 4, 8, LANES),
            (SLAB + 2, 3, 2, 8, WIDE),
            (SLAB + 1, 2, 8, WIDE),
            (SLAB, 2, 8, LANES),
        ),
        scratch(*FINE_SCRATCH),
        [meta],
        [own, after, before, pair, far],
    )
    packed = lax.all_to_all(packed, "gx", 0, 0, axis_index_groups=groups)
    packed = packed.reshape(OWN, 4, 8, LANES)
    side = lax.dynamic_slice_in_dim(packed, (OWN - HALO) * (1 - half), HALO, axis=0)
    side = lax.ppermute(side, "gx", [(i, i ^ 8) for i in range(slabs)])
    (result,) = call(
        coarse_kernel,
        "coarse",
        shapes((8, 6, 2, 8, LANES)),
        scratch(*COARSE_SCRATCH),
        [meta],
        [packed, side],
    )
    result = lax.all_to_all(result, "gx", 0, 0, axis_index_groups=groups)
    (correction,) = call(
        last_kernel,
        "last",
        shapes((3, rows, LANES)),
        scratch(*LAST_SCRATCH),
        [],
        [own, value, scale, gain, result],
    )
    return correction.reshape(right_side.shape)


def solution(mesh):
    in_specs = (P(None, None, "gx", "gy"), P(None, "gx", "gy"), P(None, "gx", "gy"))
    out_specs = P(None, None, "gx", "gy")
    return jax.shard_map(
        on_device, mesh=mesh, in_specs=in_specs, out_specs=out_specs, check_vma=False
    )
```

```python
import jax
import jax.numpy as jnp
from jax import lax
from jax.experimental import pallas as pl
from jax.experimental.pallas import tpu as pltpu
from jax.sharding import PartitionSpec as P

LEVELS = 4
Q = 16
JACOBI_WEIGHT = 0.6
SOFT_FLOOR = 0.1
LAME_FIRST = 0.3 / (1.3 * 0.4)
SHEAR_MOD = 0.5 / 1.3
RATIO = LAME_FIRST / SHEAR_MOD
UNIT = SHEAR_MOD / 16.0
GAIN = JACOBI_WEIGHT / ((RATIO + 4.0) * 16.0 / 9.0)
TINY = 1e-30

SLAB = 8
LANES = 128
LAST_UNROLL = 10
EDGE = 40
REACH = 36
WINDOW = 100
PIECE = WINDOW // 4
BACK = 66
KEYS = [(i, az, ay) for i in range(3) for az in range(2) for ay in range(2)]
VMEM_BYTES = 32 * 1024 * 1024
EDGES_BYTES = 62 * 1024 * 1024
F32 = jnp.float32


def roll(value, shift, axis):
    shift %= value.shape[axis]
    return value if shift == 0 else pltpu.roll(value, shift, axis)


def z_up(planes, step):
    if len(planes) == 1:
        return [roll(planes[0], -step, 0)]
    return [planes[1], roll(planes[0], -1, 0)]


def z_down(planes, step):
    if len(planes) == 1:
        return [roll(planes[0], step, 0)]
    return [roll(planes[1], 1, 0), planes[0]]


def fori(count, body, unroll):
    if unroll == count:
        for n in range(count):
            body(n, 0)
    else:
        lax.fori_loop(0, count, body, 0)


def rows_of(shape):
    return lax.broadcasted_iota(jnp.int32, shape, 0)


def lanes_of(shape):
    return lax.broadcasted_iota(jnp.int32, shape, 1)


def to_modes(fields, step, spacing):
    modes = {}
    for i, planes in enumerate(fields):
        ahead = [roll(p, -spacing, 1) for p in planes]
        for ay, along in ((0, [b + a for a, b in zip(planes, ahead)]), (1, [b - a for a, b in zip(planes, ahead)])):
            above = z_up(along, step)
            modes[i, 0, ay] = [b + a for a, b in zip(along, above)]
            modes[i, 1, ay] = [b - a for a, b in zip(along, above)]
    return modes


def from_modes(modes, step, spacing):
    fields = []
    for i in range(3):
        along = []
        for ay in range(2):
            low = [s - d for s, d in zip(modes[i, 0, ay], modes[i, 1, ay])]
            high = z_down([s + d for s, d in zip(modes[i, 0, ay], modes[i, 1, ay])], step)
            along.append([a + b for a, b in zip(low, high)])
        fields.append([(s - d) + roll(s + d, spacing, 1) for s, d in zip(along[0], along[1])])
    return fields


def cell(low, high, scale):
    full = {}
    for i, az, ay in KEYS:
        if az or ay:
            full[i, az, 0, ay] = high[i, az, ay] + low[i, az, ay]
        full[i, az, 1, ay] = high[i, az, ay] - low[i, az, ay]

    def mode(i, *dims):
        return full[i, int(0 in dims), int(1 in dims), int(2 in dims)]

    out = {}

    def put(value, i, *dims):
        out[i, int(0 in dims), int(1 in dims), int(2 in dims)] = value

    twice = 2.0 * scale
    half = 0.5 * scale * (RATIO / 1.5)
    third = scale * (1.0 / 3.0)
    trace = (RATIO * scale) * (mode(0, 0) + mode(1, 1) + mode(2, 2))
    for i in range(3):
        put(trace + twice * mode(i, i), i, i)
    for i, j in ((0, 1), (0, 2), (1, 2)):
        shear = scale * (mode(i, j) + mode(j, i))
        put(shear, i, j)
        put(shear, j, i)
    for q in range(3):
        p, r = [d for d in range(3) if d != q]
        first, second = mode(p, p, q), mode(r, r, q)
        both = half * (first + second)
        put(both + scale * first, p, p, q)
        put(both + scale * second, r, r, q)
    others = [[d for d in range(3) if d != i] for i in range(3)]
    total = mode(0, *others[0]) + mode(1, *others[1]) + mode(2, *others[2])
    for i in range(3):
        put(third * (total + mode(i, *others[i])), i, *others[i])
    ninth = scale * ((RATIO + 4.0) / 9.0)
    for i in range(3):
        put(ninth * mode(i, 0, 1, 2), i, 0, 1, 2)

    to_low, to_high = {}, {}
    for i, az, ay in KEYS:
        difference = out[i, az, 1, ay]
        if az or ay:
            to_low[i, az, ay] = out[i, az, 0, ay] - difference
            to_high[i, az, ay] = out[i, az, 0, ay] + difference
        else:
            to_low[i, az, ay] = -difference
            to_high[i, az, ay] = difference
    return to_low, to_high


def spread_plane(planes, step, spacing):
    rows = rows_of(planes[0].shape)
    above, below = z_up(planes, step), z_down(planes, step)
    if len(planes) == 1:
        above = [jnp.where(rows < 8 - step, above[0], 0.0)]
        below = [jnp.where(rows >= step, below[0], 0.0)]
    else:
        above = [above[0], jnp.where(rows < 7, above[1], 0.0)]
        below = [jnp.where(rows >= 1, below[0], 0.0), below[1]]
    along = [p + 0.5 * (a + b) for p, a, b in zip(planes, above, below)]
    return [p + 0.5 * (roll(p, spacing, 1) + roll(p, -spacing, 1)) for p in along]


def edges_kernel(right_hbm, density_hbm, mask_hbm, own_ref, first_ref, last_ref, right_ref, density_ref, mask_ref, sems):
    copies = [
        pltpu.make_async_copy(source, target, sems.at[n])
        for n, (source, target) in enumerate(
            ((right_hbm, right_ref), (density_hbm, density_ref), (mask_hbm, mask_ref))
        )
    ]
    for copy in copies:
        copy.start()
    for copy in copies:
        copy.wait()
    lanes = lanes_of((8, LANES))
    for x in range(SLAB):
        for e in range(2):
            rows = pl.ds(e * 8 + x, 8, stride=16)
            free = 1.0 - mask_ref[rows, :].astype(F32)
            level = density_ref[rows, :].astype(F32) / (Q - 1)
            young = SOFT_FLOOR + (1.0 - SOFT_FLOOR) * (level * level * level)
            fields = [free * right_ref[i, rows, :] for i in range(3)] + [UNIT * young, free]
            for f, value in enumerate(fields):
                own_ref[x, f, e] = value
            for group in range(2):
                members = fields[3 * group : 3 * group + 3]
                first = last = None
                for n, value in enumerate(members):
                    begin = roll(value, EDGE * n, 1)
                    end = roll(value, EDGE * n - (LANES - EDGE), 1)
                    first = begin if n == 0 else jnp.where(lanes < EDGE * n, first, begin)
                    last = end if n == 0 else jnp.where(lanes < EDGE * n, last, end)
                first_ref[x, group, e] = first
                last_ref[x, group, e] = last


WIDE = 2 * LANES

FINE_SCRATCH = (
    (5, 3, 2, 8, WIDE),
    (5, 2, 8, WIDE),
    (5, 12, 2, 8, WIDE),
    (12, 2, 8, WIDE),
    (12, 2, 8, WIDE),
    (SLAB + 2, 3, 2, 8, WIDE),
)


class Fine:
    def __init__(self, meta_ref):
        slab, line, core = meta_ref[0], meta_ref[1], meta_ref[2]
        self.core = core
        self.lanes = lanes_of((8, LANES))
        wide = lanes_of((8, WIDE))
        self.rows = rows_of((8, WIDE))
        local = jnp.where(wide < 192, wide, wide - WIDE)
        place = local + LANES * line
        self.node_in = (
            (place >= 0) & (place < 8 * LANES) & (local >= -EDGE) & (local < LANES + EDGE)
        )
        self.cell_in = (place >= 0) & (place < 8 * LANES - 1)
        self.first_slab, self.last_slab = slab == 0, slab == 15

    def inside(self, mask, x, top):
        if x < 0:
            return mask & jnp.logical_not(self.first_slab)
        if x >= top:
            return mask & jnp.logical_not(self.last_slab)
        return mask

    def widen(self, n, mid, hi, lo):
        hi = roll(hi, -EDGE * n, 1)
        lo = roll(lo, (LANES - EDGE) - EDGE * n, 1)
        return jnp.concatenate([mid, jnp.where(self.lanes < 64, hi, lo)], axis=1)

    def cells(self, x, e, young):
        mask = self.inside(self.cell_in, x, SLAB - 1)
        if e == 1:
            mask = mask & (self.rows < 7)
        return jnp.where(mask, young, 0.0)

    def smooth(self, x, scales, fields):
        total = [a + b for a, b in zip(*scales)]
        total = [a + b for a, b in zip(total, z_down(total, 1))]
        total = [a + roll(a, 1, 1) for a in total]
        nodes = self.inside(self.node_in, x, SLAB)
        free = [jnp.where(nodes, f, 0.0) for f in fields[4]]
        gains = [GAIN * f / jnp.maximum(t, TINY) for f, t in zip(free, total)]
        res = [[jnp.where(nodes, r, 0.0) for r in fields[i]] for i in range(3)]
        values = [[g * r for g, r in zip(gains, planes)] for planes in res]
        return gains, res, values


def choose_class():
    source = rows_of((WIDE, WIDE))
    target = lanes_of((WIDE, WIDE))
    y = 2 * (target % LANES) - REACH + target // LANES
    return (((target % LANES) < WINDOW) & (source == (y + WIDE) % WIDE)).astype(F32)


def split_classes(rows_in):
    return jnp.dot(
        rows_in, choose_class(), preferred_element_type=F32, precision=lax.Precision.HIGHEST
    )


def put_smoothed(x, found, res_ref, mode_ref, gain_ref, value_ref, n_res, n_mode, n_gain, n_value):
    gains, res, values = found
    modes = to_modes(values, 1, 1)
    for e in range(2):
        for i in range(3):
            res_ref[n_res, i, e] = res[i][e]
            if n_value is not None:
                value_ref[n_value, i, e] = values[i][e]
        for k, key in enumerate(KEYS):
            mode_ref[n_mode, k, e] = modes[key][e]
        if n_gain is not None:
            gain_ref[n_gain, e] = gains[e][:, :LANES]


FINE_STATE = (
    (SLAB, 2, 8, WIDE),
    (SLAB, 3, 2, 8, WIDE),
    (SLAB, 12, 2, 8, WIDE),
    (SLAB, 3, 2, 8, WIDE),
    (SLAB, 2, 8, LANES),
    (4, 2, 8, WIDE),
    (2, SLAB, 2, 8, WIDE),
)


def fine_head_kernel(
    meta_ref, own_ref, after_ref, before_ref,
    scale, res, mode, value, gain, edge, split, gather,
):
    at = Fine(meta_ref)

    def field(x, f, e):
        group, n = f // 3, f % 3
        return at.widen(n, own_ref[x, f, e], after_ref[x, group, e], before_ref[x, group, e])

    for x in range(SLAB):
        for e in range(2):
            young = field(x, 3, e)
            gather[1, x, e] = young
            scale[x, e] = at.cells(x, e, young)
            free = jnp.where(at.node_in, field(x, 4, e), 0.0)
            gather[0, x, e] = free
            if x == 0:
                for i in range(3):
                    edge[i, e] = field(0, i, e)
                edge[3, e] = free
        if x == 0:
            continue
        fields = [[field(x, i, e) for e in range(2)] for i in range(3)]
        fields += [None, [gather[0, x, e] for e in range(2)]]
        scales = [[scale[x - d, e] for e in range(2)] for d in range(2)]
        put_smoothed(x, at.smooth(x, scales, fields), res, mode, gain, value, x, x, x, x)
    parts = split_classes(gather[...].reshape(2 * SLAB * 16, WIDE))
    split[...] = parts.reshape(2, SLAB, 2, 8, WIDE)


def fine_kernel(
    meta_ref, own_scale, own_res, own_mode, own_value, own_gain, edge, split, pair_ref, far_ref,
    out_ref, value_ref, scale_ref, gain_ref,
    res, scale, mode, ahead, node, gather,
):
    at = Fine(meta_ref)

    def field(x, f, e):
        group, n = f // 3, f % 3
        p = x + 3 if x < 0 else x - SLAB
        is_pair = (at.core == 1) if x < 0 else (at.core == 0)
        parts = [
            jnp.where(is_pair, pair_ref[p, s, e], far_ref[p, s, e]) for s in (f, 5 + group, 7 + group)
        ]
        return at.widen(n, *parts)

    def scale_at(x, e):
        return own_scale[x, e] if 0 <= x < SLAB else scale[x + 3 if x < 0 else x - SLAB + 3, e]

    def mode_at(x, k, e, part):
        if 1 <= x < SLAB:
            return own_mode[x, k, e, :, part]
        return mode[x + 2 if x < 1 else x - SLAB + 3, k, e, :, part]

    def res_at(x, i, e):
        return own_res[x, i, e] if 1 <= x < SLAB else res[x + 2 if x < 1 else x - SLAB + 3, i, e]

    for x in (-3, -2, -1, 8, 9):
        for e in range(2):
            scale[x + 3 if x < 0 else x - SLAB + 3, e] = at.cells(x, e, field(x, 3, e))
    for x in (-2, -1, 0, 8, 9):
        n = x + 2 if x < 1 else x - SLAB + 3
        if x == 0:
            fields = [[edge[i, e] for e in range(2)] for i in range(3)]
            fields += [None, [edge[3, e] for e in range(2)]]
        else:
            fields = [[field(x, i, e) if i != 3 else None for e in range(2)] for i in range(5)]
        scales = [[scale_at(x - d, e) for e in range(2)] for d in range(2)]
        found = at.smooth(x, scales, fields)
        inner = -1 <= x <= SLAB
        put_smoothed(
            x, found, res, mode, gain_ref, value_ref, n, n, 0 if x == 0 else None, x + 1 if inner else None
        )
    for x in range(1, SLAB):
        for e in range(2):
            gain_ref[x, e] = own_gain[x, e]
            for i in range(3):
                value_ref[x + 1, i, e] = own_value[x, i, e]
    for x in range(-1, SLAB):
        for e in range(2):
            scale_ref[x + 1, e] = scale_at(x, e)

    for x in range(-2, SLAB + 1):
        for e in range(2):
            for t in range(2):
                part = slice(t * LANES, (t + 1) * LANES)
                low = {key: mode_at(x, k, e, part) for k, key in enumerate(KEYS)}
                high = {key: mode_at(x + 1, k, e, part) for k, key in enumerate(KEYS)}
                to_low, to_high = cell(low, high, scale_at(x, e)[:, part])
                for k, key in enumerate(KEYS):
                    if x > -2:
                        node[k, e, :, part] = to_low[key] + ahead[k, e, :, part]
                    ahead[k, e, :, part] = to_high[key]
        if x == -2:
            continue
        applied = from_modes({key: [node[k, e] for e in range(2)] for k, key in enumerate(KEYS)}, 1, 1)
        keep = at.inside(at.node_in, x, SLAB)
        for i in range(3):
            planes = [jnp.where(keep, res_at(x, i, e) - applied[i][e], 0.0) for e in range(2)]
            planes = spread_plane(planes, 1, 1)
            for e in range(2):
                gather[x + 1, i, e] = planes[e]
    rows_in = [
        gather[x + 1, i, e] + 0.5 * (gather[x, i, e] + gather[x + 2, i, e])
        for x in range(SLAB)
        for i in range(3)
        for e in range(2)
    ]
    parts = split_classes(jnp.concatenate(rows_in, axis=0)).reshape(SLAB, 3, 2, 8, WIDE)
    for x in range(SLAB):
        for e in range(2):
            for parity in range(2):
                part = slice(parity * LANES, (parity + 1) * LANES)
                young = split[1, x, e, :, part]
                mains = [parts[x, i, e, :, part] for i in range(3)] + [split[0, x, e, :, part]]
                for f in range(4):
                    piece = roll(young, WINDOW - PIECE * f, 1)
                    out_ref[e * 4 + (x % 2) * 2 + parity, x // 2, f] = jnp.where(
                        at.lanes < WINDOW, mains[f], piece
                    )


OWN = 32
HALO = 18
COUNT = OWN + HALO
PAD = 4
RES = (COUNT, 3, 8, LANES)
GAINS = (3, COUNT, 8, LANES)
SCALES = (3, PAD + COUNT, 8, LANES)
SPREAD = (2 * PAD + COUNT, 3, 8, LANES)
YOUNG = (COUNT + PAD, 8, LANES)
FREE = (COUNT, 8, LANES)
MODES = (2 * PAD + COUNT, 12, 8, LANES)
STATE = (RES, RES, GAINS, SCALES, SPREAD, SPREAD, SPREAD)
HEAD_SCRATCH = (YOUNG, FREE, RES, MODES, MODES)
TAIL_SCRATCH = (YOUNG, FREE, RES, MODES, MODES, *STATE, RES, (OWN + 8, 2, 8, LANES))
HEAD_POINTS = {1: (0, 18, 32, 16), 2: (0, 20, 30, 15), 3: (0, 22, 28, 14)}
HEAD_SWEEPS = {1: (0, 18, 32, 8), 2: (0, 20, 30, 10), 3: (0, 22, 28, 14)}
TAIL_POINTS = {1: (28, 0, 22, 11), 2: (24, 0, 26, 13), 3: (16, 2, 32, 16)}
TAIL_SWEEPS = {1: (30, 0, 20, 10), 2: (26, 2, 22, 11), 3: (20, 6, 24, 12)}
POINTS_UP = {2: (0, 11, 39, 13), 1: (0, 14, 36, 12)}
SWEEPS_UP = {2: (0, 11, 39, 13), 1: (0, 14, 36, 12)}


class Passes:
    def __init__(self, meta_ref, young, free, first, mode, ahead, state):
        self.half, origin = meta_ref[3], meta_ref[4]
        self.young, self.free, self.mode, self.ahead = young, free, mode, ahead
        self.res = {1: first, 2: state[0], 3: state[1]}
        self.gain, self.scale = state[2], state[3]
        self.spread = {1: state[4], 2: state[5], 3: state[6]}
        shape = (8, LANES)
        self.lanes, self.rows = lanes_of(shape), rows_of(shape)
        self.place = 2 * self.lanes + origin
        self.node_in = (self.place >= 0) & (self.place < 8 * LANES)
        self.first_in = self.node_in & (self.lanes >= 1) & (self.lanes < WINDOW - 1)
        self.zero = jnp.zeros(shape, F32)

    def loop(self, body, planes):
        low, high, count, unroll = planes
        begin = low + (high - low) * self.half

        def step(n, carry):
            for u in range(unroll):
                body(begin + unroll * n + u)
            return carry

        lax.fori_loop(0, count // unroll, step, 0)

    def clear(self):
        for p in range(PAD):
            self.young[COUNT + p] = self.zero
            for level in range(3):
                self.scale[level, p] = self.zero
            for spread in self.spread.values():
                for f in range(3):
                    spread[p, f] = self.zero
                    spread[PAD + COUNT + p, f] = self.zero
            for k in range(12):
                self.mode[p, k] = self.zero
                self.mode[PAD + COUNT + p, k] = self.zero

    def unpack(self, tiles, p):
        total = roll(tiles[0], -WINDOW, 1)
        for f in range(1, 4):
            total = jnp.where(self.lanes >= PIECE * f, roll(tiles[f], PIECE * f - WINDOW, 1), total)
        self.young[p] = total
        self.free[p] = jnp.where(self.first_in, tiles[3], 0.0)

    def unpack_first(self, tiles, p):
        for f in range(3):
            self.res[1][p, f] = jnp.where(self.first_in, tiles[f], 0.0)

    def coefficients(self, planes):
        for level in range(1, LEVELS):
            step, spacing = 2 ** (level - 1), 2**level
            cells = (self.place >= 0) & (self.place <= 8 * LANES - 1 - spacing) & (self.rows < 8 - step)

            def fill_scale(p):
                total = self.young[p] + self.young[p + step]
                total = total + roll(total, -step, 0)
                total = total + roll(total, -step, 1)
                inside = cells & (p + (2 * OWN - COUNT) * self.half < 2 * OWN - step)
                self.scale[level - 1, p + PAD] = jnp.where(inside, (0.125 * spacing) * total, 0.0)

            def fill_gain(p):
                total = self.scale[level - 1, p + PAD] + self.scale[level - 1, p + PAD - step]
                total = total + roll(total, step, 0)
                total = total + roll(total, step, 1)
                self.gain[level - 1, p] = GAIN * self.free[p] / jnp.maximum(total, TINY)

            self.loop(fill_scale, planes)
            self.loop(fill_gain, planes)

    def put_modes(self, p, fields, step):
        modes = to_modes([[f] for f in fields], step, step)
        for k, key in enumerate(KEYS):
            self.mode[PAD + p, k] = modes[key][0]

    def smooth(self, level, planes):
        step = 2 ** (level - 1)

        def body(p):
            fields = []
            for f in range(3):
                if level == 1:
                    now = self.res[1][p, f]
                else:
                    above, reach = self.spread[level - 1], step // 2
                    sides = above[PAD + p - reach, f] + above[PAD + p + reach, f]
                    now = jnp.where(self.node_in, above[PAD + p, f] + 0.5 * sides, 0.0)
                    self.res[level][p, f] = now
                fields.append(self.gain[level - 1, p] * now)
            self.put_modes(p, fields, step)

        self.loop(body, planes)

    def cell(self, level, p):
        step = 2 ** (level - 1)
        low = {key: self.mode[PAD + p, k] for k, key in enumerate(KEYS)}
        high = {key: self.mode[PAD + p + step, k] for k, key in enumerate(KEYS)}
        to_low, to_high = cell(low, high, self.scale[level - 1, p + PAD])
        return to_low, to_high

    def sweep(self, level, planes, finish, before=False):
        step = 2 ** (level - 1)
        begin = planes[0] + (planes[1] - planes[0]) * self.half
        for p in range(step):
            if before:
                to_high = self.cell(level, begin - step + p)[1]
            for k, key in enumerate(KEYS):
                self.ahead[begin + p, k] = to_high[key] if before else self.zero

        def body(p):
            to_low, to_high = self.cell(level, p)
            modes = {key: [to_low[key] + self.ahead[p, k]] for k, key in enumerate(KEYS)}
            for k, key in enumerate(KEYS):
                self.ahead[p + step, k] = to_high[key]
            finish(p, [a[0] for a in from_modes(modes, step, step)])

        self.loop(body, planes)

    def down(self, points, sweeps, before):
        for level in range(1, LEVELS):
            step = 2 ** (level - 1)
            spread = self.spread[level]

            def restrict(p, applied):
                for f in range(3):
                    rest = self.res[level][p, f] - applied[f]
                    spread[PAD + p, f] = spread_plane([rest], step, step)[0]

            def correct(p, applied):
                for f in range(3):
                    now = self.res[level][p, f]
                    spread[PAD + p, f] = self.gain[level - 1, p] * (now + (now - applied[f]))

            self.smooth(level, points[level])
            self.sweep(level, sweeps[level], restrict if level < LEVELS - 1 else correct, before)


def head_kernel(meta_ref, own_ref, *refs):
    state, (young, free, first, mode, ahead) = refs[: len(STATE)], refs[len(STATE) :]
    run = Passes(meta_ref, young, free, first, mode, ahead, state)
    run.clear()
    for p in range(OWN, COUNT - HALO + PAD):
        young[p] = run.zero
        free[p] = run.zero
        for k in range(12):
            mode[PAD + p, k] = run.zero
    for p in range(OWN):
        tiles = [own_ref[p, f] for f in range(4)]
        run.unpack(tiles, p + HALO * run.half)
        run.unpack_first(tiles, p + HALO * run.half)
    run.coefficients((0, HALO, OWN, 16))
    run.down(HEAD_POINTS, HEAD_SWEEPS, False)


def tail_kernel(meta_ref, own_ref, side_ref, *refs):
    given, out_ref, refs = refs[: len(STATE)], refs[len(STATE)], refs[len(STATE) + 1 :]
    young, free, first, mode, ahead = refs[:5]
    state, (value, last) = refs[5 : 5 + len(STATE)], refs[5 + len(STATE) :]
    run = Passes(meta_ref, young, free, first, mode, ahead, state)
    run.clear()

    def take(n, carry):
        for u in range(8):
            p = 8 * n + u
            q = p + HALO * run.half
            run.unpack_first([own_ref[p, f] for f in range(3)], q)
            for level in range(3):
                state[2][level, q] = given[2][level, q]
                state[3][level, q + PAD] = given[3][level, q + PAD]
            for f in range(3):
                for n_res in range(2):
                    state[n_res][q, f] = given[n_res][q, f]
                for n_spread in range(4, 7):
                    state[n_spread][PAD + q, f] = given[n_spread][PAD + q, f]
        return carry

    lax.fori_loop(0, OWN // 8, take, 0)
    for n in range(8):
        p = n + (OWN - 8) * (1 - run.half)
        run.unpack([own_ref[p, f] for f in range(4)], p + HALO * run.half)
    for p in range(HALO):
        tiles = [side_ref[p, f] for f in range(4)]
        run.unpack(tiles, p + OWN * (1 - run.half))
        run.unpack_first(tiles, p + OWN * (1 - run.half))
    run.coefficients((28, 0, 22, 22))
    run.down(TAIL_POINTS, TAIL_SWEEPS, True)

    last[3, 0] = last[3, 1] = run.zero
    last[OWN + 4, 0] = last[OWN + 4, 1] = run.zero
    for level in range(LEVELS - 2, 0, -1):
        step = 2 ** (level - 1)
        coarse = run.spread[level + 1]

        def prolong(p):
            fields = []
            for f in range(3):
                sides = coarse[PAD + p - step, f] + coarse[PAD + p + step, f]
                along = coarse[PAD + p, f] + 0.5 * sides
                along = spread_plane([along], step, step)[0]
                smoothed = run.gain[level - 1, p] * run.res[level][p, f]
                fields.append(jnp.where(run.node_in, smoothed + 0.125 * along, 0.0))
                value[p, f] = fields[f]
            run.put_modes(p, fields, step)

        def correct(p, applied):
            fields = []
            for f in range(3):
                rest = run.res[level][p, f] - applied[f]
                fields.append(value[p, f] + run.gain[level - 1, p] * rest)
            if level > 1:
                for f in range(3):
                    run.spread[level][PAD + p, f] = fields[f]
                return
            place = p + 4 - HALO * run.half
            for t in range(2):
                third = roll(fields[2], BACK - 17 - (BACK // 2) * t, 1)
                last[place, t] = jnp.where(run.lanes < BACK, roll(fields[t], -17, 1), third)

        run.loop(prolong, POINTS_UP[level])
        run.sweep(level, SWEEPS_UP[level], correct)
    for d in range(8):
        for p in range(6):
            for t in range(2):
                out_ref[d, p, t] = last[4 * d + p + 3, t]


LAST_SCRATCH = (
    (SLAB + 4, 3, 2, 8, WIDE),
    (SLAB + 2, 12, 2, 8, WIDE),
    (12, 2, 8, WIDE),
    (12, 2, 8, WIDE),
    (SLAB + 2, 3, 2, 8, LANES),
    (SLAB + 4, 3, 2, 8, WIDE),
)


def last_kernel(own_ref, value_ref, scale_ref, gain_ref, in_ref, out_ref, coarse, mode, ahead, node, field, gather):
    lanes = lanes_of((8, LANES))
    for n in range(SLAB + 4):
        slot, parity = n // 2, n % 2
        for e in range(2):
            tiles = [[in_ref[e * 4 + parity * 2 + w, slot, t] for t in range(2)] for w in range(2)]
            for w in range(2):
                part = slice(w * LANES, (w + 1) * LANES)
                first, second = tiles[w]
                third = jnp.where(
                    lanes < BACK // 2, roll(first, -BACK, 1), roll(second, BACK // 2 - BACK, 1)
                )
                gather[n, 0, e, :, part] = first
                gather[n, 1, e, :, part] = second
                gather[n, 2, e, :, part] = third
    source = rows_of((WIDE, WIDE))
    target = lanes_of((WIDE, WIDE))
    y = 2 * (source % LANES) - 2 + source // LANES
    choose = ((source % LANES) < BACK) & (target == (y + WIDE) % WIDE)
    full = jnp.dot(
        gather[...].reshape((SLAB + 4) * 48, WIDE),
        choose.astype(F32),
        preferred_element_type=F32,
        precision=lax.Precision.HIGHEST,
    )
    full = full.reshape(SLAB + 4, 3, 2, 8, WIDE)
    for n in range(SLAB + 4):
        for i in range(3):
            planes = spread_plane([full[n, i, e] for e in range(2)], 1, 1)
            for e in range(2):
                coarse[n, i, e] = planes[e]

    def prolong(n, carry):
        fields = []
        for i in range(3):
            planes = []
            for e in range(2):
                along = coarse[n + 1, i, e] + 0.5 * (coarse[n, i, e] + coarse[n + 2, i, e])
                planes.append(value_ref[n, i, e] + 0.125 * along)
                field[n, i, e] = planes[e][:, :LANES]
            fields.append(planes)
        modes = to_modes(fields, 1, 1)
        for k, key in enumerate(KEYS):
            for e in range(2):
                mode[n, k, e] = modes[key][e]
        return carry

    fori(SLAB + 2, prolong, LAST_UNROLL)

    for k in range(12):
        for e in range(2):
            ahead[k, e] = jnp.zeros((8, WIDE), F32)

    for n in range(SLAB + 1):
        x = n - 1
        for e in range(2):
            for t in range(2):
                part = slice(t * LANES, (t + 1) * LANES)
                low = {key: mode[n, k, e, :, part] for k, key in enumerate(KEYS)}
                high = {key: mode[n + 1, k, e, :, part] for k, key in enumerate(KEYS)}
                to_low, to_high = cell(low, high, scale_ref[n, e, :, part])
                for k, key in enumerate(KEYS):
                    if x >= 0:
                        node[k, e, :, part] = to_low[key] + ahead[k, e, :, part]
                    ahead[k, e, :, part] = to_high[key]
        if x < 0:
            continue
        modes = {key: [node[k, e] for e in range(2)] for k, key in enumerate(KEYS)}
        applied = from_modes(modes, 1, 1)
        for i in range(3):
            for e in range(2):
                rest = own_ref[x, i, e] - applied[i][e][:, :LANES]
                total = field[n, i, e] + gain_ref[x, e] * rest
                out_ref[i, pl.ds(e * 8 + x, 8, stride=16), :] = own_ref[x, 4, e] * total


def shapes(*sizes):
    return [jax.ShapeDtypeStruct(size, F32) for size in sizes]


def scratch(*sizes):
    return [pltpu.VMEM(size, F32) for size in sizes]


def call(kernel, name, out, scratches, scalars, arrays, space=pltpu.VMEM, limit=VMEM_BYTES):
    specs = [pl.BlockSpec(memory_space=pltpu.SMEM)] * len(scalars)
    specs += [pl.BlockSpec(memory_space=space)] * len(arrays)
    return pl.pallas_call(
        kernel,
        out_shape=out,
        in_specs=specs,
        out_specs=[pl.BlockSpec(memory_space=pltpu.VMEM)] * len(out),
        scratch_shapes=scratches,
        compiler_params=pltpu.CompilerParams(vmem_limit_bytes=limit),
        name=name,
    )(*scalars, *arrays)


def on_device(right_side, density, fixed_mask):
    slab, line = lax.axis_index("gx"), lax.axis_index("gy")
    slabs, lines = lax.axis_size("gx"), lax.axis_size("gy")
    core = slab % 2
    half = slab // 8
    origin = LANES * line - REACH + core
    meta = jnp.stack([slab, line, core, half, origin]).astype(jnp.int32)
    groups = [list(range(8)), list(range(8, 16))]
    rows = 16 * SLAB

    own, first, last = call(
        edges_kernel,
        "edges",
        shapes((SLAB, 5, 2, 8, LANES), (SLAB, 2, 2, 8, LANES), (SLAB, 2, 2, 8, LANES)),
        [
            pltpu.VMEM((3, rows, LANES), F32),
            pltpu.VMEM((rows, LANES), jnp.int32),
            pltpu.VMEM((rows, LANES), jnp.int32),
            pltpu.SemaphoreType.DMA((3,)),
        ],
        [],
        [right_side.reshape(3, rows, LANES), density.reshape(rows, LANES), fixed_mask.reshape(rows, LANES)],
        pltpu.HBM,
        EDGES_BYTES,
    )
    after = lax.ppermute(first, "gy", [((j + 1) % lines, j) for j in range(lines)])
    before = lax.ppermute(last, "gy", [(j, (j + 1) % lines) for j in range(lines)])

    def columns(begin):
        parts = [lax.dynamic_slice_in_dim(a, begin, 3, axis=0) for a in (own, after, before)]
        return jnp.concatenate(parts, axis=1)

    pair = lax.ppermute(columns(5 * (1 - core)), "gx", [(i, i ^ 1) for i in range(slabs)])
    swaps = [(i, (i + 1) % slabs) for i in range(1, slabs, 2)]
    far = lax.ppermute(columns(5 * core), "gx", swaps + [(b, a) for a, b in swaps])

    fine_state = call(
        fine_head_kernel,
        "fine_head",
        shapes(*FINE_STATE),
        scratch((2, SLAB, 2, 8, WIDE)),
        [meta],
        [own, after, before],
    )
    packed, value, scale, gain = call(
        fine_kernel,
        "fine",
        shapes(
            (8, 4, 4, 8, LANES),
            (SLAB + 2, 3, 2, 8, WIDE),
            (SLAB + 1, 2, 8, WIDE),
            (SLAB, 2, 8, LANES),
        ),
        scratch(*FINE_SCRATCH),
        [meta],
        [*fine_state, pair, far],
    )
    packed = lax.all_to_all(packed, "gx", 0, 0, axis_index_groups=groups)
    packed = packed.reshape(OWN, 4, 8, LANES)
    side = lax.dynamic_slice_in_dim(packed, (OWN - HALO) * (1 - half), HALO, axis=0)
    side = lax.ppermute(side, "gx", [(i, i ^ 8) for i in range(slabs)])
    state = call(head_kernel, "head", shapes(*STATE), scratch(*HEAD_SCRATCH), [meta], [packed])
    (result,) = call(
        tail_kernel,
        "tail",
        shapes((8, 6, 2, 8, LANES)),
        scratch(*TAIL_SCRATCH),
        [meta],
        [packed, side, *state],
    )
    result = lax.all_to_all(result, "gx", 0, 0, axis_index_groups=groups)
    (correction,) = call(
        last_kernel,
        "last",
        shapes((3, rows, LANES)),
        scratch(*LAST_SCRATCH),
        [],
        [own, value, scale, gain, result],
    )
    return correction.reshape(right_side.shape)


def solution(mesh):
    in_specs = (P(None, None, "gx", "gy"), P(None, "gx", "gy"), P(None, "gx", "gy"))
    out_specs = P(None, None, "gx", "gy")
    return jax.shard_map(
        on_device, mesh=mesh, in_specs=in_specs, out_specs=out_specs, check_vma=False
    )
```

```python
import jax
import jax.numpy as jnp
from jax import lax
from jax.experimental import pallas as pl
from jax.experimental.pallas import tpu as pltpu
from jax.sharding import PartitionSpec as P

LEVELS = 4
Q = 16
JACOBI_WEIGHT = 0.6
SOFT_FLOOR = 0.1
LAME_FIRST = 0.3 / (1.3 * 0.4)
SHEAR_MOD = 0.5 / 1.3
RATIO = LAME_FIRST / SHEAR_MOD
UNIT = SHEAR_MOD / 16.0
GAIN = JACOBI_WEIGHT / ((RATIO + 4.0) * 16.0 / 9.0)
TINY = 1e-30

SLAB = 8
LANES = 128
LAST_UNROLL = 10
EDGE = 40
REACH = 36
WINDOW = 100
PIECE = WINDOW // 4
BACK = 66
KEYS = [(i, az, ay) for i in range(3) for az in range(2) for ay in range(2)]
VMEM_BYTES = 32 * 1024 * 1024
EDGES_BYTES = 62 * 1024 * 1024
F32 = jnp.float32


def roll(value, shift, axis):
    shift %= value.shape[axis]
    return value if shift == 0 else pltpu.roll(value, shift, axis)


def z_up(planes, step):
    if len(planes) == 1:
        return [roll(planes[0], -step, 0)]
    return [planes[1], roll(planes[0], -1, 0)]


def z_down(planes, step):
    if len(planes) == 1:
        return [roll(planes[0], step, 0)]
    return [roll(planes[1], 1, 0), planes[0]]


def fori(count, body, unroll):
    if unroll == count:
        for n in range(count):
            body(n, 0)
    else:
        lax.fori_loop(0, count, body, 0)


def rows_of(shape):
    return lax.broadcasted_iota(jnp.int32, shape, 0)


def lanes_of(shape):
    return lax.broadcasted_iota(jnp.int32, shape, 1)


def to_modes(fields, step, spacing):
    modes = {}
    for i, planes in enumerate(fields):
        ahead = [roll(p, -spacing, 1) for p in planes]
        for ay, along in ((0, [b + a for a, b in zip(planes, ahead)]), (1, [b - a for a, b in zip(planes, ahead)])):
            above = z_up(along, step)
            modes[i, 0, ay] = [b + a for a, b in zip(along, above)]
            modes[i, 1, ay] = [b - a for a, b in zip(along, above)]
    return modes


def from_modes(modes, step, spacing):
    fields = []
    for i in range(3):
        along = []
        for ay in range(2):
            low = [s - d for s, d in zip(modes[i, 0, ay], modes[i, 1, ay])]
            high = z_down([s + d for s, d in zip(modes[i, 0, ay], modes[i, 1, ay])], step)
            along.append([a + b for a, b in zip(low, high)])
        fields.append([(s - d) + roll(s + d, spacing, 1) for s, d in zip(along[0], along[1])])
    return fields


def cell(low, high, scale):
    full = {}
    for i, az, ay in KEYS:
        if az or ay:
            full[i, az, 0, ay] = high[i, az, ay] + low[i, az, ay]
        full[i, az, 1, ay] = high[i, az, ay] - low[i, az, ay]

    def mode(i, *dims):
        return full[i, int(0 in dims), int(1 in dims), int(2 in dims)]

    out = {}

    def put(value, i, *dims):
        out[i, int(0 in dims), int(1 in dims), int(2 in dims)] = value

    twice = 2.0 * scale
    half = 0.5 * scale * (RATIO / 1.5)
    third = scale * (1.0 / 3.0)
    trace = (RATIO * scale) * (mode(0, 0) + mode(1, 1) + mode(2, 2))
    for i in range(3):
        put(trace + twice * mode(i, i), i, i)
    for i, j in ((0, 1), (0, 2), (1, 2)):
        shear = scale * (mode(i, j) + mode(j, i))
        put(shear, i, j)
        put(shear, j, i)
    for q in range(3):
        p, r = [d for d in range(3) if d != q]
        first, second = mode(p, p, q), mode(r, r, q)
        both = half * (first + second)
        put(both + scale * first, p, p, q)
        put(both + scale * second, r, r, q)
    others = [[d for d in range(3) if d != i] for i in range(3)]
    total = mode(0, *others[0]) + mode(1, *others[1]) + mode(2, *others[2])
    for i in range(3):
        put(third * (total + mode(i, *others[i])), i, *others[i])
    ninth = scale * ((RATIO + 4.0) / 9.0)
    for i in range(3):
        put(ninth * mode(i, 0, 1, 2), i, 0, 1, 2)

    to_low, to_high = {}, {}
    for i, az, ay in KEYS:
        difference = out[i, az, 1, ay]
        if az or ay:
            to_low[i, az, ay] = out[i, az, 0, ay] - difference
            to_high[i, az, ay] = out[i, az, 0, ay] + difference
        else:
            to_low[i, az, ay] = -difference
            to_high[i, az, ay] = difference
    return to_low, to_high


def spread_plane(planes, step, spacing):
    rows = rows_of(planes[0].shape)
    above, below = z_up(planes, step), z_down(planes, step)
    if len(planes) == 1:
        above = [jnp.where(rows < 8 - step, above[0], 0.0)]
        below = [jnp.where(rows >= step, below[0], 0.0)]
    else:
        above = [above[0], jnp.where(rows < 7, above[1], 0.0)]
        below = [jnp.where(rows >= 1, below[0], 0.0), below[1]]
    along = [p + 0.5 * (a + b) for p, a, b in zip(planes, above, below)]
    if not spacing:
        return along
    return [p + 0.5 * (roll(p, spacing, 1) + roll(p, -spacing, 1)) for p in along]


def edges_kernel(right_hbm, density_hbm, mask_hbm, own_ref, first_ref, last_ref, right_ref, density_ref, mask_ref, sems):
    copies = [
        pltpu.make_async_copy(source, target, sems.at[n])
        for n, (source, target) in enumerate(
            ((right_hbm, right_ref), (density_hbm, density_ref), (mask_hbm, mask_ref))
        )
    ]
    for copy in copies:
        copy.start()
    for copy in copies:
        copy.wait()
    lanes = lanes_of((8, LANES))
    for x in range(SLAB):
        for e in range(2):
            rows = pl.ds(e * 8 + x, 8, stride=16)
            free = 1.0 - mask_ref[rows, :].astype(F32)
            level = density_ref[rows, :].astype(F32) / (Q - 1)
            young = SOFT_FLOOR + (1.0 - SOFT_FLOOR) * (level * level * level)
            fields = [free * right_ref[i, rows, :] for i in range(3)] + [UNIT * young, free]
            for f, value in enumerate(fields):
                own_ref[x, f, e] = value
            for group in range(2):
                members = fields[3 * group : 3 * group + 3]
                first = last = None
                for n, value in enumerate(members):
                    begin = roll(value, EDGE * n, 1)
                    end = roll(value, EDGE * n - (LANES - EDGE), 1)
                    first = begin if n == 0 else jnp.where(lanes < EDGE * n, first, begin)
                    last = end if n == 0 else jnp.where(lanes < EDGE * n, last, end)
                first_ref[x, group, e] = first
                last_ref[x, group, e] = last


WIDE = 2 * LANES

FINE_SCRATCH = (
    (5, 3, 2, 8, WIDE),
    (5, 2, 8, WIDE),
    (5, 12, 2, 8, WIDE),
    (12, 2, 8, WIDE),
    (12, 2, 8, WIDE),
    (SLAB + 2, 3, 2, 8, WIDE),
)


class Fine:
    def __init__(self, meta_ref):
        slab, line, core = meta_ref[0], meta_ref[1], meta_ref[2]
        self.core = core
        self.lanes = lanes_of((8, LANES))
        wide = lanes_of((8, WIDE))
        self.rows = rows_of((8, WIDE))
        local = jnp.where(wide < 192, wide, wide - WIDE)
        place = local + LANES * line
        self.node_in = (
            (place >= 0) & (place < 8 * LANES) & (local >= -EDGE) & (local < LANES + EDGE)
        )
        self.cell_in = (place >= 0) & (place < 8 * LANES - 1)
        self.first_slab, self.last_slab = slab == 0, slab == 15

    def inside(self, mask, x, top):
        if x < 0:
            return mask & jnp.logical_not(self.first_slab)
        if x >= top:
            return mask & jnp.logical_not(self.last_slab)
        return mask

    def widen(self, n, mid, hi, lo):
        hi = roll(hi, -EDGE * n, 1)
        lo = roll(lo, (LANES - EDGE) - EDGE * n, 1)
        return jnp.concatenate([mid, jnp.where(self.lanes < 64, hi, lo)], axis=1)

    def cells(self, x, e, young):
        mask = self.inside(self.cell_in, x, SLAB - 1)
        if e == 1:
            mask = mask & (self.rows < 7)
        return jnp.where(mask, young, 0.0)

    def smooth(self, x, scales, fields):
        total = [a + b for a, b in zip(*scales)]
        total = [a + b for a, b in zip(total, z_down(total, 1))]
        total = [a + roll(a, 1, 1) for a in total]
        nodes = self.inside(self.node_in, x, SLAB)
        free = [jnp.where(nodes, f, 0.0) for f in fields[4]]
        gains = [GAIN * f / jnp.maximum(t, TINY) for f, t in zip(free, total)]
        res = [[jnp.where(nodes, r, 0.0) for r in fields[i]] for i in range(3)]
        values = [[g * r for g, r in zip(gains, planes)] for planes in res]
        return gains, res, values


def near(offset):
    apart = (offset + WIDE) % WIDE
    return jnp.where(apart == 0, 1.0, 0.0) + jnp.where((apart == 1) | (apart == WIDE - 1), 0.5, 0.0)


def choose_class(spread):
    source = rows_of((WIDE, WIDE))
    target = lanes_of((WIDE, WIDE))
    y = 2 * (target % LANES) - REACH + target // LANES
    offset = source - (y + WIDE) % WIDE
    weights = near(offset) if spread else jnp.where(offset == 0, 1.0, 0.0)
    return jnp.where((target % LANES) < WINDOW, weights, 0.0).astype(jnp.bfloat16)


def choose_place():
    source = rows_of((WIDE, WIDE))
    target = lanes_of((WIDE, WIDE))
    y = 2 * (source % LANES) - 2 + source // LANES
    weights = near(target - (y + WIDE) % WIDE)
    return jnp.where((source % LANES) < BACK, weights, 0.0).astype(jnp.bfloat16)


def select(rows_in, choose):
    total = 0.0
    for _ in range(3):
        term = rows_in.astype(jnp.bfloat16)
        rows_in = rows_in - term.astype(F32)
        total = total + jnp.dot(term, choose, preferred_element_type=F32)
    return total


def put_smoothed(x, found, res_ref, mode_ref, gain_ref, value_ref, n_res, n_mode, n_gain, n_value):
    gains, res, values = found
    modes = to_modes(values, 1, 1)
    for e in range(2):
        for i in range(3):
            res_ref[n_res, i, e] = res[i][e]
            if n_value is not None:
                value_ref[n_value, i, e] = values[i][e]
        for k, key in enumerate(KEYS):
            mode_ref[n_mode, k, e] = modes[key][e]
        if n_gain is not None:
            gain_ref[n_gain, e] = gains[e][:, :LANES]


def leave(at, x, node, res, left, n):
    applied = from_modes({key: [node[k, e] for e in range(2)] for k, key in enumerate(KEYS)}, 1, 1)
    keep = at.inside(at.node_in, x, SLAB)
    for i in range(3):
        planes = [jnp.where(keep, r - a, 0.0) for r, a in zip(res[i], applied[i])]
        planes = spread_plane(planes, 1, 0)
        for e in range(2):
            left[n, i, e] = planes[e]


FINE_STATE = (
    (SLAB, 2, 8, WIDE),
    (SLAB, 3, 2, 8, WIDE),
    (SLAB, 12, 2, 8, WIDE),
    (SLAB, 3, 2, 8, WIDE),
    (SLAB, 2, 8, LANES),
    (4, 2, 8, WIDE),
    (4, SLAB, 2, 2, 8, LANES),
    (SLAB, 3, 2, 8, WIDE),
    (2, 12, 2, 8, WIDE),
)


def fine_head_kernel(
    meta_ref, own_ref, after_ref, before_ref,
    scale, res, mode, value, gain, edge, pieces, left, border, choose, gather, node, ahead,
):
    at = Fine(meta_ref)

    def field(x, f, e):
        group, n = f // 3, f % 3
        return at.widen(n, own_ref[x, f, e], after_ref[x, group, e], before_ref[x, group, e])

    for x in range(SLAB):
        for e in range(2):
            young = field(x, 3, e)
            gather[1, x, e] = young
            scale[x, e] = at.cells(x, e, young)
            free = jnp.where(at.node_in, field(x, 4, e), 0.0)
            gather[0, x, e] = free
            if x == 0:
                for i in range(3):
                    edge[i, e] = field(0, i, e)
                edge[3, e] = free
        if x == 0:
            continue
        fields = [[field(x, i, e) for e in range(2)] for i in range(3)]
        fields += [None, [gather[0, x, e] for e in range(2)]]
        scales = [[scale[x - d, e] for e in range(2)] for d in range(2)]
        put_smoothed(x, at.smooth(x, scales, fields), res, mode, gain, value, x, x, x, x)
    parts = select(gather[...].reshape(2 * SLAB * 16, WIDE), choose_class(False))
    parts = parts.reshape(2, SLAB, 2, 8, WIDE)
    for x in range(SLAB):
        for e in range(2):
            for parity in range(2):
                part = slice(parity * LANES, (parity + 1) * LANES)
                for f in range(4):
                    tile = roll(parts[1, x, e, :, part], WINDOW - PIECE * f, 1)
                    if f == 3:
                        tile = jnp.where(at.lanes < WINDOW, parts[0, x, e, :, part], tile)
                    pieces[f, x, e, parity] = tile
    choose[...] = choose_class(True)

    for x in range(1, SLAB - 1):
        for e in range(2):
            for t in range(2):
                part = slice(t * LANES, (t + 1) * LANES)
                low = {key: mode[x, k, e, :, part] for k, key in enumerate(KEYS)}
                high = {key: mode[x + 1, k, e, :, part] for k, key in enumerate(KEYS)}
                to_low, to_high = cell(low, high, scale[x, e, :, part])
                for k, key in enumerate(KEYS):
                    if x == 1:
                        border[0, k, e, :, part] = to_low[key]
                    else:
                        node[k, e, :, part] = to_low[key] + ahead[k, e, :, part]
                    if x < SLAB - 2:
                        ahead[k, e, :, part] = to_high[key]
                    else:
                        border[1, k, e, :, part] = to_high[key]
        if x > 1:
            leave(at, x, node, [[res[x, i, e] for e in range(2)] for i in range(3)], left, x)


def fine_kernel(
    meta_ref, own_scale, own_res, own_mode, edge, pieces, left, border, choose, pair_ref, far_ref,
    out_ref, value_ref, scale_ref, gain_ref,
    res, scale, mode, ahead, node, gather,
):
    at = Fine(meta_ref)

    def field(x, f, e):
        group, n = f // 3, f % 3
        if x == -3:
            slots = (18, 19, 20)
        else:
            p = x + 2 if x < 0 else x - SLAB
            slots = (5 * p + f, 10 + 2 * p + group, 14 + 2 * p + group)
        is_pair = (at.core == 1) if x < 0 else (at.core == 0)
        parts = [jnp.where(is_pair, pair_ref[s, e], far_ref[s, e]) for s in slots]
        return at.widen(n, *parts)

    def scale_at(x, e):
        return own_scale[x, e] if 0 <= x < SLAB else scale[x + 3 if x < 0 else x - SLAB + 3, e]

    def mode_at(x, k, e, part):
        if 1 <= x < SLAB:
            return own_mode[x, k, e, :, part]
        return mode[x + 2 if x < 1 else x - SLAB + 3, k, e, :, part]

    def res_at(x, i, e):
        return own_res[x, i, e] if 1 <= x < SLAB else res[x + 2 if x < 1 else x - SLAB + 3, i, e]

    for x in (-3, -2, -1, 8, 9):
        for e in range(2):
            scale[x + 3 if x < 0 else x - SLAB + 3, e] = at.cells(x, e, field(x, 3, e))
    for x in (-2, -1, 0, 8, 9):
        n = x + 2 if x < 1 else x - SLAB + 3
        if x == 0:
            fields = [[edge[i, e] for e in range(2)] for i in range(3)]
            fields += [None, [edge[3, e] for e in range(2)]]
        else:
            fields = [[field(x, i, e) if i != 3 else None for e in range(2)] for i in range(5)]
        scales = [[scale_at(x - d, e) for e in range(2)] for d in range(2)]
        found = at.smooth(x, scales, fields)
        n_value = {-1: 0, 0: 1, SLAB: 2}.get(x)
        put_smoothed(x, found, res, mode, gain_ref, value_ref, n, n, 0 if x == 0 else None, n_value)
    for e in range(2):
        scale_ref[e] = scale_at(-1, e)

    for x in (-2, -1, 0, 1, SLAB - 1, SLAB):
        for e in range(2):
            for t in range(2):
                part = slice(t * LANES, (t + 1) * LANES)
                if x == 1:
                    for k, key in enumerate(KEYS):
                        node[k, e, :, part] = border[0, k, e, :, part] + ahead[k, e, :, part]
                    continue
                low = {key: mode_at(x, k, e, part) for k, key in enumerate(KEYS)}
                high = {key: mode_at(x + 1, k, e, part) for k, key in enumerate(KEYS)}
                to_low, to_high = cell(low, high, scale_at(x, e)[:, part])
                for k, key in enumerate(KEYS):
                    if x == SLAB - 1:
                        node[k, e, :, part] = to_low[key] + border[1, k, e, :, part]
                    elif x > -2:
                        node[k, e, :, part] = to_low[key] + ahead[k, e, :, part]
                    ahead[k, e, :, part] = to_high[key]
        if x > -2:
            now = [[res_at(x, i, e) for e in range(2)] for i in range(3)]
            leave(at, x, node, now, gather, x + 1)

    def left_at(x, i, e):
        return left[x, i, e] if 2 <= x < SLAB - 1 else gather[x + 1, i, e]

    rows_in = [
        left_at(x, i, e) + 0.5 * (left_at(x - 1, i, e) + left_at(x + 1, i, e))
        for x in range(SLAB)
        for i in range(3)
        for e in range(2)
    ]
    parts = select(jnp.concatenate(rows_in, axis=0), choose[...]).reshape(SLAB, 3, 2, 8, WIDE)
    for x in range(SLAB):
        for e in range(2):
            for parity in range(2):
                part = slice(parity * LANES, (parity + 1) * LANES)
                for f in range(4):
                    tile = pieces[f, x, e, parity]
                    if f < 3:
                        tile = jnp.where(at.lanes < WINDOW, parts[x, f, e, :, part], tile)
                    out_ref[e * 4 + (x % 2) * 2 + parity, x // 2, f] = tile


OWN = 32
HALO = 18
COUNT = OWN + HALO
PAD = 4
RES = (COUNT, 3, 8, LANES)
GAINS = (3, COUNT, 8, LANES)
SCALES = (3, PAD + COUNT, 8, LANES)
SPREAD = (2 * PAD + COUNT, 3, 8, LANES)
YOUNG = (COUNT + PAD, 8, LANES)
FREE = (COUNT, 8, LANES)
MODES = (2 * PAD + COUNT, 12, 8, LANES)
STATE = (RES, RES, GAINS, SCALES, SPREAD, SPREAD, SPREAD, YOUNG, FREE, RES)
HEAD_SCRATCH = (MODES, MODES)
TAIL_SCRATCH = (MODES, MODES, RES, (OWN + 8, 2, 8, LANES))
HEAD_POINTS = {1: (0, 18, 32, 16), 2: (0, 20, 30, 15), 3: (0, 22, 28, 14)}
HEAD_SWEEPS = {1: (0, 18, 32, 8), 2: (0, 20, 30, 10), 3: (0, 22, 28, 14)}
TAIL_POINTS = {1: (29, 1, 20, 20), 2: (24, 2, 24, 24), 3: (16, 6, 28, 28)}
TAIL_SWEEPS = {1: (30, 2, 18, 9), 2: (26, 4, 20, 10), 3: (20, 10, 20, 10)}
POINTS_UP = {2: (0, 12, 38, 19), 1: (0, 16, 34, 17)}
SWEEPS_UP = {2: (0, 12, 38, 19), 1: (0, 16, 34, 17)}


class Passes:
    def __init__(self, meta_ref, mode, ahead, state):
        self.half, origin = meta_ref[3], meta_ref[4]
        self.mode, self.ahead = mode, ahead
        self.young, self.free = state[7], state[8]
        self.res = {1: state[9], 2: state[0], 3: state[1]}
        self.gain, self.scale = state[2], state[3]
        self.spread = {1: state[4], 2: state[5], 3: state[6]}
        shape = (8, LANES)
        self.lanes, self.rows = lanes_of(shape), rows_of(shape)
        self.place = 2 * self.lanes + origin
        self.node_in = (self.place >= 0) & (self.place < 8 * LANES)
        self.first_in = self.node_in & (self.lanes >= 1) & (self.lanes < WINDOW - 1)
        self.zero = jnp.zeros(shape, F32)

    def loop(self, body, planes):
        low, high, count, unroll = planes
        begin = low + (high - low) * self.half

        def step(n, carry):
            for u in range(unroll):
                body(begin + unroll * n + u)
            return carry

        lax.fori_loop(0, count // unroll, step, 0)

    def clear(self):
        for p in range(PAD):
            for k in range(12):
                self.mode[p, k] = self.zero
                self.mode[PAD + COUNT + p, k] = self.zero

    def clear_state(self):
        for p in range(PAD):
            self.young[COUNT + p] = self.zero
            for level in range(3):
                self.scale[level, p] = self.zero
            for spread in self.spread.values():
                for f in range(3):
                    spread[p, f] = self.zero
                    spread[PAD + COUNT + p, f] = self.zero

    def unpack(self, tiles, p):
        total = roll(tiles[0], -WINDOW, 1)
        for f in range(1, 4):
            total = jnp.where(self.lanes >= PIECE * f, roll(tiles[f], PIECE * f - WINDOW, 1), total)
        self.young[p] = total
        self.free[p] = jnp.where(self.first_in, tiles[3], 0.0)
        for f in range(3):
            self.res[1][p, f] = jnp.where(self.first_in, tiles[f], 0.0)

    def coefficients(self, planes):
        levels = [(level, 2 ** (level - 1), 2**level) for level in range(1, LEVELS)]
        place, rows = self.place, self.rows
        cells = [
            (place >= 0) & (place <= 8 * LANES - 1 - spacing) & (rows < 8 - step)
            for _, step, spacing in levels
        ]

        def fill_scale(p):
            x = p + (2 * OWN - COUNT) * self.half
            for (level, step, spacing), mask in zip(levels, cells):
                total = self.young[p] + self.young[p + step]
                total = total + roll(total, -step, 0)
                total = total + roll(total, -step, 1)
                inside = mask & (x < 2 * OWN - step)
                self.scale[level - 1, p + PAD] = jnp.where(inside, (0.125 * spacing) * total, 0.0)

        def fill_gain(p):
            free = GAIN * self.free[p]
            for level, step, _ in levels:
                total = self.scale[level - 1, p + PAD] + self.scale[level - 1, p + PAD - step]
                total = total + roll(total, step, 0)
                total = total + roll(total, step, 1)
                self.gain[level - 1, p] = free / jnp.maximum(total, TINY)

        self.loop(fill_scale, planes)
        self.loop(fill_gain, planes)

    def put_modes(self, p, fields, step):
        modes = to_modes([[f] for f in fields], step, step)
        for k, key in enumerate(KEYS):
            self.mode[PAD + p, k] = modes[key][0]

    def smooth(self, level, planes):
        step = 2 ** (level - 1)

        def body(p):
            fields = []
            for f in range(3):
                if level == 1:
                    now = self.res[1][p, f]
                else:
                    above, reach = self.spread[level - 1], step // 2
                    sides = above[PAD + p - reach, f] + above[PAD + p + reach, f]
                    now = jnp.where(self.node_in, above[PAD + p, f] + 0.5 * sides, 0.0)
                    self.res[level][p, f] = now
                fields.append(self.gain[level - 1, p] * now)
            self.put_modes(p, fields, step)

        self.loop(body, planes)

    def cell(self, level, p):
        step = 2 ** (level - 1)
        low = {key: self.mode[PAD + p, k] for k, key in enumerate(KEYS)}
        high = {key: self.mode[PAD + p + step, k] for k, key in enumerate(KEYS)}
        to_low, to_high = cell(low, high, self.scale[level - 1, p + PAD])
        return to_low, to_high

    def sweep(self, level, planes, finish, before=False):
        step = 2 ** (level - 1)
        begin = planes[0] + (planes[1] - planes[0]) * self.half
        for p in range(step):
            if before:
                to_high = self.cell(level, begin - step + p)[1]
            for k, key in enumerate(KEYS):
                self.ahead[begin + p, k] = to_high[key] if before else self.zero

        def body(p):
            to_low, to_high = self.cell(level, p)
            modes = {key: [to_low[key] + self.ahead[p, k]] for k, key in enumerate(KEYS)}
            for k, key in enumerate(KEYS):
                self.ahead[p + step, k] = to_high[key]
            finish(p, [a[0] for a in from_modes(modes, step, step)])

        self.loop(body, planes)

    def down(self, points, sweeps, before):
        for level in range(1, LEVELS):
            step = 2 ** (level - 1)
            spread = self.spread[level]

            def restrict(p, applied):
                for f in range(3):
                    rest = self.res[level][p, f] - applied[f]
                    spread[PAD + p, f] = spread_plane([rest], step, step)[0]

            def correct(p, applied):
                for f in range(3):
                    now = self.res[level][p, f]
                    spread[PAD + p, f] = self.gain[level - 1, p] * (now + (now - applied[f]))

            self.smooth(level, points[level])
            self.sweep(level, sweeps[level], restrict if level < LEVELS - 1 else correct, before)


def head_kernel(meta_ref, own_ref, *refs):
    state, (place_ref, mode, ahead) = refs[: len(STATE)], refs[len(STATE) :]
    place_ref[...] = choose_place()
    run = Passes(meta_ref, mode, ahead, state)
    run.clear()
    run.clear_state()
    for p in range(OWN, OWN + PAD):
        run.young[p] = run.zero
        for k in range(12):
            mode[PAD + p, k] = run.zero
    for p in range(OWN):
        run.unpack([own_ref[p, f] for f in range(4)], p + HALO * run.half)
    run.coefficients((0, HALO, OWN, 8))
    run.down(HEAD_POINTS, HEAD_SWEEPS, False)


def tail_kernel(meta_ref, side_ref, *refs):
    refs = refs[len(STATE) :]
    out_ref, state, (mode, ahead, value, last) = refs[0], refs[1 : 1 + len(STATE)], refs[1 + len(STATE) :]
    run = Passes(meta_ref, mode, ahead, state)
    run.clear()
    for p in range(HALO):
        run.unpack([side_ref[p, f] for f in range(4)], p + OWN * (1 - run.half))
    run.coefficients((28, 0, 22, 22))
    run.down(TAIL_POINTS, TAIL_SWEEPS, True)

    last[3, 0] = last[3, 1] = run.zero
    last[OWN + 4, 0] = last[OWN + 4, 1] = run.zero
    for level in range(LEVELS - 2, 0, -1):
        step = 2 ** (level - 1)
        coarse = run.spread[level + 1]

        def prolong(p):
            fields = []
            for f in range(3):
                sides = coarse[PAD + p - step, f] + coarse[PAD + p + step, f]
                along = coarse[PAD + p, f] + 0.5 * sides
                along = spread_plane([along], step, step)[0]
                smoothed = run.gain[level - 1, p] * run.res[level][p, f]
                fields.append(jnp.where(run.node_in, smoothed + 0.125 * along, 0.0))
                value[p, f] = fields[f]
            run.put_modes(p, fields, step)

        def correct(p, applied):
            fields = []
            for f in range(3):
                rest = run.res[level][p, f] - applied[f]
                fields.append(value[p, f] + run.gain[level - 1, p] * rest)
            if level > 1:
                for f in range(3):
                    run.spread[level][PAD + p, f] = fields[f]
                return
            place = p + 4 - HALO * run.half
            for t in range(2):
                third = roll(fields[2], BACK - 17 - (BACK // 2) * t, 1)
                last[place, t] = jnp.where(run.lanes < BACK, roll(fields[t], -17, 1), third)

        run.loop(prolong, POINTS_UP[level])
        run.sweep(level, SWEEPS_UP[level], correct)
    for d in range(8):
        for p in range(6):
            for t in range(2):
                out_ref[d, p, t] = last[4 * d + p + 3, t]


LAST_SCRATCH = (
    (SLAB + 4, 3, 2, 8, WIDE),
    (SLAB + 2, 12, 2, 8, WIDE),
    (12, 2, 8, WIDE),
    (12, 2, 8, WIDE),
    (SLAB + 2, 3, 2, 8, LANES),
    (SLAB + 4, 3, 2, 8, WIDE),
)


def last_kernel(
    own_ref, own_value, own_scale, own_gain, edge_value, edge_scale, edge_gain, place_ref, in_ref, out_ref,
    coarse, mode, ahead, node, field, gather,
):
    lanes = lanes_of((8, LANES))
    for n in range(SLAB + 4):
        slot, parity = n // 2, n % 2
        for e in range(2):
            tiles = [[in_ref[e * 4 + parity * 2 + w, slot, t] for t in range(2)] for w in range(2)]
            for w in range(2):
                part = slice(w * LANES, (w + 1) * LANES)
                first, second = tiles[w]
                third = jnp.where(
                    lanes < BACK // 2, roll(first, -BACK, 1), roll(second, BACK // 2 - BACK, 1)
                )
                gather[n, 0, e, :, part] = first
                gather[n, 1, e, :, part] = second
                gather[n, 2, e, :, part] = third
    full = select(gather[...].reshape((SLAB + 4) * 48, WIDE), place_ref[...])
    full = full.reshape(SLAB + 4, 3, 2, 8, WIDE)
    for n in range(SLAB + 4):
        for i in range(3):
            planes = spread_plane([full[n, i, e] for e in range(2)], 1, 0)
            for e in range(2):
                coarse[n, i, e] = planes[e]

    def prolong(n, carry):
        fields = []
        for i in range(3):
            planes = []
            for e in range(2):
                along = coarse[n + 1, i, e] + 0.5 * (coarse[n, i, e] + coarse[n + 2, i, e])
                first = own_value[n - 1, i, e] if 2 <= n <= SLAB else edge_value[n % (SLAB - 1), i, e]
                planes.append(first + 0.125 * along)
                field[n, i, e] = planes[e][:, :LANES]
            fields.append(planes)
        modes = to_modes(fields, 1, 1)
        for k, key in enumerate(KEYS):
            for e in range(2):
                mode[n, k, e] = modes[key][e]
        return carry

    fori(SLAB + 2, prolong, LAST_UNROLL)

    for k in range(12):
        for e in range(2):
            ahead[k, e] = jnp.zeros((8, WIDE), F32)

    for n in range(SLAB + 1):
        x = n - 1
        for e in range(2):
            for t in range(2):
                part = slice(t * LANES, (t + 1) * LANES)
                low = {key: mode[n, k, e, :, part] for k, key in enumerate(KEYS)}
                high = {key: mode[n + 1, k, e, :, part] for k, key in enumerate(KEYS)}
                to_low, to_high = cell(low, high, (own_scale[x, e] if x >= 0 else edge_scale[e])[:, part])
                for k, key in enumerate(KEYS):
                    if x >= 0:
                        node[k, e, :, part] = to_low[key] + ahead[k, e, :, part]
                    ahead[k, e, :, part] = to_high[key]
        if x < 0:
            continue
        modes = {key: [node[k, e] for e in range(2)] for k, key in enumerate(KEYS)}
        applied = from_modes(modes, 1, 1)
        for i in range(3):
            for e in range(2):
                rest = own_ref[x, i, e] - applied[i][e][:, :LANES]
                total = field[n, i, e] + (own_gain[x, e] if x > 0 else edge_gain[0, e]) * rest
                out_ref[i, pl.ds(e * 8 + x, 8, stride=16), :] = own_ref[x, 4, e] * total


def shapes(*sizes):
    return [jax.ShapeDtypeStruct(size, F32) for size in sizes]


def scratch(*sizes):
    return [pltpu.VMEM(size, F32) for size in sizes]


def call(kernel, name, out, scratches, scalars, arrays, space=pltpu.VMEM, limit=VMEM_BYTES, aliases={}):
    specs = [pl.BlockSpec(memory_space=pltpu.SMEM)] * len(scalars)
    specs += [pl.BlockSpec(memory_space=space)] * len(arrays)
    return pl.pallas_call(
        kernel,
        out_shape=out,
        in_specs=specs,
        out_specs=[pl.BlockSpec(memory_space=pltpu.VMEM)] * len(out),
        scratch_shapes=scratches,
        input_output_aliases=aliases,
        compiler_params=pltpu.CompilerParams(vmem_limit_bytes=limit),
        name=name,
    )(*scalars, *arrays)


def on_device(right_side, density, fixed_mask):
    slab, line = lax.axis_index("gx"), lax.axis_index("gy")
    slabs, lines = lax.axis_size("gx"), lax.axis_size("gy")
    core = slab % 2
    half = slab // 8
    origin = LANES * line - REACH + core
    meta = jnp.stack([slab, line, core, half, origin]).astype(jnp.int32)
    groups = [list(range(8)), list(range(8, 16))]
    rows = 16 * SLAB

    own, first, last = call(
        edges_kernel,
        "edges",
        shapes((SLAB, 5, 2, 8, LANES), (SLAB, 2, 2, 8, LANES), (SLAB, 2, 2, 8, LANES)),
        [
            pltpu.VMEM((3, rows, LANES), F32),
            pltpu.VMEM((rows, LANES), jnp.int32),
            pltpu.VMEM((rows, LANES), jnp.int32),
            pltpu.SemaphoreType.DMA((3,)),
        ],
        [],
        [right_side.reshape(3, rows, LANES), density.reshape(rows, LANES), fixed_mask.reshape(rows, LANES)],
        pltpu.HBM,
        EDGES_BYTES,
    )
    after = lax.ppermute(first, "gy", [((j + 1) % lines, j) for j in range(lines)])
    before = lax.ppermute(last, "gy", [(j, (j + 1) % lines) for j in range(lines)])

    def columns(begin, scale_only):
        parts = [lax.dynamic_slice_in_dim(a, begin, 2, axis=0) for a in (own, after, before)]
        parts = [p.reshape(-1, 2, 8, LANES) for p in parts]
        for array, f in ((own, 3), (after, 1), (before, 1)):
            parts.append(lax.dynamic_slice_in_dim(array[:, f], scale_only, 1, axis=0))
        return jnp.concatenate(parts, axis=0)

    swaps = [(i, (i + 1) % slabs) for i in range(1, slabs, 2)]
    far = lax.ppermute(columns(6 * core, 5 * core), "gx", swaps + [(b, a) for a, b in swaps])
    pair = lax.ppermute(columns(6 * (1 - core), 5 * (1 - core)), "gx", [(i, i ^ 1) for i in range(slabs)])
    matrix = [jax.ShapeDtypeStruct((WIDE, WIDE), jnp.bfloat16)]
    own_scale, own_res, own_mode, own_value, own_gain, *rest = call(
        fine_head_kernel,
        "fine_head",
        shapes(*FINE_STATE) + matrix,
        scratch((2, SLAB, 2, 8, WIDE), (12, 2, 8, WIDE), (12, 2, 8, WIDE)),
        [meta],
        [own, after, before],
    )
    packed, *edges = call(
        fine_kernel,
        "fine",
        shapes((8, 4, 4, 8, LANES), (3, 3, 2, 8, WIDE), (2, 8, WIDE), (1, 2, 8, LANES)),
        scratch(*FINE_SCRATCH),
        [meta],
        [own_scale, own_res, own_mode, *rest, pair, far],
    )
    packed = lax.all_to_all(packed, "gx", 0, 0, axis_index_groups=groups)
    packed = packed.reshape(OWN, 4, 8, LANES)
    side = lax.dynamic_slice_in_dim(packed, (OWN - HALO) * (1 - half), HALO, axis=0)
    side = lax.ppermute(side, "gx", [(i, i ^ 8) for i in range(slabs)])
    *state, place = call(
        head_kernel, "head", shapes(*STATE) + matrix, scratch(*HEAD_SCRATCH), [meta], [packed]
    )
    result = call(
        tail_kernel,
        "tail",
        shapes((8, 6, 2, 8, LANES), *STATE),
        scratch(*TAIL_SCRATCH),
        [meta],
        [side, *state],
        aliases={2 + n: 1 + n for n in range(len(STATE))},
    )[0]
    result = lax.all_to_all(result, "gx", 0, 0, axis_index_groups=groups)
    (correction,) = call(
        last_kernel,
        "last",
        shapes((3, rows, LANES)),
        scratch(*LAST_SCRATCH),
        [],
        [own, own_value, own_scale, own_gain, *edges, place, result],
    )
    return correction.reshape(right_side.shape)


def solution(mesh):
    in_specs = (P(None, None, "gx", "gy"), P(None, "gx", "gy"), P(None, "gx", "gy"))
    out_specs = P(None, None, "gx", "gy")
    return jax.shard_map(
        on_device, mesh=mesh, in_specs=in_specs, out_specs=out_specs, check_vma=False
    )
```

```python
import jax
import jax.numpy as jnp
from jax import lax
from jax.experimental import pallas as pl
from jax.experimental.pallas import tpu as pltpu
from jax.sharding import PartitionSpec as P

LEVELS = 4
Q = 16
JACOBI_WEIGHT = 0.6
SOFT_FLOOR = 0.1
LAME_FIRST = 0.3 / (1.3 * 0.4)
SHEAR_MOD = 0.5 / 1.3
RATIO = LAME_FIRST / SHEAR_MOD
UNIT = SHEAR_MOD / 16.0
GAIN = JACOBI_WEIGHT / ((RATIO + 4.0) * 16.0 / 9.0)
TINY = 1e-30

SLAB = 8
LANES = 128
LAST_UNROLL = 10
EDGE = 40
REACH = 36
WINDOW = 100
PIECE = WINDOW // 4
BACK = 66
KEYS = [(i, az, ay) for i in range(3) for az in range(2) for ay in range(2)]
VMEM_BYTES = 32 * 1024 * 1024
EDGES_BYTES = 62 * 1024 * 1024
F32 = jnp.float32


def roll(value, shift, axis):
    shift %= value.shape[axis]
    return value if shift == 0 else pltpu.roll(value, shift, axis)


def z_up(planes, step):
    if len(planes) == 1:
        return [roll(planes[0], -step, 0)]
    return [planes[1], roll(planes[0], -1, 0)]


def z_down(planes, step):
    if len(planes) == 1:
        return [roll(planes[0], step, 0)]
    return [roll(planes[1], 1, 0), planes[0]]


def fori(count, body, unroll):
    if unroll == count:
        for n in range(count):
            body(n, 0)
    else:
        lax.fori_loop(0, count, body, 0)


def rows_of(shape):
    return lax.broadcasted_iota(jnp.int32, shape, 0)


def lanes_of(shape):
    return lax.broadcasted_iota(jnp.int32, shape, 1)


def to_modes(fields, step, spacing):
    modes = {}
    for i, planes in enumerate(fields):
        ahead = [roll(p, -spacing, 1) for p in planes]
        for ay, along in ((0, [b + a for a, b in zip(planes, ahead)]), (1, [b - a for a, b in zip(planes, ahead)])):
            above = z_up(along, step)
            modes[i, 0, ay] = [b + a for a, b in zip(along, above)]
            modes[i, 1, ay] = [b - a for a, b in zip(along, above)]
    return modes


def from_modes(modes, step, spacing):
    fields = []
    for i in range(3):
        along = []
        for ay in range(2):
            low = [s - d for s, d in zip(modes[i, 0, ay], modes[i, 1, ay])]
            high = z_down([s + d for s, d in zip(modes[i, 0, ay], modes[i, 1, ay])], step)
            along.append([a + b for a, b in zip(low, high)])
        fields.append([(s - d) + roll(s + d, spacing, 1) for s, d in zip(along[0], along[1])])
    return fields


def cell(low, high, scale):
    full = {}
    for i, az, ay in KEYS:
        if az or ay:
            full[i, az, 0, ay] = high[i, az, ay] + low[i, az, ay]
        full[i, az, 1, ay] = high[i, az, ay] - low[i, az, ay]

    def mode(i, *dims):
        return full[i, int(0 in dims), int(1 in dims), int(2 in dims)]

    out = {}

    def put(value, i, *dims):
        out[i, int(0 in dims), int(1 in dims), int(2 in dims)] = value

    twice = 2.0 * scale
    half = 0.5 * scale * (RATIO / 1.5)
    third = scale * (1.0 / 3.0)
    trace = (RATIO * scale) * (mode(0, 0) + mode(1, 1) + mode(2, 2))
    for i in range(3):
        put(trace + twice * mode(i, i), i, i)
    for i, j in ((0, 1), (0, 2), (1, 2)):
        shear = scale * (mode(i, j) + mode(j, i))
        put(shear, i, j)
        put(shear, j, i)
    for q in range(3):
        p, r = [d for d in range(3) if d != q]
        first, second = mode(p, p, q), mode(r, r, q)
        both = half * (first + second)
        put(both + scale * first, p, p, q)
        put(both + scale * second, r, r, q)
    others = [[d for d in range(3) if d != i] for i in range(3)]
    total = mode(0, *others[0]) + mode(1, *others[1]) + mode(2, *others[2])
    for i in range(3):
        put(third * (total + mode(i, *others[i])), i, *others[i])
    ninth = scale * ((RATIO + 4.0) / 9.0)
    for i in range(3):
        put(ninth * mode(i, 0, 1, 2), i, 0, 1, 2)

    to_low, to_high = {}, {}
    for i, az, ay in KEYS:
        difference = out[i, az, 1, ay]
        if az or ay:
            to_low[i, az, ay] = out[i, az, 0, ay] - difference
            to_high[i, az, ay] = out[i, az, 0, ay] + difference
        else:
            to_low[i, az, ay] = -difference
            to_high[i, az, ay] = difference
    return to_low, to_high


def spread_plane(planes, step, spacing):
    rows = rows_of(planes[0].shape)
    above, below = z_up(planes, step), z_down(planes, step)
    if len(planes) == 1:
        above = [jnp.where(rows < 8 - step, above[0], 0.0)]
        below = [jnp.where(rows >= step, below[0], 0.0)]
    else:
        above = [above[0], jnp.where(rows < 7, above[1], 0.0)]
        below = [jnp.where(rows >= 1, below[0], 0.0), below[1]]
    along = [p + 0.5 * (a + b) for p, a, b in zip(planes, above, below)]
    if not spacing:
        return along
    return [p + 0.5 * (roll(p, spacing, 1) + roll(p, -spacing, 1)) for p in along]


def edges_kernel(right_hbm, density_hbm, mask_hbm, own_ref, first_ref, last_ref, right_ref, density_ref, mask_ref, sems):
    copies = [
        pltpu.make_async_copy(source, target, sems.at[n])
        for n, (source, target) in enumerate(
            ((right_hbm, right_ref), (density_hbm, density_ref), (mask_hbm, mask_ref))
        )
    ]
    for copy in copies:
        copy.start()
    for copy in copies:
        copy.wait()
    lanes = lanes_of((8, LANES))
    for x in range(SLAB):
        for e in range(2):
            rows = pl.ds(e * 8 + x, 8, stride=16)
            free = 1.0 - mask_ref[rows, :].astype(F32)
            level = density_ref[rows, :].astype(F32) / (Q - 1)
            young = SOFT_FLOOR + (1.0 - SOFT_FLOOR) * (level * level * level)
            fields = [free * right_ref[i, rows, :] for i in range(3)] + [UNIT * young, free]
            for f, value in enumerate(fields):
                own_ref[x, f, e] = value
            for group in range(2):
                members = fields[3 * group : 3 * group + 3]
                first = last = None
                for n, value in enumerate(members):
                    begin = roll(value, EDGE * n, 1)
                    end = roll(value, EDGE * n - (LANES - EDGE), 1)
                    first = begin if n == 0 else jnp.where(lanes < EDGE * n, first, begin)
                    last = end if n == 0 else jnp.where(lanes < EDGE * n, last, end)
                first_ref[x, group, e] = first
                last_ref[x, group, e] = last


WIDE = 2 * LANES

FINE_SCRATCH = (
    (5, 3, 2, 8, WIDE),
    (5, 2, 8, WIDE),
    (5, 12, 2, 8, WIDE),
    (12, 2, 8, WIDE),
    (12, 2, 8, WIDE),
    (SLAB + 2, 3, 2, 8, WIDE),
)


class Fine:
    def __init__(self, meta_ref):
        slab, line, core = meta_ref[0], meta_ref[1], meta_ref[2]
        self.core = core
        self.lanes = lanes_of((8, LANES))
        wide = lanes_of((8, WIDE))
        self.rows = rows_of((8, WIDE))
        local = jnp.where(wide < 192, wide, wide - WIDE)
        place = local + LANES * line
        self.node_in = (
            (place >= 0) & (place < 8 * LANES) & (local >= -EDGE) & (local < LANES + EDGE)
        )
        self.cell_in = (place >= 0) & (place < 8 * LANES - 1)
        self.first_slab, self.last_slab = slab == 0, slab == 15

    def inside(self, mask, x, top):
        if x < 0:
            return mask & jnp.logical_not(self.first_slab)
        if x >= top:
            return mask & jnp.logical_not(self.last_slab)
        return mask

    def widen(self, n, mid, hi, lo):
        hi = roll(hi, -EDGE * n, 1)
        lo = roll(lo, (LANES - EDGE) - EDGE * n, 1)
        return jnp.concatenate([mid, jnp.where(self.lanes < 64, hi, lo)], axis=1)

    def cells(self, x, e, young):
        mask = self.inside(self.cell_in, x, SLAB - 1)
        if e == 1:
            mask = mask & (self.rows < 7)
        return jnp.where(mask, young, 0.0)

    def smooth(self, x, scales, fields):
        total = [a + b for a, b in zip(*scales)]
        total = [a + b for a, b in zip(total, z_down(total, 1))]
        total = [a + roll(a, 1, 1) for a in total]
        nodes = self.inside(self.node_in, x, SLAB)
        free = [jnp.where(nodes, f, 0.0) for f in fields[4]]
        gains = [GAIN * f / jnp.maximum(t, TINY) for f, t in zip(free, total)]
        res = [[jnp.where(nodes, r, 0.0) for r in fields[i]] for i in range(3)]
        values = [[g * r for g, r in zip(gains, planes)] for planes in res]
        return gains, res, values


def near(offset):
    apart = (offset + WIDE) % WIDE
    return jnp.where(apart == 0, 1.0, 0.0) + jnp.where((apart == 1) | (apart == WIDE - 1), 0.5, 0.0)


def choose_class(spread):
    source = rows_of((WIDE, WIDE))
    target = lanes_of((WIDE, WIDE))
    y = 2 * (target % LANES) - REACH + target // LANES
    offset = source - (y + WIDE) % WIDE
    weights = near(offset) if spread else jnp.where(offset == 0, 1.0, 0.0)
    return jnp.where((target % LANES) < WINDOW, weights, 0.0).astype(jnp.bfloat16)


def choose_place():
    source = rows_of((WIDE, WIDE))
    target = lanes_of((WIDE, WIDE))
    y = 2 * (source % LANES) - 2 + source // LANES
    weights = near(target - (y + WIDE) % WIDE)
    return jnp.where((source % LANES) < BACK, weights, 0.0).astype(jnp.bfloat16)


def select(rows_in, choose):
    total = 0.0
    for _ in range(3):
        term = rows_in.astype(jnp.bfloat16)
        rows_in = rows_in - term.astype(F32)
        total = total + jnp.dot(term, choose, preferred_element_type=F32)
    return total


def put_smoothed(x, found, res_ref, mode_ref, gain_ref, value_ref, n_res, n_mode, n_gain, n_value):
    gains, res, values = found
    modes = to_modes(values, 1, 1)
    for e in range(2):
        for i in range(3):
            res_ref[n_res, i, e] = res[i][e]
            if n_value is not None:
                value_ref[n_value, i, e] = values[i][e]
        for k, key in enumerate(KEYS):
            mode_ref[n_mode, k, e] = modes[key][e]
        if n_gain is not None:
            gain_ref[n_gain, e] = gains[e][:, :LANES]


def leave(at, x, node, res, left, n):
    applied = from_modes({key: [node[k, e] for e in range(2)] for k, key in enumerate(KEYS)}, 1, 1)
    keep = at.inside(at.node_in, x, SLAB)
    for i in range(3):
        planes = [jnp.where(keep, r - a, 0.0) for r, a in zip(res[i], applied[i])]
        planes = spread_plane(planes, 1, 0)
        for e in range(2):
            left[n, i, e] = planes[e]


FINE_STATE = (
    (SLAB, 2, 8, WIDE),
    (SLAB, 3, 2, 8, WIDE),
    (SLAB, 12, 2, 8, WIDE),
    (SLAB, 3, 2, 8, WIDE),
    (SLAB, 2, 8, LANES),
    (4, 2, 8, WIDE),
    (4, SLAB, 2, 2, 8, LANES),
    (SLAB, 3, 2, 8, WIDE),
    (2, 12, 2, 8, WIDE),
)


def fine_head_kernel(
    meta_ref, own_ref, after_ref, before_ref,
    scale, res, mode, value, gain, edge, pieces, left, border, choose, gather, node, ahead,
):
    at = Fine(meta_ref)

    def field(x, f, e):
        group, n = f // 3, f % 3
        return at.widen(n, own_ref[x, f, e], after_ref[x, group, e], before_ref[x, group, e])

    for x in range(SLAB):
        for e in range(2):
            young = field(x, 3, e)
            gather[1, x, e] = young
            scale[x, e] = at.cells(x, e, young)
            free = jnp.where(at.node_in, field(x, 4, e), 0.0)
            gather[0, x, e] = free
            if x == 0:
                for i in range(3):
                    edge[i, e] = field(0, i, e)
                edge[3, e] = free
        if x == 0:
            continue
        fields = [[field(x, i, e) for e in range(2)] for i in range(3)]
        fields += [None, [gather[0, x, e] for e in range(2)]]
        scales = [[scale[x - d, e] for e in range(2)] for d in range(2)]
        put_smoothed(x, at.smooth(x, scales, fields), res, mode, gain, value, x, x, x, x)
    parts = select(gather[...].reshape(2 * SLAB * 16, WIDE), choose_class(False))
    parts = parts.reshape(2, SLAB, 2, 8, WIDE)
    for x in range(SLAB):
        for e in range(2):
            for parity in range(2):
                part = slice(parity * LANES, (parity + 1) * LANES)
                for f in range(4):
                    tile = roll(parts[1, x, e, :, part], WINDOW - PIECE * f, 1)
                    if f == 3:
                        tile = jnp.where(at.lanes < WINDOW, parts[0, x, e, :, part], tile)
                    pieces[f, x, e, parity] = tile
    choose[...] = choose_class(True)

    for x in range(1, SLAB - 1):
        for e in range(2):
            for t in range(2):
                part = slice(t * LANES, (t + 1) * LANES)
                low = {key: mode[x, k, e, :, part] for k, key in enumerate(KEYS)}
                high = {key: mode[x + 1, k, e, :, part] for k, key in enumerate(KEYS)}
                to_low, to_high = cell(low, high, scale[x, e, :, part])
                for k, key in enumerate(KEYS):
                    if x == 1:
                        border[0, k, e, :, part] = to_low[key]
                    else:
                        node[k, e, :, part] = to_low[key] + ahead[k, e, :, part]
                    if x < SLAB - 2:
                        ahead[k, e, :, part] = to_high[key]
                    else:
                        border[1, k, e, :, part] = to_high[key]
        if x > 1:
            leave(at, x, node, [[res[x, i, e] for e in range(2)] for i in range(3)], left, x)


def fine_kernel(
    meta_ref, own_scale, own_res, own_mode, edge, pieces, left, border, choose, pair_ref, far_ref,
    out_ref, value_ref, scale_ref, gain_ref,
    res, scale, mode, ahead, node, gather,
):
    at = Fine(meta_ref)

    def field(x, f, e):
        group, n = f // 3, f % 3
        if x == -3:
            slots = (18, 19, 20)
        else:
            p = x + 2 if x < 0 else x - SLAB
            slots = (5 * p + f, 10 + 2 * p + group, 14 + 2 * p + group)
        is_pair = (at.core == 1) if x < 0 else (at.core == 0)
        parts = [jnp.where(is_pair, pair_ref[s, e], far_ref[s, e]) for s in slots]
        return at.widen(n, *parts)

    def scale_at(x, e):
        return own_scale[x, e] if 0 <= x < SLAB else scale[x + 3 if x < 0 else x - SLAB + 3, e]

    def mode_at(x, k, e, part):
        if 1 <= x < SLAB:
            return own_mode[x, k, e, :, part]
        return mode[x + 2 if x < 1 else x - SLAB + 3, k, e, :, part]

    def res_at(x, i, e):
        return own_res[x, i, e] if 1 <= x < SLAB else res[x + 2 if x < 1 else x - SLAB + 3, i, e]

    for x in (-3, -2, -1, 8, 9):
        for e in range(2):
            scale[x + 3 if x < 0 else x - SLAB + 3, e] = at.cells(x, e, field(x, 3, e))
    for x in (-2, -1, 0, 8, 9):
        n = x + 2 if x < 1 else x - SLAB + 3
        if x == 0:
            fields = [[edge[i, e] for e in range(2)] for i in range(3)]
            fields += [None, [edge[3, e] for e in range(2)]]
        else:
            fields = [[field(x, i, e) if i != 3 else None for e in range(2)] for i in range(5)]
        scales = [[scale_at(x - d, e) for e in range(2)] for d in range(2)]
        found = at.smooth(x, scales, fields)
        n_value = {-1: 0, 0: 1, SLAB: 2}.get(x)
        put_smoothed(x, found, res, mode, gain_ref, value_ref, n, n, 0 if x == 0 else None, n_value)
    for e in range(2):
        scale_ref[e] = scale_at(-1, e)

    for x in (-2, -1, 0, 1, SLAB - 1, SLAB):
        for e in range(2):
            for t in range(2):
                part = slice(t * LANES, (t + 1) * LANES)
                if x == 1:
                    for k, key in enumerate(KEYS):
                        node[k, e, :, part] = border[0, k, e, :, part] + ahead[k, e, :, part]
                    continue
                low = {key: mode_at(x, k, e, part) for k, key in enumerate(KEYS)}
                high = {key: mode_at(x + 1, k, e, part) for k, key in enumerate(KEYS)}
                to_low, to_high = cell(low, high, scale_at(x, e)[:, part])
                for k, key in enumerate(KEYS):
                    if x == SLAB - 1:
                        node[k, e, :, part] = to_low[key] + border[1, k, e, :, part]
                    elif x > -2:
                        node[k, e, :, part] = to_low[key] + ahead[k, e, :, part]
                    ahead[k, e, :, part] = to_high[key]
        if x > -2:
            now = [[res_at(x, i, e) for e in range(2)] for i in range(3)]
            leave(at, x, node, now, gather, x + 1)

    def left_at(x, i, e):
        return left[x, i, e] if 2 <= x < SLAB - 1 else gather[x + 1, i, e]

    rows_in = [
        left_at(x, i, e) + 0.5 * (left_at(x - 1, i, e) + left_at(x + 1, i, e))
        for x in range(SLAB)
        for i in range(3)
        for e in range(2)
    ]
    parts = select(jnp.concatenate(rows_in, axis=0), choose[...]).reshape(SLAB, 3, 2, 8, WIDE)
    for x in range(SLAB):
        for e in range(2):
            for parity in range(2):
                part = slice(parity * LANES, (parity + 1) * LANES)
                for f in range(4):
                    tile = pieces[f, x, e, parity]
                    if f < 3:
                        tile = jnp.where(at.lanes < WINDOW, parts[x, f, e, :, part], tile)
                    out_ref[e * 4 + (x % 2) * 2 + parity, x // 2, f] = tile


OWN = 32
HALO = 18
COUNT = OWN + HALO
PAD = 4
RES = (COUNT, 3, 8, LANES)
GAINS = (3, COUNT, 8, LANES)
SCALES = (3, PAD + COUNT, 8, LANES)
SPREAD = (2 * PAD + COUNT, 3, 8, LANES)
YOUNG = (COUNT + PAD, 8, LANES)
FREE = (COUNT, 8, LANES)
MODES = (2 * PAD + COUNT, 12, 8, LANES)
BACK_TILES = (OWN + 8, 2, 8, LANES)
STATE = (RES, RES, GAINS, SCALES, SPREAD, SPREAD, SPREAD, YOUNG, FREE, RES, SPREAD, BACK_TILES)
CLASS_SCRATCH = (MODES, MODES, RES)
HEAD_POINTS = {1: (0, 18, 32, 32), 2: (0, 20, 30, 30), 3: (0, 22, 28, 28)}
HEAD_SWEEPS = {1: (0, 18, 32, 16), 2: (0, 20, 30, 15), 3: (0, 22, 28, 14)}
TAIL_POINTS = {1: (29, 1, 20, 20), 2: (24, 2, 24, 24), 3: (16, 6, 28, 28)}
TAIL_SWEEPS = {1: (30, 2, 18, 9), 2: (26, 4, 20, 10), 3: (20, 10, 20, 10)}
HEAD_POINTS_UP = {2: (0, 30, 20, 20), 1: (0, 34, 16, 16)}
HEAD_SWEEPS_UP = {2: (0, 30, 20, 10), 1: (0, 34, 16, 16)}
TAIL_POINTS_UP = {2: (15, 13, 22, 11), 1: (14, 16, 20, 10)}
TAIL_SWEEPS_UP = {2: (17, 15, 18, 9), 1: (15, 17, 18, 9)}


class Passes:
    def __init__(self, meta_ref, mode, ahead, value, state):
        self.half, origin = meta_ref[3], meta_ref[4]
        self.mode, self.ahead, self.value = mode, ahead, value
        self.young, self.free = state[7], state[8]
        self.res = {1: state[9], 2: state[0], 3: state[1]}
        self.gain, self.scale = state[2], state[3]
        self.spread = {1: state[4], 2: state[5], 3: state[6]}
        self.corrected, self.last = {2: state[10], 3: state[6]}, state[11]
        shape = (8, LANES)
        self.lanes, self.rows = lanes_of(shape), rows_of(shape)
        self.place = 2 * self.lanes + origin
        self.node_in = (self.place >= 0) & (self.place < 8 * LANES)
        self.first_in = self.node_in & (self.lanes >= 1) & (self.lanes < WINDOW - 1)
        self.zero = jnp.zeros(shape, F32)

    def loop(self, body, planes):
        low, high, count, unroll = planes
        begin = low + (high - low) * self.half

        def step(n, carry):
            for u in range(unroll):
                body(begin + unroll * n + u)
            return carry

        lax.fori_loop(0, count // unroll, step, 0)

    def clear(self):
        for p in range(PAD):
            for k in range(12):
                self.mode[p, k] = self.zero
                self.mode[PAD + COUNT + p, k] = self.zero

    def clear_state(self):
        for p in range(PAD):
            self.young[COUNT + p] = self.zero
            for level in range(3):
                self.scale[level, p] = self.zero
            for spread in (*self.spread.values(), self.corrected[2]):
                for f in range(3):
                    spread[p, f] = self.zero
                    spread[PAD + COUNT + p, f] = self.zero
        for t in range(2):
            self.last[3, t] = self.zero
            self.last[OWN + 4, t] = self.zero

    def unpack(self, tiles, p):
        total = roll(tiles[0], -WINDOW, 1)
        for f in range(1, 4):
            total = jnp.where(self.lanes >= PIECE * f, roll(tiles[f], PIECE * f - WINDOW, 1), total)
        self.young[p] = total
        self.free[p] = jnp.where(self.first_in, tiles[3], 0.0)
        for f in range(3):
            self.res[1][p, f] = jnp.where(self.first_in, tiles[f], 0.0)

    def coefficients(self, planes):
        levels = [(level, 2 ** (level - 1), 2**level) for level in range(1, LEVELS)]
        place, rows = self.place, self.rows
        cells = [
            (place >= 0) & (place <= 8 * LANES - 1 - spacing) & (rows < 8 - step)
            for _, step, spacing in levels
        ]

        def fill_scale(p):
            x = p + (2 * OWN - COUNT) * self.half
            for (level, step, spacing), mask in zip(levels, cells):
                total = self.young[p] + self.young[p + step]
                total = total + roll(total, -step, 0)
                total = total + roll(total, -step, 1)
                inside = mask & (x < 2 * OWN - step)
                self.scale[level - 1, p + PAD] = jnp.where(inside, (0.125 * spacing) * total, 0.0)

        def fill_gain(p):
            free = GAIN * self.free[p]
            for level, step, _ in levels:
                total = self.scale[level - 1, p + PAD] + self.scale[level - 1, p + PAD - step]
                total = total + roll(total, step, 0)
                total = total + roll(total, step, 1)
                self.gain[level - 1, p] = free / jnp.maximum(total, TINY)

        self.loop(fill_scale, planes)
        self.loop(fill_gain, planes)

    def put_modes(self, p, fields, step):
        modes = to_modes([[f] for f in fields], step, step)
        for k, key in enumerate(KEYS):
            self.mode[PAD + p, k] = modes[key][0]

    def smooth(self, level, planes):
        step = 2 ** (level - 1)

        def body(p):
            fields = []
            for f in range(3):
                if level == 1:
                    now = self.res[1][p, f]
                else:
                    above, reach = self.spread[level - 1], step // 2
                    sides = above[PAD + p - reach, f] + above[PAD + p + reach, f]
                    now = jnp.where(self.node_in, above[PAD + p, f] + 0.5 * sides, 0.0)
                    self.res[level][p, f] = now
                fields.append(self.gain[level - 1, p] * now)
            self.put_modes(p, fields, step)

        self.loop(body, planes)

    def cell(self, level, p):
        step = 2 ** (level - 1)
        low = {key: self.mode[PAD + p, k] for k, key in enumerate(KEYS)}
        high = {key: self.mode[PAD + p + step, k] for k, key in enumerate(KEYS)}
        to_low, to_high = cell(low, high, self.scale[level - 1, p + PAD])
        return to_low, to_high

    def sweep(self, level, planes, finish, before=False):
        step = 2 ** (level - 1)
        begin = planes[0] + (planes[1] - planes[0]) * self.half
        for p in range(step):
            if before:
                to_high = self.cell(level, begin - step + p)[1]
            for k, key in enumerate(KEYS):
                self.ahead[begin + p, k] = to_high[key] if before else self.zero

        def body(p):
            to_low, to_high = self.cell(level, p)
            modes = {key: [to_low[key] + self.ahead[p, k]] for k, key in enumerate(KEYS)}
            for k, key in enumerate(KEYS):
                self.ahead[p + step, k] = to_high[key]
            finish(p, [a[0] for a in from_modes(modes, step, step)])

        self.loop(body, planes)

    def down(self, points, sweeps, before):
        for level in range(1, LEVELS):
            step = 2 ** (level - 1)
            spread = self.spread[level]

            def restrict(p, applied):
                for f in range(3):
                    rest = self.res[level][p, f] - applied[f]
                    spread[PAD + p, f] = spread_plane([rest], step, step)[0]

            def correct(p, applied):
                for f in range(3):
                    now = self.res[level][p, f]
                    spread[PAD + p, f] = self.gain[level - 1, p] * (now + (now - applied[f]))

            self.smooth(level, points[level])
            self.sweep(level, sweeps[level], restrict if level < LEVELS - 1 else correct, before)


    def up(self, points, sweeps, before):
        for level in range(LEVELS - 2, 0, -1):
            step = 2 ** (level - 1)
            coarse = self.corrected[level + 1]

            def prolong(p):
                fields = []
                for f in range(3):
                    sides = coarse[PAD + p - step, f] + coarse[PAD + p + step, f]
                    along = coarse[PAD + p, f] + 0.5 * sides
                    along = spread_plane([along], step, step)[0]
                    smoothed = self.gain[level - 1, p] * self.res[level][p, f]
                    fields.append(jnp.where(self.node_in, smoothed + 0.125 * along, 0.0))
                    self.value[p, f] = fields[f]
                self.put_modes(p, fields, step)

            def correct(p, applied):
                fields = []
                for f in range(3):
                    rest = self.res[level][p, f] - applied[f]
                    fields.append(self.value[p, f] + self.gain[level - 1, p] * rest)
                if level > 1:
                    for f in range(3):
                        self.corrected[level][PAD + p, f] = fields[f]
                    return
                place = p + 4 - HALO * self.half
                for t in range(2):
                    third = roll(fields[2], BACK - 17 - (BACK // 2) * t, 1)
                    first = roll(fields[t], -17, 1)
                    self.last[place, t] = jnp.where(self.lanes < BACK, first, third)

            self.loop(prolong, points[level])
            self.sweep(level, sweeps[level], correct, before)


def head_kernel(meta_ref, own_ref, *refs):
    state, (place_ref, *scratches) = refs[: len(STATE)], refs[len(STATE) :]
    place_ref[...] = choose_place()
    run = Passes(meta_ref, *scratches, state)
    run.clear()
    run.clear_state()
    for p in range(OWN, OWN + PAD):
        run.young[p] = run.zero
        for k in range(12):
            run.mode[PAD + p, k] = run.zero
    for p in range(OWN):
        run.unpack([own_ref[p, f] for f in range(4)], p + HALO * run.half)
    run.coefficients((0, HALO, OWN, 16))
    run.down(HEAD_POINTS, HEAD_SWEEPS, False)
    run.up(HEAD_POINTS_UP, HEAD_SWEEPS_UP, False)


def tail_kernel(meta_ref, side_ref, *refs):
    refs = refs[len(STATE) :]
    out_ref, state, scratches = refs[0], refs[1 : 1 + len(STATE)], refs[1 + len(STATE) :]
    run = Passes(meta_ref, *scratches, state)
    run.clear()
    for p in range(HALO):
        run.unpack([side_ref[p, f] for f in range(4)], p + OWN * (1 - run.half))
    run.coefficients((28, 0, 22, 22))
    run.down(TAIL_POINTS, TAIL_SWEEPS, True)
    run.up(TAIL_POINTS_UP, TAIL_SWEEPS_UP, True)
    for d in range(8):
        for p in range(6):
            for t in range(2):
                out_ref[d, p, t] = run.last[4 * d + p + 3, t]


LAST_SCRATCH = (
    (SLAB + 4, 3, 2, 8, WIDE),
    (SLAB + 2, 12, 2, 8, WIDE),
    (12, 2, 8, WIDE),
    (12, 2, 8, WIDE),
    (SLAB + 2, 3, 2, 8, LANES),
    (SLAB + 4, 3, 2, 8, WIDE),
)


def last_kernel(
    own_ref, own_value, own_scale, own_gain, edge_value, edge_scale, edge_gain, place_ref, in_ref, out_ref,
    coarse, mode, ahead, node, field, gather,
):
    lanes = lanes_of((8, LANES))
    for n in range(SLAB + 4):
        slot, parity = n // 2, n % 2
        for e in range(2):
            tiles = [[in_ref[e * 4 + parity * 2 + w, slot, t] for t in range(2)] for w in range(2)]
            for w in range(2):
                part = slice(w * LANES, (w + 1) * LANES)
                first, second = tiles[w]
                third = jnp.where(
                    lanes < BACK // 2, roll(first, -BACK, 1), roll(second, BACK // 2 - BACK, 1)
                )
                gather[n, 0, e, :, part] = first
                gather[n, 1, e, :, part] = second
                gather[n, 2, e, :, part] = third
    full = select(gather[...].reshape((SLAB + 4) * 48, WIDE), place_ref[...])
    full = full.reshape(SLAB + 4, 3, 2, 8, WIDE)
    for n in range(SLAB + 4):
        for i in range(3):
            planes = spread_plane([full[n, i, e] for e in range(2)], 1, 0)
            for e in range(2):
                coarse[n, i, e] = planes[e]

    def prolong(n, carry):
        fields = []
        for i in range(3):
            planes = []
            for e in range(2):
                along = coarse[n + 1, i, e] + 0.5 * (coarse[n, i, e] + coarse[n + 2, i, e])
                first = own_value[n - 1, i, e] if 2 <= n <= SLAB else edge_value[n % (SLAB - 1), i, e]
                planes.append(first + 0.125 * along)
                field[n, i, e] = planes[e][:, :LANES]
            fields.append(planes)
        modes = to_modes(fields, 1, 1)
        for k, key in enumerate(KEYS):
            for e in range(2):
                mode[n, k, e] = modes[key][e]
        return carry

    fori(SLAB + 2, prolong, LAST_UNROLL)

    for k in range(12):
        for e in range(2):
            ahead[k, e] = jnp.zeros((8, WIDE), F32)

    for n in range(SLAB + 1):
        x = n - 1
        for e in range(2):
            for t in range(2):
                part = slice(t * LANES, (t + 1) * LANES)
                low = {key: mode[n, k, e, :, part] for k, key in enumerate(KEYS)}
                high = {key: mode[n + 1, k, e, :, part] for k, key in enumerate(KEYS)}
                to_low, to_high = cell(low, high, (own_scale[x, e] if x >= 0 else edge_scale[e])[:, part])
                for k, key in enumerate(KEYS):
                    if x >= 0:
                        node[k, e, :, part] = to_low[key] + ahead[k, e, :, part]
                    ahead[k, e, :, part] = to_high[key]
        if x < 0:
            continue
        modes = {key: [node[k, e] for e in range(2)] for k, key in enumerate(KEYS)}
        applied = from_modes(modes, 1, 1)
        for i in range(3):
            for e in range(2):
                rest = own_ref[x, i, e] - applied[i][e][:, :LANES]
                total = field[n, i, e] + (own_gain[x, e] if x > 0 else edge_gain[0, e]) * rest
                out_ref[i, pl.ds(e * 8 + x, 8, stride=16), :] = own_ref[x, 4, e] * total


def shapes(*sizes):
    return [jax.ShapeDtypeStruct(size, F32) for size in sizes]


def scratch(*sizes):
    return [pltpu.VMEM(size, F32) for size in sizes]


def call(kernel, name, out, scratches, scalars, arrays, space=pltpu.VMEM, limit=VMEM_BYTES, aliases={}):
    specs = [pl.BlockSpec(memory_space=pltpu.SMEM)] * len(scalars)
    specs += [pl.BlockSpec(memory_space=space)] * len(arrays)
    return pl.pallas_call(
        kernel,
        out_shape=out,
        in_specs=specs,
        out_specs=[pl.BlockSpec(memory_space=pltpu.VMEM)] * len(out),
        scratch_shapes=scratches,
        input_output_aliases=aliases,
        compiler_params=pltpu.CompilerParams(vmem_limit_bytes=limit),
        name=name,
    )(*scalars, *arrays)


def on_device(right_side, density, fixed_mask):
    slab, line = lax.axis_index("gx"), lax.axis_index("gy")
    slabs, lines = lax.axis_size("gx"), lax.axis_size("gy")
    core = slab % 2
    half = slab // 8
    origin = LANES * line - REACH + core
    meta = jnp.stack([slab, line, core, half, origin]).astype(jnp.int32)
    groups = [list(range(8)), list(range(8, 16))]
    rows = 16 * SLAB

    own, first, last = call(
        edges_kernel,
        "edges",
        shapes((SLAB, 5, 2, 8, LANES), (SLAB, 2, 2, 8, LANES), (SLAB, 2, 2, 8, LANES)),
        [
            pltpu.VMEM((3, rows, LANES), F32),
            pltpu.VMEM((rows, LANES), jnp.int32),
            pltpu.VMEM((rows, LANES), jnp.int32),
            pltpu.SemaphoreType.DMA((3,)),
        ],
        [],
        [right_side.reshape(3, rows, LANES), density.reshape(rows, LANES), fixed_mask.reshape(rows, LANES)],
        pltpu.HBM,
        EDGES_BYTES,
    )
    after = lax.ppermute(first, "gy", [((j + 1) % lines, j) for j in range(lines)])
    before = lax.ppermute(last, "gy", [(j, (j + 1) % lines) for j in range(lines)])

    def columns(begin, scale_only):
        parts = [lax.dynamic_slice_in_dim(a, begin, 2, axis=0) for a in (own, after, before)]
        parts = [p.reshape(-1, 2, 8, LANES) for p in parts]
        for array, f in ((own, 3), (after, 1), (before, 1)):
            parts.append(lax.dynamic_slice_in_dim(array[:, f], scale_only, 1, axis=0))
        return jnp.concatenate(parts, axis=0)

    swaps = [(i, (i + 1) % slabs) for i in range(1, slabs, 2)]
    far = lax.ppermute(columns(6 * core, 5 * core), "gx", swaps + [(b, a) for a, b in swaps])
    pair = lax.ppermute(columns(6 * (1 - core), 5 * (1 - core)), "gx", [(i, i ^ 1) for i in range(slabs)])
    matrix = [jax.ShapeDtypeStruct((WIDE, WIDE), jnp.bfloat16)]
    own_scale, own_res, own_mode, own_value, own_gain, *rest = call(
        fine_head_kernel,
        "fine_head",
        shapes(*FINE_STATE) + matrix,
        scratch((2, SLAB, 2, 8, WIDE), (12, 2, 8, WIDE), (12, 2, 8, WIDE)),
        [meta],
        [own, after, before],
    )
    packed, *edges = call(
        fine_kernel,
        "fine",
        shapes((8, 4, 4, 8, LANES), (3, 3, 2, 8, WIDE), (2, 8, WIDE), (1, 2, 8, LANES)),
        scratch(*FINE_SCRATCH),
        [meta],
        [own_scale, own_res, own_mode, *rest, pair, far],
    )
    packed = lax.all_to_all(packed, "gx", 0, 0, axis_index_groups=groups)
    packed = packed.reshape(OWN, 4, 8, LANES)
    side = lax.dynamic_slice_in_dim(packed, (OWN - HALO) * (1 - half), HALO, axis=0)
    side = lax.ppermute(side, "gx", [(i, i ^ 8) for i in range(slabs)])
    *state, place = call(
        head_kernel, "head", shapes(*STATE) + matrix, scratch(*CLASS_SCRATCH), [meta], [packed]
    )
    result = call(
        tail_kernel,
        "tail",
        shapes((8, 6, 2, 8, LANES), *STATE),
        scratch(*CLASS_SCRATCH),
        [meta],
        [side, *state],
        aliases={2 + n: 1 + n for n in range(len(STATE))},
    )[0]
    result = lax.all_to_all(result, "gx", 0, 0, axis_index_groups=groups)
    (correction,) = call(
        last_kernel,
        "last",
        shapes((3, rows, LANES)),
        scratch(*LAST_SCRATCH),
        [],
        [own, own_value, own_scale, own_gain, *edges, place, result],
    )
    return correction.reshape(right_side.shape)


def solution(mesh):
    in_specs = (P(None, None, "gx", "gy"), P(None, "gx", "gy"), P(None, "gx", "gy"))
    out_specs = P(None, None, "gx", "gy")
    return jax.shard_map(
        on_device, mesh=mesh, in_specs=in_specs, out_specs=out_specs, check_vma=False
    )
```

```python
import jax
import jax.numpy as jnp
from jax import lax
from jax.experimental import pallas as pl
from jax.experimental.pallas import tpu as pltpu
from jax.sharding import PartitionSpec as P

LEVELS = 4
Q = 16
JACOBI_WEIGHT = 0.6
SOFT_FLOOR = 0.1
LAME_FIRST = 0.3 / (1.3 * 0.4)
SHEAR_MOD = 0.5 / 1.3
RATIO = LAME_FIRST / SHEAR_MOD
UNIT = SHEAR_MOD / 16.0
GAIN = JACOBI_WEIGHT / ((RATIO + 4.0) * 16.0 / 9.0)
TINY = 1e-30

SLAB = 8
LANES = 128
LAST_UNROLL = 10
EDGE = 36
REACH = 36
WINDOW = 100
PIECE = WINDOW // 4
BACK = 66
KEYS = [(i, az, ay) for i in range(3) for az in range(2) for ay in range(2)]
VMEM_BYTES = 32 * 1024 * 1024
EDGES_BYTES = 62 * 1024 * 1024
F32 = jnp.float32


def roll(value, shift, axis):
    shift %= value.shape[axis]
    return value if shift == 0 else pltpu.roll(value, shift, axis)


def z_up(planes, step):
    if len(planes) == 1:
        return [roll(planes[0], -step, 0)]
    return [planes[1], roll(planes[0], -1, 0)]


def z_down(planes, step):
    if len(planes) == 1:
        return [roll(planes[0], step, 0)]
    return [roll(planes[1], 1, 0), planes[0]]


def fori(count, body, unroll):
    if unroll == count:
        for n in range(count):
            body(n, 0)
    else:
        lax.fori_loop(0, count, body, 0)


def rows_of(shape):
    return lax.broadcasted_iota(jnp.int32, shape, 0)


def lanes_of(shape):
    return lax.broadcasted_iota(jnp.int32, shape, 1)


def to_modes(fields, step, spacing):
    modes = {}
    for i, planes in enumerate(fields):
        ahead = [roll(p, -spacing, 1) for p in planes]
        for ay, along in ((0, [b + a for a, b in zip(planes, ahead)]), (1, [b - a for a, b in zip(planes, ahead)])):
            above = z_up(along, step)
            modes[i, 0, ay] = [b + a for a, b in zip(along, above)]
            modes[i, 1, ay] = [b - a for a, b in zip(along, above)]
    return modes


def from_modes(modes, step, spacing):
    fields = []
    for i in range(3):
        along = []
        for ay in range(2):
            low = [s - d for s, d in zip(modes[i, 0, ay], modes[i, 1, ay])]
            high = z_down([s + d for s, d in zip(modes[i, 0, ay], modes[i, 1, ay])], step)
            along.append([a + b for a, b in zip(low, high)])
        fields.append([(s - d) + roll(s + d, spacing, 1) for s, d in zip(along[0], along[1])])
    return fields


def cell(low, high, scale):
    full = {}
    for i, az, ay in KEYS:
        if az or ay:
            full[i, az, 0, ay] = high[i, az, ay] + low[i, az, ay]
        full[i, az, 1, ay] = high[i, az, ay] - low[i, az, ay]

    def mode(i, *dims):
        return full[i, int(0 in dims), int(1 in dims), int(2 in dims)]

    out = {}

    def put(value, i, *dims):
        out[i, int(0 in dims), int(1 in dims), int(2 in dims)] = value

    twice = 2.0 * scale
    half = 0.5 * scale * (RATIO / 1.5)
    third = scale * (1.0 / 3.0)
    trace = (RATIO * scale) * (mode(0, 0) + mode(1, 1) + mode(2, 2))
    for i in range(3):
        put(trace + twice * mode(i, i), i, i)
    for i, j in ((0, 1), (0, 2), (1, 2)):
        shear = scale * (mode(i, j) + mode(j, i))
        put(shear, i, j)
        put(shear, j, i)
    for q in range(3):
        p, r = [d for d in range(3) if d != q]
        first, second = mode(p, p, q), mode(r, r, q)
        both = half * (first + second)
        put(both + scale * first, p, p, q)
        put(both + scale * second, r, r, q)
    others = [[d for d in range(3) if d != i] for i in range(3)]
    total = mode(0, *others[0]) + mode(1, *others[1]) + mode(2, *others[2])
    for i in range(3):
        put(third * (total + mode(i, *others[i])), i, *others[i])
    ninth = scale * ((RATIO + 4.0) / 9.0)
    for i in range(3):
        put(ninth * mode(i, 0, 1, 2), i, 0, 1, 2)

    to_low, to_high = {}, {}
    for i, az, ay in KEYS:
        difference = out[i, az, 1, ay]
        if az or ay:
            to_low[i, az, ay] = out[i, az, 0, ay] - difference
            to_high[i, az, ay] = out[i, az, 0, ay] + difference
        else:
            to_low[i, az, ay] = -difference
            to_high[i, az, ay] = difference
    return to_low, to_high


def spread_plane(planes, step, spacing):
    rows = rows_of(planes[0].shape)
    above, below = z_up(planes, step), z_down(planes, step)
    if len(planes) == 1:
        above = [jnp.where(rows < 8 - step, above[0], 0.0)]
        below = [jnp.where(rows >= step, below[0], 0.0)]
    else:
        above = [above[0], jnp.where(rows < 7, above[1], 0.0)]
        below = [jnp.where(rows >= 1, below[0], 0.0), below[1]]
    along = [p + 0.5 * (a + b) for p, a, b in zip(planes, above, below)]
    if not spacing:
        return along
    return [p + 0.5 * (roll(p, spacing, 1) + roll(p, -spacing, 1)) for p in along]


def edges_kernel(right_hbm, density_hbm, mask_hbm, own_ref, first_ref, last_ref, right_ref, density_ref, mask_ref, sems):
    copies = [
        pltpu.make_async_copy(source, target, sems.at[n])
        for n, (source, target) in enumerate(
            ((right_hbm, right_ref), (density_hbm, density_ref), (mask_hbm, mask_ref))
        )
    ]
    for copy in copies:
        copy.start()
    for copy in copies:
        copy.wait()
    lanes = lanes_of((8, LANES))
    for x in range(SLAB):
        for e in range(2):
            rows = pl.ds(e * 8 + x, 8, stride=16)
            free = 1.0 - mask_ref[rows, :].astype(F32)
            level = density_ref[rows, :].astype(F32) / (Q - 1)
            young = SOFT_FLOOR + (1.0 - SOFT_FLOOR) * (level * level * level)
            fields = [free * right_ref[i, rows, :] for i in range(3)] + [UNIT * young, free]
            for f, value in enumerate(fields):
                own_ref[x, f, e] = value
    third = EDGE * 3
    rest = LANES - third
    for pair in range(SLAB // 2):
        for e in range(2):
            even, odd = ([own_ref[2 * pair + n, f, e] for f in range(5)] for n in range(2))
            for target, start, more in ((first_ref, 0, 0), (last_ref, LANES - EDGE, 1)):
                spare = [roll(even[3], third - start + more - rest * n, 1) for n in range(2)]
                rows_of_slots = [even[:3] + [spare[0]], odd[:3] + [spare[1]], [even[4], odd[4], odd[3]]]
                for t, slots in enumerate(rows_of_slots):
                    tile = None
                    for n, value in enumerate(slots):
                        if n < 3:
                            value = roll(value, EDGE * n - start + (more if (t, n) == (2, 2) else 0), 1)
                        tile = value if n == 0 else jnp.where(lanes < EDGE * n, tile, value)
                    target[pair, t, e] = tile


WIDE = 2 * LANES

FINE_SCRATCH = (
    (5, 3, 2, 8, WIDE),
    (5, 2, 8, WIDE),
    (5, 12, 2, 8, WIDE),
    (12, 2, 8, WIDE),
    (12, 2, 8, WIDE),
    (SLAB + 2, 3, 2, 8, WIDE),
)


class Fine:
    def __init__(self, meta_ref):
        slab, line, core = meta_ref[0], meta_ref[1], meta_ref[2]
        self.core = core
        self.lanes = lanes_of((8, LANES))
        wide = lanes_of((8, WIDE))
        self.rows = rows_of((8, WIDE))
        local = jnp.where(wide < 192, wide, wide - WIDE)
        place = local + LANES * line
        self.node_in = (
            (place >= 0) & (place < 8 * LANES) & (local >= -EDGE) & (local < LANES + EDGE)
        )
        self.cell_in = (place >= 0) & (place < 8 * LANES - 1)
        self.first_slab, self.last_slab = slab == 0, slab == 15

    def inside(self, mask, x, top):
        if x < 0:
            return mask & jnp.logical_not(self.first_slab)
        if x >= top:
            return mask & jnp.logical_not(self.last_slab)
        return mask

    def widen(self, odd, f, mid, after, before):
        if f == 3 and not odd:
            rest = LANES - 3 * EDGE
            turn = LANES - EDGE - 1 - 3 * EDGE
            hi = jnp.where(
                self.lanes < rest, roll(after(0), -3 * EDGE, 1), roll(after(1), rest - 3 * EDGE, 1)
            )
            lo = jnp.where(
                self.lanes < LANES - EDGE - 1 + rest,
                roll(before(0), turn, 1),
                roll(before(1), turn + rest, 1),
            )
        else:
            t, n = (odd, f) if f < 3 else (2, 2 if f == 3 else odd)
            hi = roll(after(t), -EDGE * n, 1)
            lo = roll(before(t), LANES - EDGE - int(f == 3) - EDGE * n, 1)
        return jnp.concatenate([mid, jnp.where(self.lanes < 64, hi, lo)], axis=1)

    def cells(self, x, e, young):
        mask = self.inside(self.cell_in, x, SLAB - 1)
        if e == 1:
            mask = mask & (self.rows < 7)
        return jnp.where(mask, young, 0.0)

    def smooth(self, x, scales, fields):
        total = [a + b for a, b in zip(*scales)]
        total = [a + b for a, b in zip(total, z_down(total, 1))]
        total = [a + roll(a, 1, 1) for a in total]
        nodes = self.inside(self.node_in, x, SLAB)
        free = [jnp.where(nodes, f, 0.0) for f in fields[4]]
        gains = [GAIN * f / jnp.maximum(t, TINY) for f, t in zip(free, total)]
        res = [[jnp.where(nodes, r, 0.0) for r in fields[i]] for i in range(3)]
        values = [[g * r for g, r in zip(gains, planes)] for planes in res]
        return gains, res, values


def near(offset):
    apart = (offset + WIDE) % WIDE
    return jnp.where(apart == 0, 1.0, 0.0) + jnp.where((apart == 1) | (apart == WIDE - 1), 0.5, 0.0)


def choose_class(spread):
    source = rows_of((WIDE, WIDE))
    target = lanes_of((WIDE, WIDE))
    y = 2 * (target % LANES) - REACH + target // LANES
    offset = source - (y + WIDE) % WIDE
    weights = near(offset) if spread else jnp.where(offset == 0, 1.0, 0.0)
    return jnp.where((target % LANES) < WINDOW, weights, 0.0).astype(jnp.bfloat16)


def choose_place():
    source = rows_of((WIDE, WIDE))
    target = lanes_of((WIDE, WIDE))
    y = 2 * (source % LANES) - 2 + source // LANES
    weights = near(target - (y + WIDE) % WIDE)
    return jnp.where((source % LANES) < BACK, weights, 0.0).astype(jnp.bfloat16)


def select(rows_in, choose):
    total = 0.0
    for _ in range(3):
        term = rows_in.astype(jnp.bfloat16)
        rows_in = rows_in - term.astype(F32)
        total = total + jnp.dot(term, choose, preferred_element_type=F32)
    return total


def put_smoothed(x, found, res_ref, mode_ref, gain_ref, value_ref, n_res, n_mode, n_gain, n_value):
    gains, res, values = found
    modes = to_modes(values, 1, 1)
    for e in range(2):
        for i in range(3):
            res_ref[n_res, i, e] = res[i][e]
            if n_value is not None:
                value_ref[n_value, i, e] = values[i][e]
        for k, key in enumerate(KEYS):
            mode_ref[n_mode, k, e] = modes[key][e]
        if n_gain is not None:
            gain_ref[n_gain, e] = gains[e][:, :LANES]


def leave(at, x, node, res, left, n):
    applied = from_modes({key: [node[k, e] for e in range(2)] for k, key in enumerate(KEYS)}, 1, 1)
    keep = at.inside(at.node_in, x, SLAB)
    for i in range(3):
        planes = [jnp.where(keep, r - a, 0.0) for r, a in zip(res[i], applied[i])]
        planes = spread_plane(planes, 1, 0)
        for e in range(2):
            left[n, i, e] = planes[e]


FINE_STATE = (
    (SLAB, 2, 8, WIDE),
    (SLAB, 3, 2, 8, WIDE),
    (SLAB, 12, 2, 8, WIDE),
    (SLAB, 3, 2, 8, WIDE),
    (SLAB, 2, 8, LANES),
    (4, 2, 8, WIDE),
    (4, SLAB, 2, 2, 8, LANES),
    (SLAB, 3, 2, 8, WIDE),
    (2, 12, 2, 8, WIDE),
)


def fine_head_kernel(
    meta_ref, own_ref, after_ref, before_ref,
    scale, res, mode, value, gain, edge, pieces, left, border, choose, gather, node, ahead,
):
    at = Fine(meta_ref)

    def field(x, f, e):
        return at.widen(
            x % 2,
            f,
            own_ref[x, f, e],
            lambda t: after_ref[x // 2, t, e],
            lambda t: before_ref[x // 2, t, e],
        )

    for x in range(SLAB):
        for e in range(2):
            young = field(x, 3, e)
            gather[1, x, e] = young
            scale[x, e] = at.cells(x, e, young)
            free = jnp.where(at.node_in, field(x, 4, e), 0.0)
            gather[0, x, e] = free
            if x == 0:
                for i in range(3):
                    edge[i, e] = field(0, i, e)
                edge[3, e] = free
        if x == 0:
            continue
        fields = [[field(x, i, e) for e in range(2)] for i in range(3)]
        fields += [None, [gather[0, x, e] for e in range(2)]]
        scales = [[scale[x - d, e] for e in range(2)] for d in range(2)]
        put_smoothed(x, at.smooth(x, scales, fields), res, mode, gain, value, x, x, x, x)
    parts = select(gather[...].reshape(2 * SLAB * 16, WIDE), choose_class(False))
    parts = parts.reshape(2, SLAB, 2, 8, WIDE)
    for x in range(SLAB):
        for e in range(2):
            for parity in range(2):
                part = slice(parity * LANES, (parity + 1) * LANES)
                for f in range(4):
                    tile = roll(parts[1, x, e, :, part], WINDOW - PIECE * f, 1)
                    if f == 3:
                        tile = jnp.where(at.lanes < WINDOW, parts[0, x, e, :, part], tile)
                    pieces[f, x, e, parity] = tile
    choose[...] = choose_class(True)

    for x in range(1, SLAB - 1):
        for e in range(2):
            for t in range(2):
                part = slice(t * LANES, (t + 1) * LANES)
                low = {key: mode[x, k, e, :, part] for k, key in enumerate(KEYS)}
                high = {key: mode[x + 1, k, e, :, part] for k, key in enumerate(KEYS)}
                to_low, to_high = cell(low, high, scale[x, e, :, part])
                for k, key in enumerate(KEYS):
                    if x == 1:
                        border[0, k, e, :, part] = to_low[key]
                    else:
                        node[k, e, :, part] = to_low[key] + ahead[k, e, :, part]
                    if x < SLAB - 2:
                        ahead[k, e, :, part] = to_high[key]
                    else:
                        border[1, k, e, :, part] = to_high[key]
        if x > 1:
            leave(at, x, node, [[res[x, i, e] for e in range(2)] for i in range(3)], left, x)


def fine_kernel(
    meta_ref, own_scale, own_res, own_mode, edge, pieces, left, border, choose, pair_ref, far_ref,
    out_ref, value_ref, scale_ref, gain_ref,
    res, scale, mode, ahead, node, gather,
):
    at = Fine(meta_ref)

    def field(x, f, e):
        is_pair = (at.core == 1) if x < 0 else (at.core == 0)

        def take(slot):
            return jnp.where(is_pair, pair_ref[slot, e], far_ref[slot, e])

        if x == -3:
            return at.widen(1, f, take(16), lambda t: take(17), lambda t: take(18))
        mid = take(5 * (x % 2) + f)
        return at.widen(x % 2, f, mid, lambda t: take(10 + t), lambda t: take(13 + t))

    def scale_at(x, e):
        return own_scale[x, e] if 0 <= x < SLAB else scale[x + 3 if x < 0 else x - SLAB + 3, e]

    def mode_at(x, k, e, part):
        if 1 <= x < SLAB:
            return own_mode[x, k, e, :, part]
        return mode[x + 2 if x < 1 else x - SLAB + 3, k, e, :, part]

    def res_at(x, i, e):
        return own_res[x, i, e] if 1 <= x < SLAB else res[x + 2 if x < 1 else x - SLAB + 3, i, e]

    for x in (-3, -2, -1, 8, 9):
        for e in range(2):
            scale[x + 3 if x < 0 else x - SLAB + 3, e] = at.cells(x, e, field(x, 3, e))
    for x in (-2, -1, 0, 8, 9):
        n = x + 2 if x < 1 else x - SLAB + 3
        if x == 0:
            fields = [[edge[i, e] for e in range(2)] for i in range(3)]
            fields += [None, [edge[3, e] for e in range(2)]]
        else:
            fields = [[field(x, i, e) if i != 3 else None for e in range(2)] for i in range(5)]
        scales = [[scale_at(x - d, e) for e in range(2)] for d in range(2)]
        found = at.smooth(x, scales, fields)
        n_value = {-1: 0, 0: 1, SLAB: 2}.get(x)
        put_smoothed(x, found, res, mode, gain_ref, value_ref, n, n, 0 if x == 0 else None, n_value)
    for e in range(2):
        scale_ref[e] = scale_at(-1, e)

    for x in (-2, -1, 0, 1, SLAB - 1, SLAB):
        for e in range(2):
            for t in range(2):
                part = slice(t * LANES, (t + 1) * LANES)
                if x == 1:
                    for k, key in enumerate(KEYS):
                        node[k, e, :, part] = border[0, k, e, :, part] + ahead[k, e, :, part]
                    continue
                low = {key: mode_at(x, k, e, part) for k, key in enumerate(KEYS)}
                high = {key: mode_at(x + 1, k, e, part) for k, key in enumerate(KEYS)}
                to_low, to_high = cell(low, high, scale_at(x, e)[:, part])
                for k, key in enumerate(KEYS):
                    if x == SLAB - 1:
                        node[k, e, :, part] = to_low[key] + border[1, k, e, :, part]
                    elif x > -2:
                        node[k, e, :, part] = to_low[key] + ahead[k, e, :, part]
                    ahead[k, e, :, part] = to_high[key]
        if x > -2:
            now = [[res_at(x, i, e) for e in range(2)] for i in range(3)]
            leave(at, x, node, now, gather, x + 1)

    def left_at(x, i, e):
        return left[x, i, e] if 2 <= x < SLAB - 1 else gather[x + 1, i, e]

    rows_in = [
        left_at(x, i, e) + 0.5 * (left_at(x - 1, i, e) + left_at(x + 1, i, e))
        for x in range(SLAB)
        for i in range(3)
        for e in range(2)
    ]
    parts = select(jnp.concatenate(rows_in, axis=0), choose[...]).reshape(SLAB, 3, 2, 8, WIDE)
    for x in range(SLAB):
        for e in range(2):
            for parity in range(2):
                part = slice(parity * LANES, (parity + 1) * LANES)
                for f in range(4):
                    tile = pieces[f, x, e, parity]
                    if f < 3:
                        tile = jnp.where(at.lanes < WINDOW, parts[x, f, e, :, part], tile)
                    out_ref[e * 4 + (x % 2) * 2 + parity, x // 2, f] = tile


OWN = 32
HALO = 18
COUNT = OWN + HALO
PAD = 4
RES = (COUNT, 3, 8, LANES)
GAINS = (3, COUNT, 8, LANES)
SCALES = (3, PAD + COUNT, 8, LANES)
SPREAD = (2 * PAD + COUNT, 3, 8, LANES)
YOUNG = (COUNT + PAD, 8, LANES)
FREE = (COUNT, 8, LANES)
MODES = (2 * PAD + COUNT, 12, 8, LANES)
BACK_TILES = (OWN + 8, 2, 8, LANES)
STATE = (RES, RES, GAINS, SCALES, SPREAD, SPREAD, SPREAD, YOUNG, FREE, RES, SPREAD, BACK_TILES)
CLASS_SCRATCH = (MODES, MODES, RES)
HEAD_POINTS = {1: (0, 18, 32, 32), 2: (0, 20, 30, 30), 3: (0, 22, 28, 28)}
HEAD_SWEEPS = {1: (0, 18, 32, 16), 2: (0, 20, 30, 15), 3: (0, 22, 28, 14)}
TAIL_POINTS = {1: (29, 1, 20, 20), 2: (24, 2, 24, 24), 3: (16, 6, 28, 28)}
TAIL_SWEEPS = {1: (30, 2, 18, 9), 2: (26, 4, 20, 10), 3: (20, 10, 20, 10)}
HEAD_POINTS_UP = {2: (0, 30, 20, 20), 1: (0, 34, 16, 16)}
HEAD_SWEEPS_UP = {2: (0, 30, 20, 10), 1: (0, 34, 16, 16)}
TAIL_POINTS_UP = {2: (15, 13, 22, 11), 1: (14, 16, 20, 10)}
TAIL_SWEEPS_UP = {2: (17, 15, 18, 9), 1: (15, 17, 18, 9)}


class Passes:
    def __init__(self, meta_ref, mode, ahead, value, state):
        self.half, origin = meta_ref[3], meta_ref[4]
        self.mode, self.ahead, self.value = mode, ahead, value
        self.young, self.free = state[7], state[8]
        self.res = {1: state[9], 2: state[0], 3: state[1]}
        self.gain, self.scale = state[2], state[3]
        self.spread = {1: state[4], 2: state[5], 3: state[6]}
        self.corrected, self.last = {2: state[10], 3: state[6]}, state[11]
        shape = (8, LANES)
        self.lanes, self.rows = lanes_of(shape), rows_of(shape)
        self.place = 2 * self.lanes + origin
        self.node_in = (self.place >= 0) & (self.place < 8 * LANES)
        self.first_in = self.node_in & (self.lanes >= 1) & (self.lanes < WINDOW - 1)
        self.zero = jnp.zeros(shape, F32)

    def loop(self, body, planes):
        low, high, count, unroll = planes
        begin = low + (high - low) * self.half

        def step(n, carry):
            for u in range(unroll):
                body(begin + unroll * n + u)
            return carry

        lax.fori_loop(0, count // unroll, step, 0)

    def clear(self):
        for p in range(PAD):
            for k in range(12):
                self.mode[p, k] = self.zero
                self.mode[PAD + COUNT + p, k] = self.zero

    def clear_state(self):
        for p in range(PAD):
            self.young[COUNT + p] = self.zero
            for level in range(3):
                self.scale[level, p] = self.zero
            for spread in (*self.spread.values(), self.corrected[2]):
                for f in range(3):
                    spread[p, f] = self.zero
                    spread[PAD + COUNT + p, f] = self.zero
        for t in range(2):
            self.last[3, t] = self.zero
            self.last[OWN + 4, t] = self.zero

    def unpack(self, tiles, p):
        total = roll(tiles[0], -WINDOW, 1)
        for f in range(1, 4):
            total = jnp.where(self.lanes >= PIECE * f, roll(tiles[f], PIECE * f - WINDOW, 1), total)
        self.young[p] = total
        self.free[p] = jnp.where(self.first_in, tiles[3], 0.0)
        for f in range(3):
            self.res[1][p, f] = jnp.where(self.first_in, tiles[f], 0.0)

    def coefficients(self, planes):
        levels = [(level, 2 ** (level - 1), 2**level) for level in range(1, LEVELS)]
        place, rows = self.place, self.rows
        cells = [
            (place >= 0) & (place <= 8 * LANES - 1 - spacing) & (rows < 8 - step)
            for _, step, spacing in levels
        ]

        def fill_scale(p):
            x = p + (2 * OWN - COUNT) * self.half
            for (level, step, spacing), mask in zip(levels, cells):
                total = self.young[p] + self.young[p + step]
                total = total + roll(total, -step, 0)
                total = total + roll(total, -step, 1)
                inside = mask & (x < 2 * OWN - step)
                self.scale[level - 1, p + PAD] = jnp.where(inside, (0.125 * spacing) * total, 0.0)

        def fill_gain(p):
            free = GAIN * self.free[p]
            for level, step, _ in levels:
                total = self.scale[level - 1, p + PAD] + self.scale[level - 1, p + PAD - step]
                total = total + roll(total, step, 0)
                total = total + roll(total, step, 1)
                self.gain[level - 1, p] = free / jnp.maximum(total, TINY)

        self.loop(fill_scale, planes)
        self.loop(fill_gain, planes)

    def put_modes(self, p, fields, step):
        modes = to_modes([[f] for f in fields], step, step)
        for k, key in enumerate(KEYS):
            self.mode[PAD + p, k] = modes[key][0]

    def smooth(self, level, planes):
        step = 2 ** (level - 1)

        def body(p):
            fields = []
            for f in range(3):
                if level == 1:
                    now = self.res[1][p, f]
                else:
                    above, reach = self.spread[level - 1], step // 2
                    sides = above[PAD + p - reach, f] + above[PAD + p + reach, f]
                    now = jnp.where(self.node_in, above[PAD + p, f] + 0.5 * sides, 0.0)
                    self.res[level][p, f] = now
                fields.append(self.gain[level - 1, p] * now)
            self.put_modes(p, fields, step)

        self.loop(body, planes)

    def cell(self, level, p):
        step = 2 ** (level - 1)
        low = {key: self.mode[PAD + p, k] for k, key in enumerate(KEYS)}
        high = {key: self.mode[PAD + p + step, k] for k, key in enumerate(KEYS)}
        to_low, to_high = cell(low, high, self.scale[level - 1, p + PAD])
        return to_low, to_high

    def sweep(self, level, planes, finish, before=False):
        step = 2 ** (level - 1)
        begin = planes[0] + (planes[1] - planes[0]) * self.half
        for p in range(step):
            if before:
                to_high = self.cell(level, begin - step + p)[1]
            for k, key in enumerate(KEYS):
                self.ahead[begin + p, k] = to_high[key] if before else self.zero

        def body(p):
            to_low, to_high = self.cell(level, p)
            modes = {key: [to_low[key] + self.ahead[p, k]] for k, key in enumerate(KEYS)}
            for k, key in enumerate(KEYS):
                self.ahead[p + step, k] = to_high[key]
            finish(p, [a[0] for a in from_modes(modes, step, step)])

        self.loop(body, planes)

    def down(self, points, sweeps, before):
        for level in range(1, LEVELS):
            step = 2 ** (level - 1)
            spread = self.spread[level]

            def restrict(p, applied):
                for f in range(3):
                    rest = self.res[level][p, f] - applied[f]
                    spread[PAD + p, f] = spread_plane([rest], step, step)[0]

            def correct(p, applied):
                for f in range(3):
                    now = self.res[level][p, f]
                    spread[PAD + p, f] = self.gain[level - 1, p] * (now + (now - applied[f]))

            self.smooth(level, points[level])
            self.sweep(level, sweeps[level], restrict if level < LEVELS - 1 else correct, before)


    def up(self, points, sweeps, before):
        for level in range(LEVELS - 2, 0, -1):
            step = 2 ** (level - 1)
            coarse = self.corrected[level + 1]

            def prolong(p):
                fields = []
                for f in range(3):
                    sides = coarse[PAD + p - step, f] + coarse[PAD + p + step, f]
                    along = coarse[PAD + p, f] + 0.5 * sides
                    along = spread_plane([along], step, step)[0]
                    smoothed = self.gain[level - 1, p] * self.res[level][p, f]
                    fields.append(jnp.where(self.node_in, smoothed + 0.125 * along, 0.0))
                    self.value[p, f] = fields[f]
                self.put_modes(p, fields, step)

            def correct(p, applied):
                fields = []
                for f in range(3):
                    rest = self.res[level][p, f] - applied[f]
                    fields.append(self.value[p, f] + self.gain[level - 1, p] * rest)
                if level > 1:
                    for f in range(3):
                        self.corrected[level][PAD + p, f] = fields[f]
                    return
                place = p + 4 - HALO * self.half
                for t in range(2):
                    third = roll(fields[2], BACK - 17 - (BACK // 2) * t, 1)
                    first = roll(fields[t], -17, 1)
                    self.last[place, t] = jnp.where(self.lanes < BACK, first, third)

            self.loop(prolong, points[level])
            self.sweep(level, sweeps[level], correct, before)


def head_kernel(meta_ref, own_ref, *refs):
    state, (place_ref, *scratches) = refs[: len(STATE)], refs[len(STATE) :]
    place_ref[...] = choose_place()
    run = Passes(meta_ref, *scratches, state)
    run.clear()
    run.clear_state()
    for p in range(OWN, OWN + PAD):
        run.young[p] = run.zero
        for k in range(12):
            run.mode[PAD + p, k] = run.zero
    for p in range(OWN):
        run.unpack([own_ref[p, f] for f in range(4)], p + HALO * run.half)
    run.coefficients((0, HALO, OWN, 16))
    run.down(HEAD_POINTS, HEAD_SWEEPS, False)
    run.up(HEAD_POINTS_UP, HEAD_SWEEPS_UP, False)


def tail_kernel(meta_ref, side_ref, *refs):
    refs = refs[len(STATE) :]
    out_ref, state, scratches = refs[0], refs[1 : 1 + len(STATE)], refs[1 + len(STATE) :]
    run = Passes(meta_ref, *scratches, state)
    run.clear()
    for p in range(HALO):
        run.unpack([side_ref[p, f] for f in range(4)], p + OWN * (1 - run.half))
    run.coefficients((28, 0, 22, 22))
    run.down(TAIL_POINTS, TAIL_SWEEPS, True)
    run.up(TAIL_POINTS_UP, TAIL_SWEEPS_UP, True)
    for d in range(8):
        for p in range(6):
            for t in range(2):
                out_ref[d, p, t] = run.last[4 * d + p + 3, t]


LAST_SCRATCH = (
    (SLAB + 4, 3, 2, 8, WIDE),
    (SLAB + 2, 12, 2, 8, WIDE),
    (12, 2, 8, WIDE),
    (12, 2, 8, WIDE),
    (SLAB + 2, 3, 2, 8, LANES),
    (SLAB + 4, 3, 2, 8, WIDE),
)


def last_kernel(
    own_ref, own_value, own_scale, own_gain, edge_value, edge_scale, edge_gain, place_ref, in_ref, out_ref,
    coarse, mode, ahead, node, field, gather,
):
    lanes = lanes_of((8, LANES))
    for n in range(SLAB + 4):
        slot, parity = n // 2, n % 2
        for e in range(2):
            tiles = [[in_ref[e * 4 + parity * 2 + w, slot, t] for t in range(2)] for w in range(2)]
            for w in range(2):
                part = slice(w * LANES, (w + 1) * LANES)
                first, second = tiles[w]
                third = jnp.where(
                    lanes < BACK // 2, roll(first, -BACK, 1), roll(second, BACK // 2 - BACK, 1)
                )
                gather[n, 0, e, :, part] = first
                gather[n, 1, e, :, part] = second
                gather[n, 2, e, :, part] = third
    full = select(gather[...].reshape((SLAB + 4) * 48, WIDE), place_ref[...])
    full = full.reshape(SLAB + 4, 3, 2, 8, WIDE)
    for n in range(SLAB + 4):
        for i in range(3):
            planes = spread_plane([full[n, i, e] for e in range(2)], 1, 0)
            for e in range(2):
                coarse[n, i, e] = planes[e]

    def prolong(n, carry):
        fields = []
        for i in range(3):
            planes = []
            for e in range(2):
                along = coarse[n + 1, i, e] + 0.5 * (coarse[n, i, e] + coarse[n + 2, i, e])
                first = own_value[n - 1, i, e] if 2 <= n <= SLAB else edge_value[n % (SLAB - 1), i, e]
                planes.append(first + 0.125 * along)
                field[n, i, e] = planes[e][:, :LANES]
            fields.append(planes)
        modes = to_modes(fields, 1, 1)
        for k, key in enumerate(KEYS):
            for e in range(2):
                mode[n, k, e] = modes[key][e]
        return carry

    fori(SLAB + 2, prolong, LAST_UNROLL)

    for k in range(12):
        for e in range(2):
            ahead[k, e] = jnp.zeros((8, WIDE), F32)

    for n in range(SLAB + 1):
        x = n - 1
        for e in range(2):
            for t in range(2):
                part = slice(t * LANES, (t + 1) * LANES)
                low = {key: mode[n, k, e, :, part] for k, key in enumerate(KEYS)}
                high = {key: mode[n + 1, k, e, :, part] for k, key in enumerate(KEYS)}
                to_low, to_high = cell(low, high, (own_scale[x, e] if x >= 0 else edge_scale[e])[:, part])
                for k, key in enumerate(KEYS):
                    if x >= 0:
                        node[k, e, :, part] = to_low[key] + ahead[k, e, :, part]
                    ahead[k, e, :, part] = to_high[key]
        if x < 0:
            continue
        modes = {key: [node[k, e] for e in range(2)] for k, key in enumerate(KEYS)}
        applied = from_modes(modes, 1, 1)
        for i in range(3):
            for e in range(2):
                rest = own_ref[x, i, e] - applied[i][e][:, :LANES]
                total = field[n, i, e] + (own_gain[x, e] if x > 0 else edge_gain[0, e]) * rest
                out_ref[i, pl.ds(e * 8 + x, 8, stride=16), :] = own_ref[x, 4, e] * total


def shapes(*sizes):
    return [jax.ShapeDtypeStruct(size, F32) for size in sizes]


def scratch(*sizes):
    return [pltpu.VMEM(size, F32) for size in sizes]


def call(kernel, name, out, scratches, scalars, arrays, space=pltpu.VMEM, limit=VMEM_BYTES, aliases={}):
    specs = [pl.BlockSpec(memory_space=pltpu.SMEM)] * len(scalars)
    specs += [pl.BlockSpec(memory_space=space)] * len(arrays)
    return pl.pallas_call(
        kernel,
        out_shape=out,
        in_specs=specs,
        out_specs=[pl.BlockSpec(memory_space=pltpu.VMEM)] * len(out),
        scratch_shapes=scratches,
        input_output_aliases=aliases,
        compiler_params=pltpu.CompilerParams(vmem_limit_bytes=limit),
        name=name,
    )(*scalars, *arrays)


def on_device(right_side, density, fixed_mask):
    slab, line = lax.axis_index("gx"), lax.axis_index("gy")
    slabs, lines = lax.axis_size("gx"), lax.axis_size("gy")
    core = slab % 2
    half = slab // 8
    origin = LANES * line - REACH + core
    meta = jnp.stack([slab, line, core, half, origin]).astype(jnp.int32)
    groups = [list(range(8)), list(range(8, 16))]
    rows = 16 * SLAB

    own, first, last = call(
        edges_kernel,
        "edges",
        shapes((SLAB, 5, 2, 8, LANES), (SLAB // 2, 3, 2, 8, LANES), (SLAB // 2, 3, 2, 8, LANES)),
        [
            pltpu.VMEM((3, rows, LANES), F32),
            pltpu.VMEM((rows, LANES), jnp.int32),
            pltpu.VMEM((rows, LANES), jnp.int32),
            pltpu.SemaphoreType.DMA((3,)),
        ],
        [],
        [right_side.reshape(3, rows, LANES), density.reshape(rows, LANES), fixed_mask.reshape(rows, LANES)],
        pltpu.HBM,
        EDGES_BYTES,
    )
    after = lax.ppermute(first, "gy", [((j + 1) % lines, j) for j in range(lines)])
    before = lax.ppermute(last, "gy", [(j, (j + 1) % lines) for j in range(lines)])

    def columns(right):
        parts = [
            lax.dynamic_slice_in_dim(a, n * right, size, axis=0).reshape(-1, 2, 8, LANES)
            for a, n, size in ((own, 6, 2), (after, 3, 1), (before, 3, 1))
        ]
        for array, f, n in ((own, 3, 5), (after, 2, 2), (before, 2, 2)):
            parts.append(lax.dynamic_slice_in_dim(array[:, f], n * right, 1, axis=0))
        return jnp.concatenate(parts, axis=0)

    swaps = [(i, (i + 1) % slabs) for i in range(1, slabs, 2)]
    far = lax.ppermute(columns(core), "gx", swaps + [(b, a) for a, b in swaps])
    pair = lax.ppermute(columns(1 - core), "gx", [(i, i ^ 1) for i in range(slabs)])
    matrix = [jax.ShapeDtypeStruct((WIDE, WIDE), jnp.bfloat16)]
    own_scale, own_res, own_mode, own_value, own_gain, *rest = call(
        fine_head_kernel,
        "fine_head",
        shapes(*FINE_STATE) + matrix,
        scratch((2, SLAB, 2, 8, WIDE), (12, 2, 8, WIDE), (12, 2, 8, WIDE)),
        [meta],
        [own, after, before],
    )
    packed, *edges = call(
        fine_kernel,
        "fine",
        shapes((8, 4, 4, 8, LANES), (3, 3, 2, 8, WIDE), (2, 8, WIDE), (1, 2, 8, LANES)),
        scratch(*FINE_SCRATCH),
        [meta],
        [own_scale, own_res, own_mode, *rest, pair, far],
    )
    packed = lax.all_to_all(packed, "gx", 0, 0, axis_index_groups=groups)
    packed = packed.reshape(OWN, 4, 8, LANES)
    side = lax.dynamic_slice_in_dim(packed, (OWN - HALO) * (1 - half), HALO, axis=0)
    side = lax.ppermute(side, "gx", [(i, i ^ 8) for i in range(slabs)])
    *state, place = call(
        head_kernel, "head", shapes(*STATE) + matrix, scratch(*CLASS_SCRATCH), [meta], [packed]
    )
    result = call(
        tail_kernel,
        "tail",
        shapes((8, 6, 2, 8, LANES), *STATE),
        scratch(*CLASS_SCRATCH),
        [meta],
        [side, *state],
        aliases={2 + n: 1 + n for n in range(len(STATE))},
    )[0]
    result = lax.all_to_all(result, "gx", 0, 0, axis_index_groups=groups)
    (correction,) = call(
        last_kernel,
        "last",
        shapes((3, rows, LANES)),
        scratch(*LAST_SCRATCH),
        [],
        [own, own_value, own_scale, own_gain, *edges, place, result],
    )
    return correction.reshape(right_side.shape)


def solution(mesh):
    in_specs = (P(None, None, "gx", "gy"), P(None, "gx", "gy"), P(None, "gx", "gy"))
    out_specs = P(None, None, "gx", "gy")
    return jax.shard_map(
        on_device, mesh=mesh, in_specs=in_specs, out_specs=out_specs, check_vma=False
    )
```

```python
import jax
import jax.numpy as jnp
from jax import lax
from jax.experimental import pallas as pl
from jax.experimental.pallas import tpu as pltpu
from jax.sharding import PartitionSpec as P

LEVELS = 4
Q = 16
JACOBI_WEIGHT = 0.6
SOFT_FLOOR = 0.1
LAME_FIRST = 0.3 / (1.3 * 0.4)
SHEAR_MOD = 0.5 / 1.3
RATIO = LAME_FIRST / SHEAR_MOD
UNIT = SHEAR_MOD / 16.0
GAIN = JACOBI_WEIGHT / ((RATIO + 4.0) * 16.0 / 9.0)
TINY = 1e-30

SLAB = 8
LANES = 128
LAST_UNROLL = 10
EDGE = 36
REACH = 36
WINDOW = 100
PIECE = WINDOW // 4
BACK = 66
KEYS = [(i, az, ay) for i in range(3) for az in range(2) for ay in range(2)]
VMEM_BYTES = 32 * 1024 * 1024
EDGES_BYTES = 62 * 1024 * 1024
F32 = jnp.float32


def roll(value, shift, axis):
    shift %= value.shape[axis]
    return value if shift == 0 else pltpu.roll(value, shift, axis)


def z_up(planes, step):
    if len(planes) == 1:
        return [roll(planes[0], -step, 0)]
    return [planes[1], roll(planes[0], -1, 0)]


def z_down(planes, step):
    if len(planes) == 1:
        return [roll(planes[0], step, 0)]
    return [roll(planes[1], 1, 0), planes[0]]


def fori(count, body, unroll):
    if unroll == count:
        for n in range(count):
            body(n, 0)
    else:
        lax.fori_loop(0, count, body, 0)


def rows_of(shape):
    return lax.broadcasted_iota(jnp.int32, shape, 0)


def lanes_of(shape):
    return lax.broadcasted_iota(jnp.int32, shape, 1)


def to_modes(fields, step, spacing):
    modes = {}
    for i, planes in enumerate(fields):
        ahead = [roll(p, -spacing, 1) for p in planes]
        for ay, along in ((0, [b + a for a, b in zip(planes, ahead)]), (1, [b - a for a, b in zip(planes, ahead)])):
            above = z_up(along, step)
            modes[i, 0, ay] = [b + a for a, b in zip(along, above)]
            modes[i, 1, ay] = [b - a for a, b in zip(along, above)]
    return modes


def from_modes(modes, step, spacing):
    fields = []
    for i in range(3):
        along = []
        for ay in range(2):
            low = [s - d for s, d in zip(modes[i, 0, ay], modes[i, 1, ay])]
            high = z_down([s + d for s, d in zip(modes[i, 0, ay], modes[i, 1, ay])], step)
            along.append([a + b for a, b in zip(low, high)])
        fields.append([(s - d) + roll(s + d, spacing, 1) for s, d in zip(along[0], along[1])])
    return fields


def cell(low, high, scale):
    full = {}
    for i, az, ay in KEYS:
        if az or ay:
            full[i, az, 0, ay] = high[i, az, ay] + low[i, az, ay]
        full[i, az, 1, ay] = high[i, az, ay] - low[i, az, ay]

    def mode(i, *dims):
        return full[i, int(0 in dims), int(1 in dims), int(2 in dims)]

    out = {}

    def put(value, i, *dims):
        out[i, int(0 in dims), int(1 in dims), int(2 in dims)] = value

    twice = 2.0 * scale
    half = 0.5 * scale * (RATIO / 1.5)
    third = scale * (1.0 / 3.0)
    trace = (RATIO * scale) * (mode(0, 0) + mode(1, 1) + mode(2, 2))
    for i in range(3):
        put(trace + twice * mode(i, i), i, i)
    for i, j in ((0, 1), (0, 2), (1, 2)):
        shear = scale * (mode(i, j) + mode(j, i))
        put(shear, i, j)
        put(shear, j, i)
    for q in range(3):
        p, r = [d for d in range(3) if d != q]
        first, second = mode(p, p, q), mode(r, r, q)
        both = half * (first + second)
        put(both + scale * first, p, p, q)
        put(both + scale * second, r, r, q)
    others = [[d for d in range(3) if d != i] for i in range(3)]
    total = mode(0, *others[0]) + mode(1, *others[1]) + mode(2, *others[2])
    for i in range(3):
        put(third * (total + mode(i, *others[i])), i, *others[i])
    ninth = scale * ((RATIO + 4.0) / 9.0)
    for i in range(3):
        put(ninth * mode(i, 0, 1, 2), i, 0, 1, 2)

    to_low, to_high = {}, {}
    for i, az, ay in KEYS:
        difference = out[i, az, 1, ay]
        if az or ay:
            to_low[i, az, ay] = out[i, az, 0, ay] - difference
            to_high[i, az, ay] = out[i, az, 0, ay] + difference
        else:
            to_low[i, az, ay] = -difference
            to_high[i, az, ay] = difference
    return to_low, to_high


def spread_plane(planes, step, spacing):
    rows = rows_of(planes[0].shape)
    above, below = z_up(planes, step), z_down(planes, step)
    if len(planes) == 1:
        above = [jnp.where(rows < 8 - step, above[0], 0.0)]
        below = [jnp.where(rows >= step, below[0], 0.0)]
    else:
        above = [above[0], jnp.where(rows < 7, above[1], 0.0)]
        below = [jnp.where(rows >= 1, below[0], 0.0), below[1]]
    along = [p + 0.5 * (a + b) for p, a, b in zip(planes, above, below)]
    if not spacing:
        return along
    return [p + 0.5 * (roll(p, spacing, 1) + roll(p, -spacing, 1)) for p in along]


def edges_kernel(right_hbm, density_hbm, mask_hbm, own_ref, first_ref, last_ref, right_ref, density_ref, mask_ref, sems):
    copies = [
        pltpu.make_async_copy(source, target, sems.at[n])
        for n, (source, target) in enumerate(
            ((right_hbm, right_ref), (density_hbm, density_ref), (mask_hbm, mask_ref))
        )
    ]
    for copy in copies:
        copy.start()
    for copy in copies:
        copy.wait()
    lanes = lanes_of((8, LANES))
    for x in range(SLAB):
        for e in range(2):
            rows = pl.ds(e * 8 + x, 8, stride=16)
            free = 1.0 - mask_ref[rows, :].astype(F32)
            level = density_ref[rows, :].astype(F32) / (Q - 1)
            young = SOFT_FLOOR + (1.0 - SOFT_FLOOR) * (level * level * level)
            fields = [free * right_ref[i, rows, :] for i in range(3)] + [UNIT * young, free]
            for f, value in enumerate(fields):
                own_ref[x, f, e] = value
    third = EDGE * 3
    rest = LANES - third
    for pair in range(SLAB // 2):
        for e in range(2):
            even, odd = ([own_ref[2 * pair + n, f, e] for f in range(5)] for n in range(2))
            for target, start, more in ((first_ref, 0, 0), (last_ref, LANES - EDGE, 1)):
                spare = [roll(even[3], third - start + more - rest * n, 1) for n in range(2)]
                rows_of_slots = [even[:3] + [spare[0]], odd[:3] + [spare[1]], [even[4], odd[4], odd[3]]]
                for t, slots in enumerate(rows_of_slots):
                    tile = None
                    for n, value in enumerate(slots):
                        if n < 3:
                            value = roll(value, EDGE * n - start + (more if (t, n) == (2, 2) else 0), 1)
                        tile = value if n == 0 else jnp.where(lanes < EDGE * n, tile, value)
                    target[pair, t, e] = tile


WIDE = 2 * LANES

FINE_SCRATCH = (
    (5, 3, 2, 8, WIDE),
    (5, 2, 8, WIDE),
    (5, 12, 2, 8, WIDE),
    (12, 2, 8, WIDE),
    (12, 2, 8, WIDE),
    (SLAB + 2, 3, 2, 8, WIDE),
)


class Fine:
    def __init__(self, meta_ref):
        slab, line, core = meta_ref[0], meta_ref[1], meta_ref[2]
        self.core = core
        self.lanes = lanes_of((8, LANES))
        wide = lanes_of((8, WIDE))
        self.rows = rows_of((8, WIDE))
        local = jnp.where(wide < 192, wide, wide - WIDE)
        place = local + LANES * line
        self.node_in = (
            (place >= 0) & (place < 8 * LANES) & (local >= -EDGE) & (local < LANES + EDGE)
        )
        self.cell_in = (place >= 0) & (place < 8 * LANES - 1)
        self.first_slab, self.last_slab = slab == 0, slab == 15

    def inside(self, mask, x, top):
        if x < 0:
            return mask & jnp.logical_not(self.first_slab)
        if x >= top:
            return mask & jnp.logical_not(self.last_slab)
        return mask

    def widen(self, odd, f, mid, after, before):
        if f == 3 and not odd:
            rest = LANES - 3 * EDGE
            turn = LANES - EDGE - 1 - 3 * EDGE
            hi = jnp.where(
                self.lanes < rest, roll(after(0), -3 * EDGE, 1), roll(after(1), rest - 3 * EDGE, 1)
            )
            lo = jnp.where(
                self.lanes < LANES - EDGE - 1 + rest,
                roll(before(0), turn, 1),
                roll(before(1), turn + rest, 1),
            )
        else:
            t, n = (odd, f) if f < 3 else (2, 2 if f == 3 else odd)
            hi = roll(after(t), -EDGE * n, 1)
            lo = roll(before(t), LANES - EDGE - int(f == 3) - EDGE * n, 1)
        return jnp.concatenate([mid, jnp.where(self.lanes < 64, hi, lo)], axis=1)

    def cells(self, x, e, young):
        mask = self.inside(self.cell_in, x, SLAB - 1)
        if e == 1:
            mask = mask & (self.rows < 7)
        return jnp.where(mask, young, 0.0)

    def smooth(self, x, scales, fields):
        total = [a + b for a, b in zip(*scales)]
        total = [a + b for a, b in zip(total, z_down(total, 1))]
        total = [a + roll(a, 1, 1) for a in total]
        nodes = self.inside(self.node_in, x, SLAB)
        free = [jnp.where(nodes, f, 0.0) for f in fields[4]]
        gains = [GAIN * f / jnp.maximum(t, TINY) for f, t in zip(free, total)]
        res = [[jnp.where(nodes, r, 0.0) for r in fields[i]] for i in range(3)]
        values = [[g * r for g, r in zip(gains, planes)] for planes in res]
        return gains, res, values


def near(offset):
    apart = (offset + WIDE) % WIDE
    return jnp.where(apart == 0, 1.0, 0.0) + jnp.where((apart == 1) | (apart == WIDE - 1), 0.5, 0.0)


def choose_class(spread):
    source = rows_of((WIDE, WIDE))
    target = lanes_of((WIDE, WIDE))
    y = 2 * (target % LANES) - REACH + target // LANES
    offset = source - (y + WIDE) % WIDE
    weights = near(offset) if spread else jnp.where(offset == 0, 1.0, 0.0)
    return jnp.where((target % LANES) < WINDOW, weights, 0.0).astype(jnp.bfloat16)


def choose_place():
    source = rows_of((WIDE, WIDE))
    target = lanes_of((WIDE, WIDE))
    y = 2 * (source % LANES) - 2 + source // LANES
    weights = near(target - (y + WIDE) % WIDE)
    return jnp.where((source % LANES) < BACK, weights, 0.0).astype(jnp.bfloat16)


def select(rows_in, choose, terms):
    total = 0.0
    for _ in range(terms):
        term = rows_in.astype(jnp.bfloat16)
        rows_in = rows_in - term.astype(F32)
        total = total + jnp.dot(term, choose, preferred_element_type=F32)
    return total


def put_smoothed(x, found, res_ref, mode_ref, gain_ref, value_ref, n_res, n_mode, n_gain, n_value):
    gains, res, values = found
    modes = to_modes(values, 1, 1)
    for e in range(2):
        for i in range(3):
            res_ref[n_res, i, e] = res[i][e]
            if n_value is not None:
                value_ref[n_value, i, e] = values[i][e]
        for k, key in enumerate(KEYS):
            mode_ref[n_mode, k, e] = modes[key][e]
        if n_gain is not None:
            gain_ref[n_gain, e] = gains[e][:, :LANES]


def leave(at, x, node, res, left, n):
    applied = from_modes({key: [node[k, e] for e in range(2)] for k, key in enumerate(KEYS)}, 1, 1)
    keep = at.inside(at.node_in, x, SLAB)
    for i in range(3):
        planes = [jnp.where(keep, r - a, 0.0) for r, a in zip(res[i], applied[i])]
        planes = spread_plane(planes, 1, 0)
        for e in range(2):
            left[n, i, e] = planes[e]


FINE_STATE = (
    (SLAB, 2, 8, WIDE),
    (SLAB, 3, 2, 8, WIDE),
    (SLAB, 12, 2, 8, WIDE),
    (SLAB, 3, 2, 8, WIDE),
    (SLAB, 2, 8, LANES),
    (4, 2, 8, WIDE),
    (4, SLAB, 2, 2, 8, LANES),
    (SLAB, 3, 2, 8, WIDE),
    (2, 12, 2, 8, WIDE),
)


def fine_head_kernel(
    meta_ref, own_ref, after_ref, before_ref,
    scale, res, mode, value, gain, edge, pieces, left, border, choose, gather, node, ahead,
):
    at = Fine(meta_ref)

    def field(x, f, e):
        return at.widen(
            x % 2,
            f,
            own_ref[x, f, e],
            lambda t: after_ref[x // 2, t, e],
            lambda t: before_ref[x // 2, t, e],
        )

    for x in range(SLAB):
        for e in range(2):
            young = field(x, 3, e)
            gather[1, x, e] = young
            scale[x, e] = at.cells(x, e, young)
            free = jnp.where(at.node_in, field(x, 4, e), 0.0)
            gather[0, x, e] = free
            if x == 0:
                for i in range(3):
                    edge[i, e] = field(0, i, e)
                edge[3, e] = free
        if x == 0:
            continue
        fields = [[field(x, i, e) for e in range(2)] for i in range(3)]
        fields += [None, [gather[0, x, e] for e in range(2)]]
        scales = [[scale[x - d, e] for e in range(2)] for d in range(2)]
        put_smoothed(x, at.smooth(x, scales, fields), res, mode, gain, value, x, x, x, x)
    parts = select(gather[...].reshape(2 * SLAB * 16, WIDE), choose_class(False), 3)
    parts = parts.reshape(2, SLAB, 2, 8, WIDE)
    for x in range(SLAB):
        for e in range(2):
            for parity in range(2):
                part = slice(parity * LANES, (parity + 1) * LANES)
                for f in range(4):
                    tile = roll(parts[1, x, e, :, part], WINDOW - PIECE * f, 1)
                    if f == 3:
                        tile = jnp.where(at.lanes < WINDOW, parts[0, x, e, :, part], tile)
                    pieces[f, x, e, parity] = tile
    choose[...] = choose_class(True)

    for x in range(1, SLAB - 1):
        for e in range(2):
            for t in range(2):
                part = slice(t * LANES, (t + 1) * LANES)
                low = {key: mode[x, k, e, :, part] for k, key in enumerate(KEYS)}
                high = {key: mode[x + 1, k, e, :, part] for k, key in enumerate(KEYS)}
                to_low, to_high = cell(low, high, scale[x, e, :, part])
                for k, key in enumerate(KEYS):
                    if x == 1:
                        border[0, k, e, :, part] = to_low[key]
                    else:
                        node[k, e, :, part] = to_low[key] + ahead[k, e, :, part]
                    if x < SLAB - 2:
                        ahead[k, e, :, part] = to_high[key]
                    else:
                        border[1, k, e, :, part] = to_high[key]
        if x > 1:
            leave(at, x, node, [[res[x, i, e] for e in range(2)] for i in range(3)], left, x)


def fine_kernel(
    meta_ref, own_scale, own_res, own_mode, edge, pieces, left, border, choose, pair_ref, far_ref,
    out_ref, value_ref, scale_ref, gain_ref,
    res, scale, mode, ahead, node, gather,
):
    at = Fine(meta_ref)

    def field(x, f, e):
        is_pair = (at.core == 1) if x < 0 else (at.core == 0)

        def take(slot):
            return jnp.where(is_pair, pair_ref[slot, e], far_ref[slot, e])

        if x == -3:
            return at.widen(1, f, take(16), lambda t: take(17), lambda t: take(18))
        mid = take(5 * (x % 2) + f)
        return at.widen(x % 2, f, mid, lambda t: take(10 + t), lambda t: take(13 + t))

    def scale_at(x, e):
        return own_scale[x, e] if 0 <= x < SLAB else scale[x + 3 if x < 0 else x - SLAB + 3, e]

    def mode_at(x, k, e, part):
        if 1 <= x < SLAB:
            return own_mode[x, k, e, :, part]
        return mode[x + 2 if x < 1 else x - SLAB + 3, k, e, :, part]

    def res_at(x, i, e):
        return own_res[x, i, e] if 1 <= x < SLAB else res[x + 2 if x < 1 else x - SLAB + 3, i, e]

    for x in (-3, -2, -1, 8, 9):
        for e in range(2):
            scale[x + 3 if x < 0 else x - SLAB + 3, e] = at.cells(x, e, field(x, 3, e))
    for x in (-2, -1, 0, 8, 9):
        n = x + 2 if x < 1 else x - SLAB + 3
        if x == 0:
            fields = [[edge[i, e] for e in range(2)] for i in range(3)]
            fields += [None, [edge[3, e] for e in range(2)]]
        else:
            fields = [[field(x, i, e) if i != 3 else None for e in range(2)] for i in range(5)]
        scales = [[scale_at(x - d, e) for e in range(2)] for d in range(2)]
        found = at.smooth(x, scales, fields)
        n_value = {-1: 0, 0: 1, SLAB: 2}.get(x)
        put_smoothed(x, found, res, mode, gain_ref, value_ref, n, n, 0 if x == 0 else None, n_value)
    for e in range(2):
        scale_ref[e] = scale_at(-1, e)

    for x in (-2, -1, 0, 1, SLAB - 1, SLAB):
        for e in range(2):
            for t in range(2):
                part = slice(t * LANES, (t + 1) * LANES)
                if x == 1:
                    for k, key in enumerate(KEYS):
                        node[k, e, :, part] = border[0, k, e, :, part] + ahead[k, e, :, part]
                    continue
                low = {key: mode_at(x, k, e, part) for k, key in enumerate(KEYS)}
                high = {key: mode_at(x + 1, k, e, part) for k, key in enumerate(KEYS)}
                to_low, to_high = cell(low, high, scale_at(x, e)[:, part])
                for k, key in enumerate(KEYS):
                    if x == SLAB - 1:
                        node[k, e, :, part] = to_low[key] + border[1, k, e, :, part]
                    elif x > -2:
                        node[k, e, :, part] = to_low[key] + ahead[k, e, :, part]
                    ahead[k, e, :, part] = to_high[key]
        if x > -2:
            now = [[res_at(x, i, e) for e in range(2)] for i in range(3)]
            leave(at, x, node, now, gather, x + 1)

    def left_at(x, i, e):
        return left[x, i, e] if 2 <= x < SLAB - 1 else gather[x + 1, i, e]

    rows_in = [
        left_at(x, i, e) + 0.5 * (left_at(x - 1, i, e) + left_at(x + 1, i, e))
        for x in range(SLAB)
        for i in range(3)
        for e in range(2)
    ]
    parts = select(jnp.concatenate(rows_in, axis=0), choose[...], 2).reshape(SLAB, 3, 2, 8, WIDE)
    for x in range(SLAB):
        for e in range(2):
            for parity in range(2):
                part = slice(parity * LANES, (parity + 1) * LANES)
                for f in range(4):
                    tile = pieces[f, x, e, parity]
                    if f < 3:
                        tile = jnp.where(at.lanes < WINDOW, parts[x, f, e, :, part], tile)
                    out_ref[e * 4 + (x % 2) * 2 + parity, x // 2, f] = tile


OWN = 32
HALO = 18
COUNT = OWN + HALO
PAD = 4
RES = (COUNT, 3, 8, LANES)
GAINS = (3, COUNT, 8, LANES)
SCALES = (3, PAD + COUNT, 8, LANES)
SPREAD = (2 * PAD + COUNT, 3, 8, LANES)
YOUNG = (COUNT + PAD, 8, LANES)
FREE = (COUNT, 8, LANES)
MODES = (2 * PAD + COUNT, 12, 8, LANES)
BACK_TILES = (OWN + 8, 2, 8, LANES)
STATE = (RES, RES, GAINS, SCALES, SPREAD, SPREAD, SPREAD, YOUNG, FREE, RES, SPREAD, BACK_TILES)
CLASS_SCRATCH = (MODES, MODES, RES)
HEAD_POINTS = {1: (0, 18, 32, 32), 2: (0, 20, 30, 30), 3: (0, 22, 28, 28)}
HEAD_SWEEPS = {1: (0, 18, 32, 16), 2: (0, 20, 30, 15), 3: (0, 22, 28, 14)}
TAIL_POINTS = {1: (29, 1, 20, 20), 2: (24, 2, 24, 24), 3: (16, 6, 28, 28)}
TAIL_SWEEPS = {1: (30, 2, 18, 9), 2: (26, 4, 20, 10), 3: (20, 10, 20, 10)}
HEAD_POINTS_UP = {2: (0, 30, 20, 20), 1: (0, 34, 16, 16)}
HEAD_SWEEPS_UP = {2: (0, 30, 20, 10), 1: (0, 34, 16, 16)}
TAIL_POINTS_UP = {2: (15, 13, 22, 11), 1: (14, 16, 20, 10)}
TAIL_SWEEPS_UP = {2: (17, 15, 18, 9), 1: (15, 17, 18, 9)}


class Passes:
    def __init__(self, meta_ref, mode, ahead, value, state):
        self.half, origin = meta_ref[3], meta_ref[4]
        self.mode, self.ahead, self.value = mode, ahead, value
        self.young, self.free = state[7], state[8]
        self.res = {1: state[9], 2: state[0], 3: state[1]}
        self.gain, self.scale = state[2], state[3]
        self.spread = {1: state[4], 2: state[5], 3: state[6]}
        self.corrected, self.last = {2: state[10], 3: state[6]}, state[11]
        shape = (8, LANES)
        self.lanes, self.rows = lanes_of(shape), rows_of(shape)
        self.place = 2 * self.lanes + origin
        self.node_in = (self.place >= 0) & (self.place < 8 * LANES)
        self.first_in = self.node_in & (self.lanes >= 1) & (self.lanes < WINDOW - 1)
        self.zero = jnp.zeros(shape, F32)

    def loop(self, body, planes):
        low, high, count, unroll = planes
        begin = low + (high - low) * self.half

        def step(n, carry):
            for u in range(unroll):
                body(begin + unroll * n + u)
            return carry

        lax.fori_loop(0, count // unroll, step, 0)

    def clear(self):
        for p in range(PAD):
            for k in range(12):
                self.mode[p, k] = self.zero
                self.mode[PAD + COUNT + p, k] = self.zero

    def clear_state(self):
        for p in range(PAD):
            self.young[COUNT + p] = self.zero
            for level in range(3):
                self.scale[level, p] = self.zero
            for spread in (*self.spread.values(), self.corrected[2]):
                for f in range(3):
                    spread[p, f] = self.zero
                    spread[PAD + COUNT + p, f] = self.zero
        for t in range(2):
            self.last[3, t] = self.zero
            self.last[OWN + 4, t] = self.zero

    def unpack(self, tiles, p):
        total = roll(tiles[0], -WINDOW, 1)
        for f in range(1, 4):
            total = jnp.where(self.lanes >= PIECE * f, roll(tiles[f], PIECE * f - WINDOW, 1), total)
        self.young[p] = total
        self.free[p] = jnp.where(self.first_in, tiles[3], 0.0)
        for f in range(3):
            self.res[1][p, f] = jnp.where(self.first_in, tiles[f], 0.0)

    def coefficients(self, planes):
        levels = [(level, 2 ** (level - 1), 2**level) for level in range(1, LEVELS)]
        place, rows = self.place, self.rows
        cells = [
            (place >= 0) & (place <= 8 * LANES - 1 - spacing) & (rows < 8 - step)
            for _, step, spacing in levels
        ]

        def fill_scale(p):
            x = p + (2 * OWN - COUNT) * self.half
            for (level, step, spacing), mask in zip(levels, cells):
                total = self.young[p] + self.young[p + step]
                total = total + roll(total, -step, 0)
                total = total + roll(total, -step, 1)
                inside = mask & (x < 2 * OWN - step)
                self.scale[level - 1, p + PAD] = jnp.where(inside, (0.125 * spacing) * total, 0.0)

        def fill_gain(p):
            free = GAIN * self.free[p]
            for level, step, _ in levels:
                total = self.scale[level - 1, p + PAD] + self.scale[level - 1, p + PAD - step]
                total = total + roll(total, step, 0)
                total = total + roll(total, step, 1)
                self.gain[level - 1, p] = free / jnp.maximum(total, TINY)

        self.loop(fill_scale, planes)
        self.loop(fill_gain, planes)

    def put_modes(self, p, fields, step):
        modes = to_modes([[f] for f in fields], step, step)
        for k, key in enumerate(KEYS):
            self.mode[PAD + p, k] = modes[key][0]

    def smooth(self, level, planes):
        step = 2 ** (level - 1)

        def body(p):
            fields = []
            for f in range(3):
                if level == 1:
                    now = self.res[1][p, f]
                else:
                    above, reach = self.spread[level - 1], step // 2
                    sides = above[PAD + p - reach, f] + above[PAD + p + reach, f]
                    now = jnp.where(self.node_in, above[PAD + p, f] + 0.5 * sides, 0.0)
                    self.res[level][p, f] = now
                fields.append(self.gain[level - 1, p] * now)
            self.put_modes(p, fields, step)

        self.loop(body, planes)

    def cell(self, level, p):
        step = 2 ** (level - 1)
        low = {key: self.mode[PAD + p, k] for k, key in enumerate(KEYS)}
        high = {key: self.mode[PAD + p + step, k] for k, key in enumerate(KEYS)}
        to_low, to_high = cell(low, high, self.scale[level - 1, p + PAD])
        return to_low, to_high

    def sweep(self, level, planes, finish, before=False):
        step = 2 ** (level - 1)
        begin = planes[0] + (planes[1] - planes[0]) * self.half
        for p in range(step):
            if before:
                to_high = self.cell(level, begin - step + p)[1]
            for k, key in enumerate(KEYS):
                self.ahead[begin + p, k] = to_high[key] if before else self.zero

        def body(p):
            to_low, to_high = self.cell(level, p)
            modes = {key: [to_low[key] + self.ahead[p, k]] for k, key in enumerate(KEYS)}
            for k, key in enumerate(KEYS):
                self.ahead[p + step, k] = to_high[key]
            finish(p, [a[0] for a in from_modes(modes, step, step)])

        self.loop(body, planes)

    def down(self, points, sweeps, before):
        for level in range(1, LEVELS):
            step = 2 ** (level - 1)
            spread = self.spread[level]

            def restrict(p, applied):
                for f in range(3):
                    rest = self.res[level][p, f] - applied[f]
                    spread[PAD + p, f] = spread_plane([rest], step, step)[0]

            def correct(p, applied):
                for f in range(3):
                    now = self.res[level][p, f]
                    spread[PAD + p, f] = self.gain[level - 1, p] * (now + (now - applied[f]))

            self.smooth(level, points[level])
            self.sweep(level, sweeps[level], restrict if level < LEVELS - 1 else correct, before)


    def up(self, points, sweeps, before):
        for level in range(LEVELS - 2, 0, -1):
            step = 2 ** (level - 1)
            coarse = self.corrected[level + 1]

            def prolong(p):
                fields = []
                for f in range(3):
                    sides = coarse[PAD + p - step, f] + coarse[PAD + p + step, f]
                    along = coarse[PAD + p, f] + 0.5 * sides
                    along = spread_plane([along], step, step)[0]
                    smoothed = self.gain[level - 1, p] * self.res[level][p, f]
                    fields.append(jnp.where(self.node_in, smoothed + 0.125 * along, 0.0))
                    self.value[p, f] = fields[f]
                self.put_modes(p, fields, step)

            def correct(p, applied):
                fields = []
                for f in range(3):
                    rest = self.res[level][p, f] - applied[f]
                    fields.append(self.value[p, f] + self.gain[level - 1, p] * rest)
                if level > 1:
                    for f in range(3):
                        self.corrected[level][PAD + p, f] = fields[f]
                    return
                place = p + 4 - HALO * self.half
                for t in range(2):
                    third = roll(fields[2], BACK - 17 - (BACK // 2) * t, 1)
                    first = roll(fields[t], -17, 1)
                    self.last[place, t] = jnp.where(self.lanes < BACK, first, third)

            self.loop(prolong, points[level])
            self.sweep(level, sweeps[level], correct, before)


def head_kernel(meta_ref, own_ref, *refs):
    state, (place_ref, *scratches) = refs[: len(STATE)], refs[len(STATE) :]
    place_ref[...] = choose_place()
    run = Passes(meta_ref, *scratches, state)
    run.clear()
    run.clear_state()
    for p in range(OWN, OWN + PAD):
        run.young[p] = run.zero
        for k in range(12):
            run.mode[PAD + p, k] = run.zero
    for p in range(OWN):
        run.unpack([own_ref[p, f] for f in range(4)], p + HALO * run.half)
    run.coefficients((0, HALO, OWN, 16))
    run.down(HEAD_POINTS, HEAD_SWEEPS, False)
    run.up(HEAD_POINTS_UP, HEAD_SWEEPS_UP, False)


def tail_kernel(meta_ref, side_ref, *refs):
    refs = refs[len(STATE) :]
    out_ref, state, scratches = refs[0], refs[1 : 1 + len(STATE)], refs[1 + len(STATE) :]
    run = Passes(meta_ref, *scratches, state)
    run.clear()
    for p in range(HALO):
        run.unpack([side_ref[p, f] for f in range(4)], p + OWN * (1 - run.half))
    run.coefficients((28, 0, 22, 22))
    run.down(TAIL_POINTS, TAIL_SWEEPS, True)
    run.up(TAIL_POINTS_UP, TAIL_SWEEPS_UP, True)
    for d in range(8):
        for p in range(6):
            for t in range(2):
                out_ref[d, p, t] = run.last[4 * d + p + 3, t]


LAST_SCRATCH = (
    (SLAB + 4, 3, 2, 8, WIDE),
    (SLAB + 2, 12, 2, 8, WIDE),
    (12, 2, 8, WIDE),
    (12, 2, 8, WIDE),
    (SLAB + 2, 3, 2, 8, LANES),
    (SLAB + 4, 3, 2, 8, WIDE),
)


def last_kernel(
    own_ref, own_value, own_scale, own_gain, edge_value, edge_scale, edge_gain, place_ref, in_ref, out_ref,
    coarse, mode, ahead, node, field, gather,
):
    lanes = lanes_of((8, LANES))
    for n in range(SLAB + 4):
        slot, parity = n // 2, n % 2
        for e in range(2):
            tiles = [[in_ref[e * 4 + parity * 2 + w, slot, t] for t in range(2)] for w in range(2)]
            for w in range(2):
                part = slice(w * LANES, (w + 1) * LANES)
                first, second = tiles[w]
                third = jnp.where(
                    lanes < BACK // 2, roll(first, -BACK, 1), roll(second, BACK // 2 - BACK, 1)
                )
                gather[n, 0, e, :, part] = first
                gather[n, 1, e, :, part] = second
                gather[n, 2, e, :, part] = third
    full = select(gather[...].reshape((SLAB + 4) * 48, WIDE), place_ref[...], 2)
    full = full.reshape(SLAB + 4, 3, 2, 8, WIDE)
    for n in range(SLAB + 4):
        for i in range(3):
            planes = spread_plane([full[n, i, e] for e in range(2)], 1, 0)
            for e in range(2):
                coarse[n, i, e] = planes[e]

    def prolong(n, carry):
        fields = []
        for i in range(3):
            planes = []
            for e in range(2):
                along = coarse[n + 1, i, e] + 0.5 * (coarse[n, i, e] + coarse[n + 2, i, e])
                first = own_value[n - 1, i, e] if 2 <= n <= SLAB else edge_value[n % (SLAB - 1), i, e]
                planes.append(first + 0.125 * along)
                field[n, i, e] = planes[e][:, :LANES]
            fields.append(planes)
        modes = to_modes(fields, 1, 1)
        for k, key in enumerate(KEYS):
            for e in range(2):
                mode[n, k, e] = modes[key][e]
        return carry

    fori(SLAB + 2, prolong, LAST_UNROLL)

    for k in range(12):
        for e in range(2):
            ahead[k, e] = jnp.zeros((8, WIDE), F32)

    for n in range(SLAB + 1):
        x = n - 1
        for e in range(2):
            for t in range(2):
                part = slice(t * LANES, (t + 1) * LANES)
                low = {key: mode[n, k, e, :, part] for k, key in enumerate(KEYS)}
                high = {key: mode[n + 1, k, e, :, part] for k, key in enumerate(KEYS)}
                to_low, to_high = cell(low, high, (own_scale[x, e] if x >= 0 else edge_scale[e])[:, part])
                for k, key in enumerate(KEYS):
                    if x >= 0:
                        node[k, e, :, part] = to_low[key] + ahead[k, e, :, part]
                    ahead[k, e, :, part] = to_high[key]
        if x < 0:
            continue
        modes = {key: [node[k, e] for e in range(2)] for k, key in enumerate(KEYS)}
        applied = from_modes(modes, 1, 1)
        for i in range(3):
            for e in range(2):
                rest = own_ref[x, i, e] - applied[i][e][:, :LANES]
                total = field[n, i, e] + (own_gain[x, e] if x > 0 else edge_gain[0, e]) * rest
                out_ref[i, pl.ds(e * 8 + x, 8, stride=16), :] = own_ref[x, 4, e] * total


def shapes(*sizes):
    return [jax.ShapeDtypeStruct(size, F32) for size in sizes]


def scratch(*sizes):
    return [pltpu.VMEM(size, F32) for size in sizes]


def call(kernel, name, out, scratches, scalars, arrays, space=pltpu.VMEM, limit=VMEM_BYTES, aliases={}):
    specs = [pl.BlockSpec(memory_space=pltpu.SMEM)] * len(scalars)
    specs += [pl.BlockSpec(memory_space=space)] * len(arrays)
    return pl.pallas_call(
        kernel,
        out_shape=out,
        in_specs=specs,
        out_specs=[pl.BlockSpec(memory_space=pltpu.VMEM)] * len(out),
        scratch_shapes=scratches,
        input_output_aliases=aliases,
        compiler_params=pltpu.CompilerParams(vmem_limit_bytes=limit),
        name=name,
    )(*scalars, *arrays)


def on_device(right_side, density, fixed_mask):
    slab, line = lax.axis_index("gx"), lax.axis_index("gy")
    slabs, lines = lax.axis_size("gx"), lax.axis_size("gy")
    core = slab % 2
    half = slab // 8
    origin = LANES * line - REACH + core
    meta = jnp.stack([slab, line, core, half, origin]).astype(jnp.int32)
    groups = [list(range(8)), list(range(8, 16))]
    rows = 16 * SLAB

    own, first, last = call(
        edges_kernel,
        "edges",
        shapes((SLAB, 5, 2, 8, LANES), (SLAB // 2, 3, 2, 8, LANES), (SLAB // 2, 3, 2, 8, LANES)),
        [
            pltpu.VMEM((3, rows, LANES), F32),
            pltpu.VMEM((rows, LANES), jnp.int32),
            pltpu.VMEM((rows, LANES), jnp.int32),
            pltpu.SemaphoreType.DMA((3,)),
        ],
        [],
        [right_side.reshape(3, rows, LANES), density.reshape(rows, LANES), fixed_mask.reshape(rows, LANES)],
        pltpu.HBM,
        EDGES_BYTES,
    )
    after = lax.ppermute(first, "gy", [((j + 1) % lines, j) for j in range(lines)])
    before = lax.ppermute(last, "gy", [(j, (j + 1) % lines) for j in range(lines)])

    def columns(right):
        parts = [
            lax.dynamic_slice_in_dim(a, n * right, size, axis=0).reshape(-1, 2, 8, LANES)
            for a, n, size in ((own, 6, 2), (after, 3, 1), (before, 3, 1))
        ]
        for array, f, n in ((own, 3, 5), (after, 2, 2), (before, 2, 2)):
            parts.append(lax.dynamic_slice_in_dim(array[:, f], n * right, 1, axis=0))
        return jnp.concatenate(parts, axis=0)

    swaps = [(i, (i + 1) % slabs) for i in range(1, slabs, 2)]
    far = lax.ppermute(columns(core), "gx", swaps + [(b, a) for a, b in swaps])
    pair = lax.ppermute(columns(1 - core), "gx", [(i, i ^ 1) for i in range(slabs)])
    matrix = [jax.ShapeDtypeStruct((WIDE, WIDE), jnp.bfloat16)]
    own_scale, own_res, own_mode, own_value, own_gain, *rest = call(
        fine_head_kernel,
        "fine_head",
        shapes(*FINE_STATE) + matrix,
        scratch((2, SLAB, 2, 8, WIDE), (12, 2, 8, WIDE), (12, 2, 8, WIDE)),
        [meta],
        [own, after, before],
    )
    packed, *edges = call(
        fine_kernel,
        "fine",
        shapes((8, 4, 4, 8, LANES), (3, 3, 2, 8, WIDE), (2, 8, WIDE), (1, 2, 8, LANES)),
        scratch(*FINE_SCRATCH),
        [meta],
        [own_scale, own_res, own_mode, *rest, pair, far],
    )
    packed = lax.all_to_all(packed, "gx", 0, 0, axis_index_groups=groups)
    packed = packed.reshape(OWN, 4, 8, LANES)
    side = lax.dynamic_slice_in_dim(packed, (OWN - HALO) * (1 - half), HALO, axis=0)
    side = lax.ppermute(side, "gx", [(i, i ^ 8) for i in range(slabs)])
    *state, place = call(
        head_kernel, "head", shapes(*STATE) + matrix, scratch(*CLASS_SCRATCH), [meta], [packed]
    )
    result = call(
        tail_kernel,
        "tail",
        shapes((8, 6, 2, 8, LANES), *STATE),
        scratch(*CLASS_SCRATCH),
        [meta],
        [side, *state],
        aliases={2 + n: 1 + n for n in range(len(STATE))},
    )[0]
    result = lax.all_to_all(result, "gx", 0, 0, axis_index_groups=groups)
    (correction,) = call(
        last_kernel,
        "last",
        shapes((3, rows, LANES)),
        scratch(*LAST_SCRATCH),
        [],
        [own, own_value, own_scale, own_gain, *edges, place, result],
    )
    return correction.reshape(right_side.shape)


def solution(mesh):
    in_specs = (P(None, None, "gx", "gy"), P(None, "gx", "gy"), P(None, "gx", "gy"))
    out_specs = P(None, None, "gx", "gy")
    return jax.shard_map(
        on_device, mesh=mesh, in_specs=in_specs, out_specs=out_specs, check_vma=False
    )
```
